32 devices in a mesh: dp: 2 (over y), row: 4 (over x, core), col: 4 (over z).
Axes of the slice: x: 2, y: 2, z: 4, core: 2. Of those that a mesh axis runs over, the one named last changes fastest.
Arguments:
- layer_input: bfloat16 [4096, 2048], P(('dp', 'row'), 'col'), may hold values from -40 to 40
- segment_ids: int32 [4096], P('dp'), may hold values from 0 to 2, as said below
- positions: int32 [4096], P('dp'), may hold values from 0 to 2047, as said below
- norm_gain: float32 [2, 2048], P(None, 'col'), may hold values from 0.25 to 1.75
- norm_bias: float32 [2, 2048], P(None, 'col'), may hold values from -4 to 4
- qkv_weight: bfloat16 [2, 2048, 3, 2048], P(None, ('dp', 'row'), None, 'col'), may hold values from -0.125 to 0.125
- qkv_bias: float32 [2, 3, 2048], P(None, None, 'col'), may hold values from -4 to 4
- dense_weight: bfloat16 [2, 2048, 2048], P(None, 'col', ('dp', 'row')), may hold values from -1.75 to 1.75
- dense_bias: float32 [2, 2048], P(None, 'col'), may hold values from -4 to 4
- up_weight: bfloat16 [2, 2048, 8192], P(None, ('dp', 'row'), 'col'), may hold values from -0.125 to 0.125
- up_bias: float32 [2, 8192], P(None, 'col'), may hold values from -4 to 4
- down_weight: bfloat16 [2, 8192, 2048], P(None, 'col', ('dp', 'row')), may hold values from -0.0625 to 0.0625
- down_bias: float32 [2, 2048], P(None, 'col'), may hold values from -4 to 4
- output_cotangent: bfloat16 [4096, 2048], P(('dp', 'row'), 'col'), may hold values from -4 to 4
Outputs:
- layer_outputs: float32 [2, 4096, 2048], P(None, ('dp', 'row'), 'col')
- input_gradient: float32 [4096, 2048], P(('dp', 'row'), 'col')
- norm_gain_gradient: float32 [2, 2048], P(None, 'col')
- norm_bias_gradient: float32 [2, 2048], P(None, 'col')
- qkv_weight_gradient: float32 [2, 2048, 3, 2048], P(None, ('dp', 'row'), None, 'col')
- qkv_bias_gradient: float32 [2, 3, 2048], P(None, None, 'col')
- dense_weight_gradient: float32 [2, 2048, 2048], P(None, 'col', ('dp', 'row'))
- dense_bias_gradient: float32 [2, 2048], P(None, 'col')
- up_weight_gradient: float32 [2, 2048, 8192], P(None, ('dp', 'row'), 'col')
- up_bias_gradient: float32 [2, 8192], P(None, 'col')
- down_weight_gradient: float32 [2, 8192, 2048], P(None, 'col', ('dp', 'row'))
- down_bias_gradient: float32 [2, 2048], P(None, 'col')
The draws below stay inside these ranges and needn't reach their ends.
Inputs may be any that keep to these rules, and one draw needn't show every extreme that they name: `segment_ids`: each index of dp holds one sequence of 2048 tokens in three documents numbered 0, 1, 2 in order; document 0 ends within the sequence's first 512 tokens and document 2 begins within its last 512 tokens. `positions`: within a document the position rises by one from token to token; document 1 starts at 0 and document 2 ends at 2047.
All inputs are finite; a program needn't handle non-finite values.
Results may differ from the reference program's by a relative error of at most 0.014.
Values may be sent and summed in bfloat16 or wider, within the bound.
No kernel may reach another device: no remote copies, remote signals or barrier semaphores. Data moves between devices by JAX's collectives and lax.ppermute only.
A program may use at most 256 MiB of HBM per device.

```python
import math
import jax
import jax.numpy as jnp
from jax import lax

D = 2048
HEADS = 32
HEAD_DIM = 64
ROT = 32
FF = 8192
LAYERS = 2
TOK_DEV = 512
SEQ = 2048
TOKENS = 4096
N_DP = 2


def document_bounds(key):
    first_key, last_key, shift_key = jax.random.split(key, 3)
    sequence_count = TOKENS // SEQ
    first_end = jax.random.randint(first_key, (sequence_count, 1), 1, TOK_DEV, dtype=jnp.int32)
    last_start = SEQ - jax.random.randint(last_key, (sequence_count, 1), 1, TOK_DEV, dtype=jnp.int32)
    prefix_shift = jax.random.randint(shift_key, (sequence_count, 1), 0, SEQ - TOK_DEV + 1, dtype=jnp.int32)
    token_place = jnp.arange(SEQ, dtype=jnp.int32)[None, :]
    return (first_end, last_start, prefix_shift, token_place)


def draw_segment_ids(key, part):
    first_end, last_start, prefix_shift, token_place = document_bounds(key)
    numbers = (token_place >= first_end).astype(jnp.int32) + (token_place >= last_start).astype(jnp.int32)
    return numbers.reshape(TOKENS)


def draw_positions(key, part):
    first_end, last_start, prefix_shift, token_place = document_bounds(key)
    inside = jnp.where(token_place < last_start, token_place - first_end, token_place)
    places = jnp.where(token_place < first_end, prefix_shift + token_place, inside)
    return places.reshape(TOKENS)


def draw_layer_input(key, part):
    key = jax.random.fold_in(key, 17)
    noise_key, scale_key = jax.random.split(key)
    column_place = jnp.arange(D, dtype=jnp.float32) / (D - 1)
    noise_values = jnp.clip(jax.random.normal(noise_key, (TOKENS, D), jnp.float32), -4.0, 4.0)
    row_scale = jnp.exp(jax.random.uniform(scale_key, (TOKENS, 1), jnp.float32, -1.15, 1.15))
    column_scale = jnp.exp(2.3 * column_place - 1.15)
    return (noise_values * row_scale * column_scale[None, :]).astype(jnp.bfloat16)


def draw_output_cotangent(key, part):
    key = jax.random.fold_in(key, 29)
    noise_key = jax.random.fold_in(key, 0)
    return jnp.clip(jax.random.normal(noise_key, (TOKENS, D), jnp.float32), -4.0, 4.0).astype(jnp.bfloat16)


def steps_of(rng, dims, pieces, low, high):
    def one(axis_at, blocks):
        heights = jax.random.uniform(jax.random.fold_in(jax.random.fold_in(rng, 6), axis_at), (blocks,), jnp.float32, low / len(pieces), high / len(pieces))
        return jnp.repeat(jnp.exp(heights), dims[axis_at] // blocks).reshape((-1,) + (1,) * (len(dims) - axis_at - 1))

    factor_of = one(*pieces[0])
    for cut in pieces[1:]:
        factor_of = factor_of * one(*cut)
    return factor_of


def bell_draw(rng, extent, scale, limit, shards=(), kind=jnp.bfloat16):
    values = jax.random.normal(rng, extent, jnp.float32) * scale
    if len(shards) > 0:
        values = steps_of(rng, extent, shards, -0.22, 0.18) * values
    return jnp.clip(values, min=-limit, max=limit).astype(kind)


def setup_inputs(seed: int = 0) -> dict:
    seeds = jax.random.split(jax.random.key(seed), 15)
    return {
        "layer_input": draw_layer_input(jax.random.fold_in(seeds[14], 71), 0),
        "segment_ids": draw_segment_ids(jax.random.fold_in(seeds[14], 71), 0),
        "positions": draw_positions(jax.random.fold_in(seeds[14], 71), 0),
        "norm_gain": jnp.clip(1.0 + 0.15 * jax.random.normal(seeds[3], (LAYERS, D), jnp.float32), 0.25, 1.75),
        "norm_bias": bell_draw(seeds[4], (LAYERS, D), 0.3, 4.0, ((1, 4),), jnp.float32),
        "qkv_weight": bell_draw(seeds[5], (LAYERS, D, 3, D), D ** -0.5, 0.125, ((1, 8), (3, 4))),
        "qkv_bias": bell_draw(seeds[6], (LAYERS, 3, D), 0.5, 4.0, ((2, 4),), jnp.float32),
        "dense_weight": bell_draw(seeds[7], (LAYERS, D, D), 12 ** -0.5, 1.75, ((1, 4), (2, 8))),
        "dense_bias": bell_draw(seeds[8], (LAYERS, D), 0.3, 4.0, ((1, 4),), jnp.float32),
        "up_weight": bell_draw(seeds[9], (LAYERS, D, FF), D ** -0.5, 0.125, ((1, 8), (2, 4))),
        "up_bias": bell_draw(seeds[10], (LAYERS, FF), 0.5, 4.0, ((1, 4),), jnp.float32),
        "down_weight": bell_draw(seeds[11], (LAYERS, FF, D), FF ** -0.5, 0.0625, ((1, 4), (2, 8))),
        "down_bias": bell_draw(seeds[12], (LAYERS, D), 0.3, 4.0, ((1, 4),), jnp.float32),
        "output_cotangent": draw_output_cotangent(jax.random.fold_in(seeds[14], 71), 0),
    }


EPSILON = 1e-05
HIGHEST = lax.Precision.HIGHEST

@jax.custom_vjp
def low(v):
    return lax.optimization_barrier(v.astype(jnp.bfloat16)).astype(jnp.float32)

@jax.custom_vjp
def low_back(v):
    return v

def low_keep(v):
    return (low(v), None)

def low_pass(kept, grad):
    return (grad,)

def back_keep(v):
    return (v, None)

def back_low(kept, grad):
    return (low(grad),)
low.defvjp(low_keep, low_pass)
low_back.defvjp(back_keep, back_low)

def rotate(tensor, position):
    half_width = ROT // 2
    freq_table = 1.0 / 10000.0 ** (jnp.arange(half_width, dtype=jnp.float32) * 2.0 / ROT)
    angles = position.astype(jnp.float32)[..., None] * freq_table
    cosine_table = jnp.cos(angles)[..., None, :]
    sine_table = jnp.sin(angles)[..., None, :]
    first_half = tensor[..., :half_width]
    second_half = tensor[..., half_width:ROT]
    return jnp.concatenate([first_half * cosine_table - second_half * sine_table, second_half * cosine_table + first_half * sine_table, tensor[..., ROT:]], axis=-1)

def attend(queries, keys_all, values_all, segments):
    block_size = math.gcd(SEQ, 512)
    block_count = SEQ // block_size
    key_place = jnp.arange(SEQ, dtype=jnp.int32)
    score_scale = HEAD_DIM ** (-0.5)

    def one_block(block_index):
        sequence_index = block_index // block_count
        query_begin = block_index % block_count * block_size
        query_sequence = lax.dynamic_index_in_dim(queries, sequence_index, 0, keepdims=False)
        key_sequence = lax.dynamic_index_in_dim(keys_all, sequence_index, 0, keepdims=False)
        value_sequence = lax.dynamic_index_in_dim(values_all, sequence_index, 0, keepdims=False)
        segment_sequence = lax.dynamic_index_in_dim(segments, sequence_index, 0, keepdims=False)
        query_block = lax.dynamic_slice_in_dim(query_sequence, query_begin, block_size, 0)
        query_segments = lax.dynamic_slice_in_dim(segment_sequence, query_begin, block_size, 0)
        query_place = query_begin + jnp.arange(block_size, dtype=jnp.int32)
        scores = jnp.einsum('qhe,khe->hqk', query_block, key_sequence, precision=HIGHEST) * score_scale
        scores = low_back(scores)
        allowed = (key_place[None, :] <= query_place[:, None]) & (query_segments[:, None] == segment_sequence[None, :])
        scores = jnp.where(allowed[None], scores, -1e+30)
        largest = lax.optimization_barrier(jnp.max(scores, axis=-1, keepdims=True))
        exp_scores = jnp.exp(scores - largest)
        softmax_weights = low(exp_scores / lax.optimization_barrier(jnp.sum(exp_scores, axis=-1, keepdims=True)))
        return jnp.einsum('hqk,khe->qhe', softmax_weights, value_sequence, precision=HIGHEST)
    indices = jnp.arange(N_DP * block_count, dtype=jnp.int32)
    stacked = lax.map(jax.checkpoint(one_block), indices)
    return stacked.reshape(queries.shape)

def layer_forward(state, layer_params, segments, position):
    norm_gain, norm_bias, qkv_weight, qkv_bias, dense_weight, dense_bias, up_weight, up_bias, down_weight, down_bias = layer_params
    center = lax.optimization_barrier(jnp.mean(state, axis=-1, keepdims=True))
    spread = lax.optimization_barrier(jnp.mean(state * state, axis=-1, keepdims=True)) - center * center
    normed = low((state - center) * lax.rsqrt(spread + EPSILON) * norm_gain + norm_bias)
    projected = low_back(jnp.dot(normed, qkv_weight.reshape(D, 3 * D), precision=HIGHEST) + qkv_bias.reshape(3 * D))
    expanded = low_back(jnp.dot(normed, up_weight, precision=HIGHEST) + up_bias)
    shaped = projected.reshape(N_DP, SEQ, 3, HEADS, HEAD_DIM)
    queries = low(rotate(shaped[:, :, 0], position))
    keys_all = low(rotate(shaped[:, :, 1], position))
    values_all = low(shaped[:, :, 2])
    mixed_heads = attend(queries, keys_all, values_all, segments).reshape(TOKENS, D)
    mixed_heads = low(low_back(mixed_heads))
    activated = low(jax.nn.gelu(expanded, approximate=True))
    branch = low_back(jnp.dot(mixed_heads, dense_weight, precision=HIGHEST) + jnp.dot(activated, down_weight, precision=HIGHEST))
    return state + branch + dense_bias + down_bias

def reference(layer_input, segment_ids, positions, norm_gain, norm_bias, qkv_weight, qkv_bias, dense_weight, dense_bias, up_weight, up_bias, down_weight, down_bias, output_cotangent):
    segments = segment_ids.reshape(N_DP, SEQ)
    position = positions.reshape(N_DP, SEQ)
    params = tuple((operand.astype(jnp.float32) for operand in (norm_gain, norm_bias, qkv_weight, qkv_bias, dense_weight, dense_bias, up_weight, up_bias, down_weight, down_bias)))

    def forward(initial_state, weights):
        state = initial_state
        outputs = []
        for layer_index in range(LAYERS):
            layer_params = tuple((member[layer_index] for member in weights))
            state = layer_forward(state, layer_params, segments, position)
            outputs.append(state)
        return jnp.stack(outputs)
    initial_state = layer_input.astype(jnp.float32)
    outputs, pull_back = jax.vjp(forward, initial_state, params)
    cotangent = jnp.concatenate([jnp.zeros((LAYERS - 1, TOKENS, D), jnp.float32), output_cotangent.astype(jnp.float32)[None]], axis=0)
    start_grad, param_grads = pull_back(cotangent)
    return (outputs, start_grad, param_grads[0], param_grads[1], param_grads[2], param_grads[3], param_grads[4], param_grads[5], param_grads[6], param_grads[7], param_grads[8], param_grads[9])
```

```python
import functools
import math

import jax
import jax.numpy as jnp
from jax import lax
from jax.experimental import pallas as pl
from jax.experimental.pallas import tpu as pltpu
from jax.sharding import Mesh
from jax.sharding import PartitionSpec as P

HEAD_DIM = 64
ROT = 32
EPSILON = 1e-05
NEGATIVE = -1e30
LANES = 128
VMEM_BYTES = 48 * 1024 * 1024
F32 = jnp.float32
BF16 = jnp.bfloat16


def gelu_curve(values):
    return jax.nn.gelu(values, approximate=True)


def rotation_tables(place_values):
    half_width = ROT // 2
    freq_table = 1.0 / 10000.0 ** (jnp.arange(half_width, dtype=F32) * 2.0 / ROT)
    angles = place_values.astype(F32)[:, None] * freq_table
    return (jnp.cos(angles)[:, None, :], jnp.sin(angles)[:, None, :])


def rotate(tensor, cosine_table, sine_table):
    half_width = cosine_table.shape[-1]
    first_half = tensor[..., :half_width]
    second_half = tensor[..., half_width : 2 * half_width]
    return jnp.concatenate(
        [
            first_half * cosine_table - second_half * sine_table,
            second_half * cosine_table + first_half * sine_table,
            tensor[..., 2 * half_width :],
        ],
        axis=-1,
    )


def shift(value, axis, step):
    size = lax.axis_size(axis)
    return lax.ppermute(value, axis, [(i, (i + step) % size) for i in range(size)])


def small_sum(value, axes):
    for axis in axes:
        value = value + sum(shift(value, axis, k) for k in range(1, lax.axis_size(axis)))
    return value


def gather_blocks(own):
    n_y, n_x = lax.axis_size("dp"), lax.axis_size("x")
    half = own.shape[0] // 2
    blocks = {(0, 0): own}
    for b in range(1, n_x):
        blocks[0, b] = shift(own, "x", b)
    for a in range(1, n_y):
        blocks[a, 0] = shift(own, "dp", a)
    for a in range(1, n_y):
        for b in range(1, n_x):
            first = shift(blocks[0, b][:half], "dp", a)
            second = shift(blocks[a, 0][half:], "x", b)
            blocks[a, b] = jnp.concatenate([first, second], axis=0)
    return [blocks[a, b] for a in range(n_y) for b in range(n_x)]


def scatter_blocks(parts):
    n_y, n_x = lax.axis_size("dp"), lax.axis_size("x")
    blocks = {(a, b): parts[a * n_x + b] for a in range(n_y) for b in range(n_x)}
    half = parts[0].shape[0] // 2
    top = {a: [blocks[a, 0][:half]] for a in range(1, n_y)}
    bottom = {b: [blocks[0, b][half:]] for b in range(1, n_x)}
    for a in range(1, n_y):
        for b in range(1, n_x):
            top[a].append(shift(blocks[a, b][:half], "x", -b))
            bottom[b].append(shift(blocks[a, b][half:], "dp", -a))

    def added(terms):
        return sum(term.astype(F32) for term in terms).astype(BF16)

    total = blocks[0, 0].astype(F32)
    for a in range(1, n_y):
        block = jnp.concatenate([added(top[a]), blocks[a, 0][half:]], axis=0)
        total = total + shift(block, "dp", -a).astype(F32)
    for b in range(1, n_x):
        block = jnp.concatenate([blocks[0, b][:half], added(bottom[b])], axis=0)
        total = total + shift(block, "x", -b).astype(F32)
    return total


def swap_core(value):
    return shift(value, "core", 1)


def in_core_order(own, other, axis):
    core = lax.axis_index("core")
    return jnp.where(
        core == 0,
        jnp.concatenate([own, other], axis=axis),
        jnp.concatenate([other, own], axis=axis),
    )


def width_table():
    n_y, n_x, n_c = lax.axis_size("dp"), lax.axis_size("x"), lax.axis_size("core")
    y, x, c = lax.axis_index("dp"), lax.axis_index("x"), lax.axis_index("core")
    entries = [
        (((y - a + n_y) % n_y) * n_x + (x - b + n_x) % n_x) * n_c + (c - k + n_c) % n_c
        for a in range(n_y)
        for b in range(n_x)
        for k in range(n_c)
    ]
    return jnp.stack(entries + [c]).astype(jnp.int32)


def to_own_order(own, other, table):
    tokens, width = own.shape
    places = table.shape[0] - 1
    block = width // places
    rows = math.gcd(tokens, 256)
    steps = tokens // rows

    def body(table_ref, own_ref, other_ref, out_ref):
        def move(source):
            for place in range(places):
                begin = pl.multiple_of(table_ref[place] * block, block)
                out_ref[:, place * block : (place + 1) * block] = source[:, pl.ds(begin, block)]

        pl.when(pl.program_id(0) == 0)(lambda: move(own_ref))
        pl.when(pl.program_id(0) == 1)(lambda: move(other_ref))

    return pl.pallas_call(
        body,
        grid_spec=pltpu.PrefetchScalarGridSpec(
            num_scalar_prefetch=1,
            grid=(2, steps),
            in_specs=[
                pl.BlockSpec((rows, width), lambda s, i, t: (jnp.where(s == 0, i, steps - 1), 0)),
                pl.BlockSpec((rows, width), lambda s, i, t: (jnp.where(s == 0, 0, i), 0)),
            ],
            out_specs=pl.BlockSpec(
                (rows, width), lambda s, i, t: ((t[places] + s) % 2 * steps + i, 0)
            ),
        ),
        out_shape=jax.ShapeDtypeStruct((2 * tokens, width), own.dtype),
        cost_estimate=pl.CostEstimate(
            flops=0, bytes_accessed=8 * tokens * width, transcendentals=0
        ),
        name="to_own_order",
    )(table, own, other)


def from_own_order(partial, received, table):
    tokens, width = received.shape
    places = table.shape[0] - 1
    block = width // places
    rows = math.gcd(tokens, 256)
    steps = tokens // rows

    def body(table_ref, own_ref, other_ref, out_ref):
        for place in range(places):
            begin = pl.multiple_of(table_ref[place] * block, block)
            here = slice(place * block, (place + 1) * block)
            there = slice((place ^ 1) * block, ((place ^ 1) + 1) * block)
            total = own_ref[:, here].astype(F32) + other_ref[:, there].astype(F32)
            out_ref[:, pl.ds(begin, block)] = total.astype(BF16)

    return pl.pallas_call(
        body,
        grid_spec=pltpu.PrefetchScalarGridSpec(
            num_scalar_prefetch=1,
            grid=(steps,),
            in_specs=[
                pl.BlockSpec((rows, width), lambda i, t: (t[places] * steps + i, 0)),
                pl.BlockSpec((rows, width), lambda i, t: (i, 0)),
            ],
            out_specs=pl.BlockSpec((rows, width), lambda i, t: (i, 0)),
        ),
        out_shape=jax.ShapeDtypeStruct((tokens, width), BF16),
        cost_estimate=pl.CostEstimate(
            flops=tokens * width, bytes_accessed=6 * tokens * width, transcendentals=0
        ),
        name="from_own_order",
    )(table, partial, received)


def contract(left, right, left_dim, right_dim):
    return lax.dot_general(
        left, right, (((left_dim,), (right_dim,)), ((), ())), preferred_element_type=F32
    )


def head_part(value, head):
    lane = lax.broadcasted_iota(jnp.int32, value.shape, 1)
    keep = (lane >= head * HEAD_DIM) & (lane < (head + 1) * HEAD_DIM)
    return jnp.where(keep, value, jnp.zeros_like(value))


def allowed_pairs(query_begin, key_begin, starts, shape):
    key_place = key_begin + lax.broadcasted_iota(jnp.int32, shape, 0)
    query_place = query_begin + lax.broadcasted_iota(jnp.int32, shape, 1)
    return (key_place <= query_place) & (key_place >= starts)


LOG2E = math.log2(math.e)
HEADS_TILE = LANES // HEAD_DIM


def attend_forward(queries, keys, values, starts, query_begin):
    tokens, columns = queries.shape
    total_keys = keys.shape[0]
    block_q = math.gcd(tokens, 256)
    block_k = math.gcd(total_keys, 512)
    pairs = columns // LANES
    scale = HEAD_DIM**-0.5 * LOG2E
    steps = tokens // block_q
    scalars = jnp.concatenate([query_begin[None], starts[0, ::block_q]]).astype(jnp.int32)

    def body(scalar_ref, q_ref, k_ref, v_ref, start_ref, mixed_ref, exact_ref, log_ref):
        step = pl.program_id(1)
        begin = scalar_ref[0] + step * block_q
        first = scalar_ref[1 + step] // block_k
        last = (begin + block_q - 1) // block_k + 1
        q = q_ref[...]
        start_row = start_ref[...]

        def one(index, carried):
            key_begin = pl.multiple_of(index * block_k, block_k)
            k = k_ref[pl.ds(key_begin, block_k), :]
            v = v_ref[pl.ds(key_begin, block_k), :]
            allowed = allowed_pairs(begin, key_begin, start_row, (block_k, block_q))
            out = []
            for head in range(HEADS_TILE):
                top, total, summed = carried[head]
                scores = contract(head_part(k, head), q, 1, 1) * scale
                scores = jnp.where(allowed, scores, NEGATIVE)
                new_top = jnp.maximum(top, jnp.max(scores, axis=0, keepdims=True))
                terms = jnp.exp2(scores - new_top)
                shrink = jnp.exp2(top - new_top)
                total = total * shrink + jnp.sum(terms, axis=0, keepdims=True)
                summed = summed * shrink + contract(v, terms.astype(BF16), 0, 0)
                out.append((new_top, total, summed))
            return tuple(out)

        zero = (
            jnp.full((1, block_q), NEGATIVE, F32),
            jnp.zeros((1, block_q), F32),
            jnp.zeros((LANES, block_q), F32),
        )
        state = lax.fori_loop(first, last, one, (zero,) * HEADS_TILE)
        pieces = []
        for head in range(HEADS_TILE):
            top, total, summed = state[head]
            here = slice(head * HEAD_DIM, (head + 1) * HEAD_DIM)
            pieces.append(summed[here] * (1.0 / total))
            log_ref[head : head + 1, :] = top + jnp.log2(total)
        mixed = jnp.concatenate(pieces, axis=0).T
        exact_ref[...] = mixed
        mixed_ref[...] = mixed.astype(BF16)

    flops = 4 * tokens * total_keys * columns
    return pl.pallas_call(
        body,
        grid_spec=pltpu.PrefetchScalarGridSpec(
            num_scalar_prefetch=1,
            grid=(pairs, steps),
            in_specs=[
                pl.BlockSpec((block_q, LANES), lambda p, i, s: (i, p)),
                pl.BlockSpec((total_keys, LANES), lambda p, i, s: (0, p)),
                pl.BlockSpec((total_keys, LANES), lambda p, i, s: (0, p)),
                pl.BlockSpec((1, block_q), lambda p, i, s: (0, i)),
            ],
            out_specs=[
                pl.BlockSpec((block_q, LANES), lambda p, i, s: (i, p)),
                pl.BlockSpec((block_q, LANES), lambda p, i, s: (i, p)),
                pl.BlockSpec((None, HEADS_TILE, block_q), lambda p, i, s: (p, 0, i)),
            ],
        ),
        out_shape=[
            jax.ShapeDtypeStruct((tokens, columns), BF16),
            jax.ShapeDtypeStruct((tokens, columns), F32),
            jax.ShapeDtypeStruct((pairs, HEADS_TILE, tokens), F32),
        ],
        compiler_params=pltpu.CompilerParams(vmem_limit_bytes=VMEM_BYTES),
        cost_estimate=pl.CostEstimate(
            flops=flops, bytes_accessed=8 * (tokens + total_keys) * columns, transcendentals=0
        ),
        name="attend_forward",
    )(scalars, queries, keys, values, starts)


def attend_backward(queries, keys, values, starts, query_begin, exact, logs, mixed_grad):
    tokens, columns = queries.shape
    total_keys = keys.shape[0]
    block_q = math.gcd(tokens, 256)
    block_k = math.gcd(total_keys, 512)
    pairs = columns // LANES
    scale = HEAD_DIM**-0.5
    steps = tokens // block_q
    scalars = jnp.concatenate([query_begin[None], starts[0, ::block_q]]).astype(jnp.int32)

    def body(
        scalar_ref, q_ref, k_ref, v_ref, start_ref, exact_ref, log_ref, dm_ref,
        dq_ref, dk_ref, dv_ref, dq_sum, dk_sum, dv_sum, delta_ref,
    ):
        index = pl.program_id(1)
        query_base = scalar_ref[0]
        key_begin = index * block_k

        @pl.when(index == 0)
        def _():
            dq_sum[...] = jnp.zeros_like(dq_sum)
            product = (exact_ref[...] * dm_ref[...].astype(F32)).T
            for head in range(HEADS_TILE):
                here = slice(head * HEAD_DIM, (head + 1) * HEAD_DIM)
                delta_ref[head : head + 1, :] = jnp.sum(product[here], axis=0, keepdims=True)

        dk_sum[...] = jnp.zeros_like(dk_sum)
        dv_sum[...] = jnp.zeros_like(dv_sum)
        k = k_ref[...]
        v = v_ref[...]
        k_parts = [head_part(k, head) for head in range(HEADS_TILE)]
        v_parts = [head_part(v, head) for head in range(HEADS_TILE)]

        def one(step, carried):
            begin = query_base + step * block_q

            @pl.when(scalar_ref[1 + step] < key_begin + block_k)
            def _():
                here = pl.ds(pl.multiple_of(step * block_q, block_q), block_q)
                q = q_ref[here, :]
                dm = dm_ref[here, :]
                allowed = allowed_pairs(
                    begin, key_begin, start_ref[:, here], (block_k, block_q)
                )
                for head in range(HEADS_TILE):
                    log_row = log_ref[head : head + 1, here]
                    scores = contract(k_parts[head], q, 1, 1) * (scale * LOG2E) - log_row
                    weights = jnp.exp2(jnp.where(allowed, scores, NEGATIVE))
                    weight_grad = contract(v_parts[head], dm, 1, 1)
                    score_grad = weights * (weight_grad - delta_ref[head : head + 1, here])
                    score_grad = score_grad.astype(BF16)
                    dv_sum[...] += contract(weights.astype(BF16), head_part(dm, head), 1, 0)
                    dk_sum[...] += contract(score_grad, head_part(q, head), 1, 0)
                    dq_sum[:, here] += contract(k_parts[head], score_grad, 0, 0)

            return carried

        first = jnp.maximum(key_begin - query_base, 0) // block_q
        lax.fori_loop(jnp.minimum(first, steps), steps, one, 0)
        dk_ref[...] = (dk_sum[...] * scale).astype(BF16)
        dv_ref[...] = dv_sum[...].astype(BF16)

        @pl.when(index == pl.num_programs(1) - 1)
        def _():
            dq_ref[...] = dq_sum[...].T * scale

    flops = 10 * tokens * total_keys * columns
    whole = lambda p, j, s: (0, p)
    return pl.pallas_call(
        body,
        grid_spec=pltpu.PrefetchScalarGridSpec(
            num_scalar_prefetch=1,
            grid=(pairs, total_keys // block_k),
            in_specs=[
                pl.BlockSpec((tokens, LANES), whole),
                pl.BlockSpec((block_k, LANES), lambda p, j, s: (j, p)),
                pl.BlockSpec((block_k, LANES), lambda p, j, s: (j, p)),
                pl.BlockSpec((1, tokens), lambda p, j, s: (0, 0)),
                pl.BlockSpec((tokens, LANES), whole),
                pl.BlockSpec((None, HEADS_TILE, tokens), lambda p, j, s: (p, 0, 0)),
                pl.BlockSpec((tokens, LANES), whole),
            ],
            out_specs=[
                pl.BlockSpec((tokens, LANES), whole),
                pl.BlockSpec((block_k, LANES), lambda p, j, s: (j, p)),
                pl.BlockSpec((block_k, LANES), lambda p, j, s: (j, p)),
            ],
            scratch_shapes=[
                pltpu.VMEM((LANES, tokens), F32),
                pltpu.VMEM((block_k, LANES), F32),
                pltpu.VMEM((block_k, LANES), F32),
                pltpu.VMEM((HEADS_TILE, tokens), F32),
            ],
        ),
        out_shape=[
            jax.ShapeDtypeStruct((tokens, columns), F32),
            jax.ShapeDtypeStruct((total_keys, columns), BF16),
            jax.ShapeDtypeStruct((total_keys, columns), BF16),
        ],
        compiler_params=pltpu.CompilerParams(vmem_limit_bytes=VMEM_BYTES),
        cost_estimate=pl.CostEstimate(
            flops=flops, bytes_accessed=12 * (tokens + total_keys) * columns, transcendentals=0
        ),
        name="attend_backward",
    )(scalars, queries, keys, values, starts, exact, logs, mixed_grad)


def core_half(value, axis, which):
    size = value.shape[axis] // lax.axis_size("core")
    return lax.dynamic_slice_in_dim(value, which * size, size, axis)


def spread_weights(weight, axis):
    core = lax.axis_index("core")
    own = core_half(weight, axis, core)
    other = swap_core(core_half(weight, axis, 1 - core))
    return own, other


def per_device(
    layer_input,
    segment_ids,
    positions,
    norm_gain,
    norm_bias,
    qkv_weight,
    qkv_bias,
    dense_weight,
    dense_bias,
    up_weight,
    up_bias,
    down_weight,
    down_bias,
    output_cotangent,
):
    layer_count = qkv_weight.shape[0]
    core = lax.axis_index("core")
    x = lax.axis_index("x")
    n_x = lax.axis_size("x")
    own_tokens = layer_input.shape[0]
    tokens = own_tokens * lax.axis_size("core")
    full_width = layer_input.shape[1] * lax.axis_size("col")
    columns = qkv_weight.shape[3] // lax.axis_size("core")
    hidden = up_weight.shape[2] // lax.axis_size("core")
    heads = columns // HEAD_DIM
    query_begin = x * tokens
    query_segments = lax.dynamic_slice_in_dim(segment_ids, query_begin, tokens, 0)
    query_places = lax.dynamic_slice_in_dim(positions, query_begin, tokens, 0)
    starts = jnp.sum(
        (segment_ids[:, None] < query_segments[None, :]).astype(jnp.int32), axis=0, keepdims=True
    )
    cosine_table, sine_table = rotation_tables(query_places)
    table = width_table()

    def weights_of(layer):
        qkv_own, qkv_other = spread_weights(qkv_weight[layer], 2)
        qkv_block = jnp.concatenate([qkv_own, qkv_other], axis=0).reshape(-1, 3 * columns)
        up_own, up_other = spread_weights(up_weight[layer], 1)
        up_block = jnp.concatenate([up_own, up_other], axis=0)
        joined = jnp.concatenate(
            [
                jnp.concatenate(spread_weights(dense_weight[layer], 0), axis=1),
                jnp.concatenate(spread_weights(down_weight[layer], 0), axis=1),
            ],
            axis=0,
        )
        return (
            jnp.concatenate(gather_blocks(qkv_block), axis=0),
            jnp.concatenate(gather_blocks(up_block), axis=0),
            jnp.concatenate(gather_blocks(joined), axis=1),
        )

    def all_features(block):
        features = lax.all_gather(block, "col", axis=1, tiled=True)
        return to_own_order(features, swap_core(features), table)

    def to_owner(partial):
        away = lax.dynamic_slice_in_dim(partial, (1 - core) * own_tokens, own_tokens, 0)
        summed = from_own_order(partial, swap_core(away), table)
        return lax.psum_scatter(summed, "col", scatter_dimension=1, tiled=True).astype(F32)

    def join_x(local):
        whole = jnp.zeros((n_x * local.shape[0], local.shape[1]), local.dtype)
        for k in range(n_x):
            piece = local if k == 0 else shift(local, "x", k)
            place = (x - k + n_x) % n_x
            whole = lax.dynamic_update_slice_in_dim(whole, piece, place * local.shape[0], 0)
        return whole

    weights = [weights_of(layer) for layer in range(layer_count)]
    residual = layer_input.astype(F32)
    outputs = []
    kept = []
    for layer in range(layer_count):
        qkv_all, up_all, out_all = weights[layer]
        stats = jnp.stack([jnp.sum(residual, axis=1), jnp.sum(residual * residual, axis=1)])
        stats = small_sum(stats, ("col",)) / full_width
        center = stats[0]
        inverse = lax.rsqrt(stats[1] - center * center + EPSILON)
        centred = (residual - center[:, None]) * inverse[:, None]
        normed = (centred * norm_gain[layer] + norm_bias[layer]).astype(BF16)
        features = all_features(normed)
        qkv_shift = core_half(qkv_bias[layer], 1, core).reshape(-1)
        up_shift = core_half(up_bias[layer], 0, core)
        projected = jnp.dot(features, qkv_all, preferred_element_type=F32) + qkv_shift
        shaped = projected.reshape(tokens, 3, heads, HEAD_DIM)
        queries = rotate(shaped[:, 0], cosine_table, sine_table).astype(BF16)
        keys = rotate(shaped[:, 1], cosine_table, sine_table).astype(BF16)
        key_values = jnp.concatenate(
            [keys.reshape(tokens, columns), shaped[:, 2].astype(BF16).reshape(tokens, columns)],
            axis=1,
        )
        queries = queries.reshape(tokens, columns)
        key_values = join_x(key_values)
        all_keys, all_values = key_values[:, :columns], key_values[:, columns:]
        mixed, exact, logs = attend_forward(queries, all_keys, all_values, starts, query_begin)
        expanded = jnp.dot(features, up_all, preferred_element_type=F32) + up_shift
        activated = gelu_curve(expanded).astype(BF16)
        inner = jnp.concatenate([mixed, activated], axis=1)
        partial = jnp.dot(inner, out_all, preferred_element_type=F32).astype(BF16)
        residual = residual + to_owner(partial) + dense_bias[layer] + down_bias[layer]
        outputs.append(residual)
        kept.append(
            (centred, inverse, features, queries, all_keys, all_values, exact, logs, expanded, inner)
        )

    gradient = output_cotangent.astype(F32)
    small_terms = [None] * layer_count
    weight_terms = [None] * layer_count
    for layer in reversed(range(layer_count)):
        centred, inverse, features, queries, all_keys, all_values, exact, logs, expanded, inner = kept[
            layer
        ]
        qkv_all, up_all, out_all = weights[layer]
        grad_features = all_features(gradient.astype(BF16))
        mixed_grad = contract(grad_features, out_all[:columns], 1, 1).astype(BF16)
        active_grad = contract(grad_features, out_all[columns:], 1, 1)
        up_low = jax.vjp(gelu_curve, expanded)[1](active_grad)[0].astype(BF16)
        query_grad, key_grads, value_grads = attend_backward(
            queries, all_keys, all_values, starts, query_begin, exact, logs, mixed_grad
        )
        pair_grads = jnp.concatenate([key_grads, value_grads], axis=1)
        pair_grad = lax.dynamic_slice_in_dim(pair_grads, query_begin, tokens, 0).astype(F32)
        for k in range(1, n_x):
            place = (x - k + n_x) % n_x
            away = lax.dynamic_slice_in_dim(pair_grads, place * tokens, tokens, 0)
            pair_grad = pair_grad + shift(away, "x", -k).astype(F32)
        query_pre = rotate(
            query_grad.reshape(tokens, heads, HEAD_DIM), cosine_table, -sine_table
        ).reshape(tokens, columns)
        key_pre = rotate(
            pair_grad[:, :columns].reshape(tokens, heads, HEAD_DIM), cosine_table, -sine_table
        ).reshape(tokens, columns)
        qkv_low = jnp.concatenate([query_pre, key_pre, pair_grad[:, columns:]], axis=1).astype(BF16)
        feature_grad = (
            contract(qkv_low, qkv_all, 1, 1) + contract(up_low, up_all, 1, 1)
        ).astype(BF16)
        normed_grad = to_owner(feature_grad)
        scaled_grad = normed_grad * norm_gain[layer]
        sums = jnp.stack(
            [jnp.sum(scaled_grad, axis=1), jnp.sum(scaled_grad * centred, axis=1)]
        )
        sums = small_sum(sums, ("col",)) / full_width

        out_term = contract(inner, grad_features, 0, 0).astype(BF16)
        qkv_term = contract(features, qkv_low, 0, 0).astype(BF16)
        up_term = contract(features, up_low, 0, 0).astype(BF16)
        places = lax.axis_size("dp") * n_x
        block = full_width // places
        cut = lambda term, axis: [
            lax.slice_in_dim(term, i * block, (i + 1) * block, axis=axis) for i in range(places)
        ]
        half = block // 2
        out_sum = scatter_blocks(cut(out_term, 1))
        out_mine = in_core_order(
            out_sum[:, :half], swap_core(out_sum[:, half:].astype(BF16)).astype(F32), 0
        )
        rows = columns + hidden
        dense_mine = jnp.concatenate([out_mine[:columns], out_mine[rows : rows + columns]], axis=0)
        down_mine = jnp.concatenate([out_mine[columns:rows], out_mine[rows + columns :]], axis=0)
        up_sum = scatter_blocks(cut(up_term, 0))
        up_mine = in_core_order(up_sum[:half], swap_core(up_sum[half:].astype(BF16)).astype(F32), 1)
        qkv_sum = scatter_blocks(cut(qkv_term, 0))
        qkv_mine = in_core_order(
            qkv_sum[:half].reshape(half, 3, columns),
            swap_core(qkv_sum[half:].astype(BF16)).astype(F32).reshape(half, 3, columns),
            2,
        )
        weight_terms[layer] = (qkv_mine, dense_mine, up_mine, down_mine)

        def to_both(value):
            zero = jnp.zeros_like(value)
            return jnp.where(
                core == 0,
                jnp.concatenate([value, zero], axis=-1),
                jnp.concatenate([zero, value], axis=-1),
            ).reshape(-1)

        small = jnp.concatenate(
            [
                jnp.sum(normed_grad * centred, axis=0),
                jnp.sum(normed_grad, axis=0),
                to_both(jnp.sum(qkv_low, axis=0, dtype=F32).reshape(3, columns)),
                jnp.sum(gradient, axis=0),
                to_both(jnp.sum(up_low, axis=0, dtype=F32)),
            ]
        )
        small_terms[layer] = small_sum(small, ("core", "x", "dp"))
        gradient = gradient + inverse[:, None] * (
            scaled_grad - sums[0][:, None] - centred * sums[1][:, None]
        )

    small = jnp.stack(small_terms)
    width = layer_input.shape[1]
    both = 2 * columns
    ends = [0]
    for size in (width, width, 3 * both, width, 2 * hidden):
        ends.append(ends[-1] + size)
    gain_grad, shift_grad, qkv_grad, out_bias_grad, up_grad = [
        small[:, begin:end] for begin, end in zip(ends[:-1], ends[1:])
    ]
    return (
        jnp.stack(outputs),
        gradient,
        gain_grad,
        shift_grad,
        jnp.stack([terms[0] for terms in weight_terms]),
        qkv_grad.reshape(layer_count, 3, both),
        jnp.stack([terms[1] for terms in weight_terms]),
        out_bias_grad,
        jnp.stack([terms[2] for terms in weight_terms]),
        up_grad,
        jnp.stack([terms[3] for terms in weight_terms]),
        out_bias_grad,
    )


def solution(mesh):
    n_y, n_row, n_z = (mesh.shape[name] for name in ("dp", "row", "col"))
    split = Mesh(mesh.devices.reshape(n_y, n_row // 2, 2, n_z), ("dp", "x", "core", "col"))
    rows = ("dp", "x", "core")
    placed = (
        P(rows, "col"),
        P("dp"),
        P("dp"),
        P(None, "col"),
        P(None, "col"),
        P(None, rows, None, "col"),
        P(None, None, "col"),
        P(None, "col", rows),
        P(None, "col"),
        P(None, rows, "col"),
        P(None, "col"),
        P(None, "col", rows),
        P(None, "col"),
        P(rows, "col"),
    )
    return jax.shard_map(
        per_device,
        mesh=split,
        in_specs=placed,
        out_specs=(
            P(None, rows, "col"),
            P(rows, "col"),
            P(None, "col"),
            P(None, "col"),
            P(None, rows, None, "col"),
            P(None, None, "col"),
            P(None, "col", rows),
            P(None, "col"),
            P(None, rows, "col"),
            P(None, "col"),
            P(None, "col", rows),
            P(None, "col"),
        ),
        check_vma=False,
    )
```

```python
import math

import jax
import jax.numpy as jnp
from jax import lax
from jax.experimental import pallas as pl
from jax.experimental.pallas import tpu as pltpu
from jax.sharding import Mesh
from jax.sharding import PartitionSpec as P

HEAD_DIM = 64
ROT = 32
EPSILON = 1e-05
NEGATIVE = -1e30
LANES = 128
HEADS_TILE = LANES // HEAD_DIM
VMEM_BYTES = 40 * 1024 * 1024
F32 = jnp.float32
BF16 = jnp.bfloat16
ANY = pl.BlockSpec(memory_space=pl.ANY)
COST = pl.CostEstimate(flops=1, bytes_accessed=1, transcendentals=0)


def contract(left, right, left_dim, right_dim):
    return lax.dot_general(
        left, right, (((left_dim,), (right_dim,)), ((), ())), preferred_element_type=F32
    )


def shift(value, axis, step):
    size = lax.axis_size(axis)
    return lax.ppermute(value, axis, [(i, (i + step) % size) for i in range(size)])


def swap_core(value):
    return shift(value, "core", 1)


class Order:
    def __init__(self):
        self.last = []
        self.links = {}
        self.newest = {}

    def now(self, values):
        def one(value):
            while id(value) in self.newest:
                value = self.newest[id(value)][1]
            return value

        return jax.tree.map(one, values)

    def after(self, values, *others):
        leaves, tree = jax.tree.flatten(self.now(values))
        held = self.now([other for other in (*self.last, *others) if other is not None])
        every = {id(value): value for value in (*leaves, *held)}
        if held:
            for old, new in zip(every.values(), lax.optimization_barrier(tuple(every.values()))):
                self.newest[id(old)] = (old, new)
        return self.now(jax.tree.unflatten(tree, leaves))

    def run(self, function, *values):
        out = function(*self.after(values))
        self.last = jax.tree.leaves(out)
        return out

    def send(self, value, axis, step, depth=2):
        queue = self.links.setdefault(axis, [])
        held = queue[-depth] if len(queue) >= depth else None
        out = shift(self.after([value], held)[0], axis, step)
        queue.append(out)
        return out

    def wait(self, *values):
        out = self.after(list(values))
        self.last = [*self.last, *out]
        return out


def sum_over(value, axis):
    size = lax.axis_size(axis)
    if size & (size - 1):
        return value + sum(shift(value, axis, k) for k in range(1, size))
    step = 1
    while step < size:
        value = value + lax.ppermute(value, axis, [(i, i ^ step) for i in range(size)])
        step *= 2
    return value


def width_table(layout):
    n_y, n_x, n_c = lax.axis_size("dp"), lax.axis_size("x"), lax.axis_size("core")
    y, x, c = lax.axis_index("dp"), lax.axis_index("x"), lax.axis_index("core")
    begins = jnp.stack(
        [
            ((((y - a + n_y) % n_y) * n_x + (x - b + n_x) % n_x) * n_c + (c - k + n_c) % n_c)
            * layout.place
            for a in range(n_y)
            for b in range(n_x)
            for k in range(n_c)
        ]
    )
    return jnp.concatenate(
        [begins // layout.part, begins % layout.part, c[None], begins]
    ).astype(jnp.int32)


class Layout:
    def __init__(self, own_tokens, part):
        self.n_y, self.n_x, self.n_c, self.n_z = (
            lax.axis_size(name) for name in ("dp", "x", "core", "col")
        )
        self.own_tokens = own_tokens
        self.tokens = own_tokens * self.n_c
        self.part = part
        self.width = part * self.n_z
        self.places = self.n_y * self.n_x * self.n_c
        self.place = self.width // self.places
        self.block = self.place * self.n_c
        self.blocks = self.n_y * self.n_x

    def fetch(self, table, gathered, core, places, target, sems, first):
        copies = []
        for slot, at in enumerate(places):
            begin = pl.multiple_of(table[self.places + at], self.place)
            copies.append(
                pltpu.make_async_copy(
                    gathered.at[core * self.n_z + table[at], :, pl.ds(begin, self.place)],
                    target.at[:, slot * self.place : (slot + 1) * self.place],
                    sems.at[first + slot],
                )
            )
        return copies


def kernel_call(body, table, inputs, in_specs, out_shape, out_specs, scratch, name, grid=(1,), aliases=None):
    return pl.pallas_call(
        body,
        grid_spec=pltpu.PrefetchScalarGridSpec(
            num_scalar_prefetch=1,
            grid=grid,
            in_specs=in_specs,
            out_specs=out_specs,
            scratch_shapes=scratch,
        ),
        out_shape=out_shape,
        input_output_aliases=aliases or {},
        compiler_params=pltpu.CompilerParams(vmem_limit_bytes=VMEM_BYTES),
        cost_estimate=COST,
        name=name,
    )(table, *inputs)


def full(array_or_shape):
    shape = getattr(array_or_shape, "shape", array_or_shape)
    return pl.BlockSpec(tuple(shape), lambda i, t: (0,) * len(shape))


def start_all(copies):
    for copy in copies:
        copy.start()


def wait_all(copies):
    for copy in copies:
        copy.wait()


def rope(value, cosine, lower, upper):
    half = ROT // 2
    return (
        value * cosine
        + pltpu.roll(value, LANES - half, 1) * lower
        + pltpu.roll(value, half, 1) * upper
    )


def rope_tables(place_values):
    half = ROT // 2
    freq_table = 1.0 / 10000.0 ** (jnp.arange(half, dtype=F32) * 2.0 / ROT)
    angles = place_values.astype(F32)[:, None] * freq_table
    cosine, sine = jnp.cos(angles), jnp.sin(angles)
    rest = jnp.ones((angles.shape[0], HEAD_DIM - ROT), F32)
    none = jnp.zeros_like(sine)
    pair = lambda *pieces: jnp.concatenate(pieces * HEADS_TILE, axis=1)
    return (
        pair(cosine, cosine, rest),
        pair(-sine, none, 0.0 * rest),
        pair(none, sine, 0.0 * rest),
    )


class Stream:
    def __init__(self, layout, table, gathered, weights, features, buffers, sems, w_sems, window=None):
        self.layout, self.features, self.buffers = layout, features, buffers
        if window is not None:
            weights = [ref.at[:, window] for ref in weights]
        n_c = layout.n_c
        self.pieces = [
            [
                layout.fetch(
                    table,
                    gathered,
                    core,
                    range(b * n_c, (b + 1) * n_c),
                    features.at[core, b],
                    sems.at[core, b],
                    0,
                )
                for b in range(layout.blocks)
            ]
            for core in range(n_c)
        ]
        self.weights = [
            pltpu.make_async_copy(ref, buffer, w_sems.at[b])
            for b, (ref, buffer) in enumerate(zip(weights, buffers))
        ]
        for core in range(n_c):
            for b in range(layout.blocks):
                if core == 0:
                    self.weights[b].start()
                start_all(self.pieces[core][b])

    def run(self, total, parts, product, finish):
        last = self.layout.blocks - 1
        for core in range(self.layout.n_c):
            for b in range(last + 1):
                if core == 0:
                    self.weights[b].wait()
                wait_all(self.pieces[core][b])
                for part in parts:
                    term = product(self.features[core, b], self.buffers[b], part)
                    if 0 < b:
                        term = total[:, part] + term
                    if b < last:
                        total[:, part] = term
                    else:
                        finish(core, part, term)

    @staticmethod
    def scratch(layout, shape, outputs):
        n_c, count = layout.n_c, layout.blocks
        return [
            pltpu.VMEM((n_c, count, layout.own_tokens, layout.block), BF16),
            *[pltpu.VMEM(shape, BF16) for _ in range(count)],
            pltpu.SemaphoreType.DMA((n_c, count, n_c)),
            pltpu.SemaphoreType.DMA((count,)),
            pltpu.VMEM((layout.own_tokens, outputs), F32),
        ]


def chunks(size, step=256):
    step = math.gcd(size, step)
    return [slice(begin, begin + step) for begin in range(0, size, step)]


def project_qkv(layout, table, gathered, blocks, bias, tables):
    columns = bias.shape[1] // 3
    rows, count = layout.own_tokens, layout.blocks

    def body(table_ref, g_ref, *rest):
        w_refs, rest = rest[:count], rest[count:]
        bias_ref, cos_ref, low_ref, up_ref, q_ref, kv_ref, features = rest[:7]
        buffers, (sems, w_sems, total) = rest[7 : 7 + count], rest[7 + count :]
        window = slice(0, 3 * columns)
        stream = Stream(layout, table_ref, g_ref, w_refs, features, buffers, sems, w_sems, window)

        def finish(core, part, value):
            here = slice(core * rows, (core + 1) * rows)
            value = value + bias_ref[:, part]
            for lanes in chunks(columns, LANES):
                piece = value[:, lanes]
                if part.start < 2 * columns:
                    piece = rope(piece, cos_ref[here], low_ref[here], up_ref[here])
                begin = part.start + lanes.start
                if part.start < columns:
                    q_ref[here, begin : begin + LANES] = piece.astype(BF16)
                else:
                    kv_ref[here, begin - columns : begin - columns + LANES] = piece.astype(BF16)

        stream.run(
            total,
            [slice(i * columns, (i + 1) * columns) for i in range(3)],
            lambda f, w, part: jnp.dot(f, w[:, part], preferred_element_type=F32),
            finish,
        )

    out = [
        jax.ShapeDtypeStruct((layout.tokens, columns), BF16),
        jax.ShapeDtypeStruct((layout.tokens, 2 * columns), BF16),
    ]
    return kernel_call(
        body,
        table,
        [gathered, *blocks, bias, *tables],
        [ANY] * (1 + count) + [full(bias)] + [full(t) for t in tables],
        out,
        [full(o) for o in out],
        Stream.scratch(layout, (layout.block, 3 * columns), 3 * columns),
        "project_qkv",
    )


def gelu_and_slope(v):
    inner = math.sqrt(2 / math.pi) * v * (1.0 + 0.044715 * v * v)
    curve = jnp.tanh(inner)
    slope = 0.5 * (1.0 + curve) + 0.5 * v * (1.0 - curve * curve) * math.sqrt(2 / math.pi) * (
        1.0 + 3 * 0.044715 * v * v
    )
    return 0.5 * v * (1.0 + curve), slope


def project_up(layout, table, gathered, blocks, bias, active_grad=None):
    hidden = bias.shape[1]
    window = slice(blocks[0].shape[1] - hidden, blocks[0].shape[1])
    rows, count = layout.own_tokens, layout.blocks
    known = active_grad is not None

    def body(table_ref, g_ref, *rest):
        w_refs, rest = rest[:count], rest[count:]
        if known:
            grad_ref, rest = rest[0], rest[1:]
        bias_ref, act_ref, slope_ref, features = rest[:4]
        buffers, (sems, w_sems, total, act_buf, slope_buf, out_sems) = rest[4 : 4 + count], rest[4 + count :]
        stream = Stream(layout, table_ref, g_ref, w_refs, features, buffers, sems, w_sems, window)
        outs = []
        parts = chunks(hidden)

        def finish(core, part, value):
            here = slice(core * rows, (core + 1) * rows)
            active, slope = gelu_and_slope(value + bias_ref[:, part])
            act_buf[here, part] = active.astype(BF16)
            if known:
                slope = slope * grad_ref[here, part].astype(F32)
            slope_buf[here, part] = slope.astype(BF16)
            if part.stop == hidden:
                for i, (buffer, ref) in enumerate(((act_buf, act_ref), (slope_buf, slope_ref))):
                    outs.append(
                        pltpu.make_async_copy(buffer.at[here], ref.at[here], out_sems.at[core, i])
                    )
                    outs[-1].start()

        stream.run(
            total,
            parts,
            lambda f, w, part: jnp.dot(f, w[:, part], preferred_element_type=F32),
            finish,
        )
        wait_all(outs)

    out = [jax.ShapeDtypeStruct((layout.tokens, hidden), BF16)] * 2
    extra = [active_grad] if known else []
    return kernel_call(
        body,
        table,
        [gathered, *blocks, *extra, bias],
        [ANY] * (1 + count) + [full(e) for e in extra] + [full(bias)],
        out,
        [ANY, ANY],
        Stream.scratch(layout, (layout.block, hidden), hidden)
        + [pltpu.VMEM((layout.tokens, hidden), BF16)] * 2
        + [pltpu.SemaphoreType.DMA((layout.n_c, 2))],
        "project_up",
    )


def branch_grads(layout, table, gathered, blocks, columns, slope=None):
    rows, count = layout.own_tokens, layout.blocks
    height = blocks[0].shape[0]
    hidden = height - columns
    known = slope is not None

    def body(table_ref, g_ref, *rest):
        w_refs, rest = rest[:count], rest[count:]
        if known:
            slope_ref, rest = rest[0], rest[1:]
        mixed_ref, hidden_ref, features = rest[:3]
        buffers, (sems, w_sems, total, mixed_buf, hidden_buf, out_sems) = (
            rest[3 : 3 + count],
            rest[3 + count :],
        )
        stream = Stream(layout, table_ref, g_ref, w_refs, features, buffers, sems, w_sems)
        outs = []

        def finish(core, part, value):
            here = slice(core * rows, (core + 1) * rows)
            if part.start < columns:
                mixed_buf[here, part] = value.astype(BF16)
            else:
                to = slice(part.start - columns, part.stop - columns)
                if known:
                    value = value * slope_ref[here, to].astype(F32)
                hidden_buf[here, to] = value.astype(BF16)
            if part.stop == height:
                for i, (buffer, ref) in enumerate(((mixed_buf, mixed_ref), (hidden_buf, hidden_ref))):
                    outs.append(
                        pltpu.make_async_copy(buffer.at[here], ref.at[here], out_sems.at[core, i])
                    )
                    outs[-1].start()

        stream.run(
            total,
            chunks(height, math.gcd(columns, 256)),
            lambda f, w, part: contract(f, w[part, :], 1, 1),
            finish,
        )
        wait_all(outs)

    out = [
        jax.ShapeDtypeStruct((layout.tokens, columns), BF16),
        jax.ShapeDtypeStruct((layout.tokens, hidden), BF16),
    ]
    extra = [slope] if known else []
    return kernel_call(
        body,
        table,
        [gathered, *blocks, *extra],
        [ANY] * (1 + count) + [full(e) for e in extra],
        out,
        [ANY, ANY],
        Stream.scratch(layout, blocks[0].shape, height)
        + [pltpu.VMEM(o.shape, BF16) for o in out]
        + [pltpu.SemaphoreType.DMA((layout.n_c, 2))],
        "branch_grads",
    )


def project_back(layout, table, lefts, weights, transposed, name):
    rows, count = layout.own_tokens, len(weights)
    per_block = len(weights[0])
    sizes = [left.shape[1] for left in lefts]
    flat = [w for block in weights for w in block]
    n = len(lefts)

    def body(table_ref, *rest):
        left_refs, rest = rest[:n], rest[n:]
        w_refs, rest = rest[: len(flat)], rest[len(flat) :]
        out_refs, rest = rest[:3], rest[3:]
        left_bufs, rest = rest[:n], rest[n:]
        w_bufs, (out_buf, sems, w_sems, out_sems) = rest[: len(flat)], rest[len(flat) :]
        core = table_ref[2 * layout.places]
        copies = []
        for half, which in enumerate((lax.rem(core + 1, layout.n_c), core)):
            begin = pl.multiple_of(which * rows, rows)
            copies.append(
                [
                    pltpu.make_async_copy(
                        ref.at[pl.ds(begin, rows), :], buf.at[half], sems.at[half, i]
                    )
                    for i, (ref, buf) in enumerate(zip(left_refs, left_bufs))
                ]
            )
        w_copies = [
            pltpu.make_async_copy(ref, buf, w_sems.at[i])
            for i, (ref, buf) in enumerate(zip(w_refs, w_bufs))
        ]
        start_all(copies[0] + w_copies)
        start_all(copies[1])
        outs = []
        for half in range(2):
            wait_all(copies[half])
            for b in range(count):
                if half == 0:
                    wait_all(w_copies[b * per_block : (b + 1) * per_block])
                total = None
                at = 0
                for i, buf in enumerate(left_bufs):
                    if per_block == 1:
                        here = slice(at, at + sizes[i])
                        w = w_bufs[b][:, here] if transposed else w_bufs[b][here, :]
                        at += sizes[i]
                    else:
                        w = w_bufs[b * per_block + i][...]
                    term = contract(buf[half], w, 1, 1 if transposed else 0)
                    total = term if total is None else total + term
                out_buf[half, :, b * layout.block : (b + 1) * layout.block] = total.astype(BF16)
            pieces = [out_buf.at[0, : rows // 2], out_buf.at[0, rows // 2 :]] if half == 0 else [out_buf.at[1]]
            for piece in pieces:
                at = len(outs)
                outs.append(pltpu.make_async_copy(piece, out_refs[at], out_sems.at[at]))
                outs[-1].start()
        wait_all(outs)

    out = [jax.ShapeDtypeStruct((size, layout.width), BF16) for size in (rows // 2, rows // 2, rows)]
    return kernel_call(
        body,
        table,
        [*lefts, *flat],
        [ANY] * (n + len(flat)),
        out,
        [ANY] * 3,
        [pltpu.VMEM((2, rows, size), BF16) for size in sizes]
        + [pltpu.VMEM(w.shape, BF16) for w in flat]
        + [
            pltpu.VMEM((2, rows, layout.width), BF16),
            pltpu.SemaphoreType.DMA((2, n)),
            pltpu.SemaphoreType.DMA((len(flat),)),
            pltpu.SemaphoreType.DMA((3,)),
        ],
        name,
    )


def merge_cores(layout, table, own, received):
    rows = layout.own_tokens // 2
    place, places, n_c = layout.place, layout.places, layout.n_c

    def body(table_ref, own_ref, first_ref, second_ref, out_ref):
        def write(other_ref):
            for at in range(places):
                begin = pl.multiple_of(table_ref[2 * places + 1 + at], place)
                there = at // n_c * n_c + (n_c - at % n_c) % n_c if n_c != 2 else at ^ 1
                total = own_ref[:, at * place : (at + 1) * place].astype(F32)
                total = total + other_ref[:, there * place : (there + 1) * place].astype(F32)
                out_ref[:, pl.ds(begin, place)] = total.astype(BF16)

        pl.when(pl.program_id(0) == 0)(lambda: write(first_ref))
        pl.when(pl.program_id(0) == 1)(lambda: write(second_ref))

    spec = pl.BlockSpec((rows, layout.width), lambda i, t: (i, 0))
    return kernel_call(
        body,
        table,
        [own, *received],
        [spec] + [full(piece) for piece in received],
        jax.ShapeDtypeStruct((layout.own_tokens, layout.width), BF16),
        spec,
        [],
        "merge_cores",
        grid=(2,),
    )


def fetch_blocks(layout, table, gathered, which, features, sems):
    n_c, rows = layout.n_c, layout.own_tokens
    return [
        [
            layout.fetch(
                table,
                gathered,
                core,
                range(b * n_c, (b + 1) * n_c),
                features.at[i, pl.ds(core * rows, rows), :],
                sems.at[i, core],
                0,
            )
            for core in range(n_c)
        ]
        for i, b in enumerate(which)
    ]


def grad_in(layout, table, gathered, right, which, added=None):
    n = right.shape[1]
    count, place, n_c, block = len(which), layout.place, layout.n_c, layout.block
    final = added is not None
    extra = list(added or [])

    def body(table_ref, g_ref, right_ref, *rest):
        add_refs, rest = rest[: len(extra)], rest[len(extra) :]
        outs, rest = rest[: len(out)], rest[len(out) :]
        features, right_buf, sems, right_sem, rest = *rest[:4], rest[4:]
        pieces = fetch_blocks(layout, table_ref, g_ref, which, features, sems)
        right_copy = pltpu.make_async_copy(right_ref, right_buf, right_sem)
        right_copy.start()
        for group in pieces:
            for piece in group:
                start_all(piece)
        add_bufs, rest = rest[: len(extra)], rest[len(extra) :]
        if final:
            add_sems, rest = rest[0], rest[1:]
            add_copies = [
                pltpu.make_async_copy(ref, buf, add_sems.at[i])
                for i, (ref, buf) in enumerate(zip(add_refs, add_bufs))
            ]
            start_all(add_copies)
        right_copy.wait()
        if not final:
            out_buf, out_sems = rest
        copies = []
        for i in range(count):
            for piece in pieces[i]:
                wait_all(piece)
            if final and i == 0:
                wait_all(add_copies)
            for k in range(n_c):
                value = contract(features[i, :, k * place : (k + 1) * place], right_buf[...], 0, 0)
                begin = i * block + k * place
                if not final:
                    out_buf[begin : begin + place, :] = value.astype(BF16)
                    continue
                for buf in add_bufs:
                    value = value + buf[begin : begin + place, :].astype(F32)
                if k > 0:
                    away = outs[2] if i == 0 else outs[3]
                    at = (max(i - 1, 0) * (n_c - 1) + k - 1) * place
                    away[at : at + place, :] = value.astype(BF16)
                elif i == 0:
                    outs[0][...] = value
                else:
                    outs[1][(i - 1) * place : i * place, :] = value.astype(BF16)
            if not final:
                here = slice(i * block, (i + 1) * block)
                copies.append(pltpu.make_async_copy(out_buf.at[here], outs[0].at[here], out_sems.at[i]))
                copies[-1].start()
        wait_all(copies)

    if final:
        away = (n_c - 1) * place
        out = [
            jax.ShapeDtypeStruct((place, n), F32),
            jax.ShapeDtypeStruct(((count - 1) * place, n), BF16),
            jax.ShapeDtypeStruct((away, n), BF16),
            jax.ShapeDtypeStruct(((count - 1) * away, n), BF16),
        ]
        more = [pltpu.VMEM(e.shape, BF16) for e in extra]
        more.append(pltpu.SemaphoreType.DMA((len(extra),)))
    else:
        out = [jax.ShapeDtypeStruct((count * block, n), BF16)]
        more = [pltpu.VMEM(out[0].shape, BF16), pltpu.SemaphoreType.DMA((count,))]
    return kernel_call(
        body,
        table,
        [gathered, right, *extra],
        [ANY] * (2 + len(extra)),
        out,
        [full(o) for o in out] if final else [ANY],
        [
            pltpu.VMEM((count, layout.tokens, block), BF16),
            pltpu.VMEM(right.shape, BF16),
            pltpu.SemaphoreType.DMA((count, n_c, n_c)),
            pltpu.SemaphoreType.DMA,
        ]
        + more,
        "grad_in",
    )


def grad_out(layout, table, lefts, gathered, which, added=None):
    sizes = [left.shape[1] for left in lefts]
    m, n = sum(sizes), len(lefts)
    count, place, n_c, block = len(which), layout.place, layout.n_c, layout.block
    final = added is not None
    extra = [e for block_added in added for e in block_added] if final else []
    per_block = len(extra) // count

    def body(table_ref, g_ref, *rest):
        left_refs, rest = rest[:n], rest[n:]
        add_refs, rest = rest[: len(extra)], rest[len(extra) :]
        outs, rest = rest[: len(out)], rest[len(out) :]
        features, sems, left_sems, rest = *rest[:3], rest[3:]
        left_bufs, rest = rest[:n], rest[n:]
        left_copies = [
            pltpu.make_async_copy(ref, buf, left_sems.at[i])
            for i, (ref, buf) in enumerate(zip(left_refs, left_bufs))
        ]
        pieces = fetch_blocks(layout, table_ref, g_ref, which, features, sems)
        start_all(left_copies[:1])
        for piece in pieces[0]:
            start_all(piece)
        start_all(left_copies[1:])
        for group in pieces[1:]:
            for piece in group:
                start_all(piece)
        add_bufs, rest = rest[: len(extra)], rest[len(extra) :]
        if final:
            add_sems, rest = rest[0], rest[1:]
            add_copies = [
                pltpu.make_async_copy(ref, buf, add_sems.at[i])
                for i, (ref, buf) in enumerate(zip(add_refs, add_bufs))
            ]
            start_all(add_copies)
        if not final:
            out_buf, out_sems = rest
        copies = []
        for i in range(count):
            for piece in pieces[i]:
                wait_all(piece)
            if final:
                wait_all(add_copies[i * per_block : (i + 1) * per_block])
            at = 0
            for j, (left_buf, size) in enumerate(zip(left_bufs, sizes)):
                if i == 0:
                    left_copies[j].wait()
                for part in chunks(size):
                    rows = slice(at + part.start, at + part.stop)
                    value = contract(left_buf[:, part], features[i], 0, 0)
                    if not final:
                        out_buf[i, rows, :] = value.astype(BF16)
                        continue
                    for buf in add_bufs[i * per_block : (i + 1) * per_block]:
                        value = value + buf[rows, :].astype(F32)
                    if i == 0:
                        outs[0][rows, :] = value[:, :place]
                        outs[2][rows, :] = value[:, place:].astype(BF16)
                    else:
                        outs[1][i - 1, rows, :] = value[:, :place].astype(BF16)
                        outs[3][i - 1, rows, :] = value[:, place:].astype(BF16)
                at += size
            if not final:
                copies.append(pltpu.make_async_copy(out_buf.at[i], outs[i], out_sems.at[i]))
                copies[-1].start()
        wait_all(copies)

    if final:
        out = [
            jax.ShapeDtypeStruct((m, place), F32),
            jax.ShapeDtypeStruct((count - 1, m, place), BF16),
            jax.ShapeDtypeStruct((m, block - place), BF16),
            jax.ShapeDtypeStruct((count - 1, m, block - place), BF16),
        ]
        more = [pltpu.VMEM(e.shape, BF16) for e in extra]
        more.append(pltpu.SemaphoreType.DMA((len(extra),)))
    else:
        out = [jax.ShapeDtypeStruct((m, block), BF16)] * count
        more = [pltpu.VMEM((count, m, block), BF16), pltpu.SemaphoreType.DMA((count,))]
    return kernel_call(
        body,
        table,
        [gathered, *lefts, *extra],
        [ANY] * (1 + n + len(extra)),
        out,
        [full(o) for o in out] if final else [ANY] * count,
        [
            pltpu.VMEM((count, layout.tokens, block), BF16),
            pltpu.SemaphoreType.DMA((count, n_c, n_c)),
            pltpu.SemaphoreType.DMA((n,)),
        ]
        + [pltpu.VMEM(left.shape, BF16) for left in lefts]
        + more,
        "grad_out",
    )


def place_in(layout, table, layer, owns, others, shape, held, parts):
    rows, n = owns[0].shape
    step = n // parts
    inputs = [*owns, *others]

    def body(table_ref, *refs):
        refs, out_ref = refs[: len(inputs)], refs[-1]

        def write(sources):
            value = sum(ref[...].astype(F32) for ref in sources)
            if parts == 1:
                out_ref[...] = value
            else:
                for i in range(parts):
                    out_ref[:, i, :] = value[:, i * step : (i + 1) * step]

        pl.when(pl.program_id(0) == 0)(lambda: write(refs[: len(owns)]))
        pl.when(pl.program_id(0) == 1)(lambda: write(refs[len(owns) :]))

    half = lambda i, t: lax.rem(t[2 * layout.places] + i, layout.n_c)
    if parts == 1:
        spec = pl.BlockSpec((None, rows, n), lambda i, t: (layer, 0, half(i, t)))
    else:
        spec = pl.BlockSpec((None, rows, parts, step), lambda i, t: (layer, 0, 0, half(i, t)))
    more = [] if held is None else [held]
    return kernel_call(
        body,
        table,
        inputs + more,
        [full(v) for v in inputs] + [ANY] * len(more),
        jax.ShapeDtypeStruct(shape, F32),
        spec,
        [],
        "place_in",
        grid=(2,),
        aliases={1 + len(inputs): 0} if more else None,
    )


def place_out(layout, table, layer, owns, others, shapes, held):
    m, place = owns[0].shape
    inputs = [*owns, *others]
    sizes = [shape[1] // layout.n_c for shape in shapes]
    more = [] if held is None else list(held)

    def body(table_ref, *refs):
        refs, out_refs = refs[: len(inputs)], refs[len(inputs) + len(more) :]

        def write(sources):
            at = 0
            for ref, size in zip(out_refs, sizes):
                ref[...] = sum(source[at : at + size, :].astype(F32) for source in sources)
                at += size

        pl.when(pl.program_id(0) == 0)(lambda: write(refs[: len(owns)]))
        pl.when(pl.program_id(0) == 1)(lambda: write(refs[len(owns) :]))

    half = lambda i, t: lax.rem(t[2 * layout.places] + i, layout.n_c)
    return kernel_call(
        body,
        table,
        inputs + more,
        [full(v) for v in inputs] + [ANY] * len(more),
        [jax.ShapeDtypeStruct(shape, F32) for shape in shapes],
        [pl.BlockSpec((None, size, place), lambda i, t: (layer, half(i, t), 0)) for size in sizes],
        [],
        "place_out",
        grid=(2,),
        aliases={1 + len(inputs) + i: i for i in range(len(more))} or None,
    )


def head_part(value, head):
    lane = lax.broadcasted_iota(jnp.int32, value.shape, 1)
    keep = (lane >= head * HEAD_DIM) & (lane < (head + 1) * HEAD_DIM)
    return jnp.where(keep, value, jnp.zeros_like(value))


def mask_bias(query_begin, key_begin, starts, shape, key_axis):
    key_place = key_begin + lax.broadcasted_iota(jnp.int32, shape, key_axis)
    query_place = query_begin + lax.broadcasted_iota(jnp.int32, shape, 1 - key_axis)
    allowed = (key_place >= starts) & (key_place <= query_place)
    return jnp.where(allowed, 0.0, NEGATIVE).astype(F32)


def attend(begins, queries, key_values, starts, before=None):
    tokens, columns = queries.shape
    own = before is None
    block_q = math.gcd(tokens, 256 if own else 512)
    heads, pairs = columns // HEAD_DIM, columns // LANES
    keys = key_values.shape[0]
    steps = tokens // block_q
    tall = LANES + 16

    def body(begin_ref, q_ref, kv_ref, start_ref, *rest):
        if not own:
            (old_ref, old_log_ref), rest = rest[:2], rest[2:]
        low_ref, mixed_ref, log_ref, turned = rest
        step = pl.program_id(0)

        @pl.when(step == 0)
        def _():
            for pair in range(pairs):
                there = slice(columns + pair * LANES, columns + (pair + 1) * LANES)
                turned[pair * tall : pair * tall + LANES, :] = kv_ref[:, there].T
                turned[pair * tall + LANES : (pair + 1) * tall, :] = jnp.ones((16, keys), BF16)

        def work(count, at):
            bias = mask_bias(
                begin_ref[0] + at * block_q, begin_ref[1], start_ref[...], (count, block_q), 0
            )
            for pair in range(pairs):
                here = slice(pair * LANES, (pair + 1) * LANES)
                q = q_ref[:, here] * jnp.asarray(HEAD_DIM**-0.5, BF16)
                shares, terms = [], []
                for head in range(HEADS_TILE):
                    index = HEADS_TILE * pair + head
                    score = contract(kv_ref[:count, here], head_part(q, head), 1, 1) + bias
                    top = jnp.max(score, axis=0, keepdims=True)
                    weight = jnp.exp(score - top).astype(BF16)
                    found = jnp.dot(
                        turned[pair * tall : (pair + 1) * tall, :count],
                        weight,
                        preferred_element_type=F32,
                    )
                    value = found[head * HEAD_DIM : (head + 1) * HEAD_DIM]
                    total = found[LANES : LANES + 1]
                    joined = top + jnp.log(total)
                    if own:
                        value = value * (1.0 / total)
                    else:
                        old = old_log_ref[index : index + 1, :]
                        most = jnp.maximum(old, joined)
                        joined = most + jnp.log(jnp.exp(old - most) + jnp.exp(joined - most))
                        value = value * jnp.exp(top - joined)
                        shares.append(jnp.broadcast_to(jnp.exp(old - joined), value.shape))
                    log_ref[index : index + 1, :] = joined
                    terms.append(value)
                value = jnp.concatenate(terms, axis=0).T
                if not own:
                    value = value + old_ref[:, here] * jnp.concatenate(shares, axis=0).T
                mixed_ref[:, here] = value
                low_ref[:, here] = value.astype(BF16)

        if own:
            for at in range(steps):
                pl.when(step == at)(lambda at=at: work((at + 1) * block_q, at))
        else:
            work(keys, step)

    row = lambda i, s: (i, 0)
    lane = lambda i, s: (0, i)
    wide = pl.BlockSpec((block_q, columns), row)
    slim = pl.BlockSpec((heads, block_q), lane)
    extra = [] if own else list(before)
    return kernel_call(
        body,
        begins,
        [queries, key_values, starts, *extra],
        [wide, full(key_values), pl.BlockSpec((1, block_q), lane)] + ([] if own else [wide, slim]),
        [
            jax.ShapeDtypeStruct((tokens, columns), BF16),
            jax.ShapeDtypeStruct((tokens, columns), F32),
            jax.ShapeDtypeStruct((heads, tokens), F32),
        ],
        [wide, wide, slim],
        [pltpu.VMEM((pairs * tall, keys), BF16)],
        "attend_own" if own else "attend_far",
        grid=(steps,),
    )


def attend_backward(begins, queries, key_values, starts, mixed, logs, mixed_grad, own, before=None):
    tokens, columns = queries.shape
    block_q = math.gcd(tokens, 256)
    heads = columns // HEAD_DIM
    keys = key_values.shape[0]
    steps = tokens // block_q
    scale = HEAD_DIM**-0.5
    pairs = columns // LANES

    def body(begin_ref, q_ref, kv_ref, start_ref, mixed_ref, log_ref, grad_ref, *rest):
        if before is not None:
            before_ref, rest = rest[0], rest[1:]
        dq_ref, dkv_ref, turned, key_sum, value_sum = rest
        step = pl.program_id(0)

        @pl.when(step == 0)
        def _():
            key_sum[...] = jnp.zeros_like(key_sum)
            value_sum[...] = jnp.zeros_like(value_sum)
            for pair in range(pairs):
                here = slice(pair * LANES, (pair + 1) * LANES)
                turned[here, :] = kv_ref[:, here].T

        def work(count, at):
            bias = mask_bias(
                begin_ref[0] + at * block_q, begin_ref[1], start_ref[...], (count, block_q), 0
            )
            for pair in range(pairs):
                here = slice(pair * LANES, (pair + 1) * LANES)
                there = slice(columns + pair * LANES, columns + (pair + 1) * LANES)
                q, grad = q_ref[:, here], grad_ref[:, here]
                product = (mixed_ref[:, here] * grad.astype(F32)).T
                k, v = kv_ref[:count, here], kv_ref[:count, there]
                key_terms, value_terms, query_terms = [], [], []
                for head in range(HEADS_TILE):
                    q_head, grad_head = head_part(q, head), head_part(grad, head)
                    inner = slice(head * HEAD_DIM, (head + 1) * HEAD_DIM)
                    delta = jnp.sum(product[inner], axis=0, keepdims=True)
                    index = HEADS_TILE * pair + head
                    score = contract(k, q_head, 1, 1) * scale + bias
                    weight = jnp.exp(score - log_ref[index : index + 1, :])
                    weight_grad = contract(v, grad_head, 1, 1)
                    score_grad = (weight * (weight_grad - delta)).astype(BF16)
                    value_terms.append(
                        jnp.dot(weight.astype(BF16), grad_head, preferred_element_type=F32)
                    )
                    key_terms.append(jnp.dot(score_grad, q_head, preferred_element_type=F32))
                    begin = pair * LANES + head * HEAD_DIM
                    query_terms.append(
                        jnp.dot(
                            turned[begin : begin + HEAD_DIM, :count],
                            score_grad,
                            preferred_element_type=F32,
                        )
                    )
                value_sum[:count, here] += value_terms[0] + value_terms[1]
                key_sum[:count, here] += key_terms[0] + key_terms[1]
                found = jnp.concatenate(query_terms, axis=0).T * scale
                if before is not None:
                    found = found + before_ref[:, here]
                dq_ref[:, here] = found

        if own:
            for at in range(steps):
                pl.when(step == at)(lambda at=at: work((at + 1) * block_q, at))
        else:
            work(keys, step)

        @pl.when(step == steps - 1)
        def _():
            dkv_ref[:, :columns] = (key_sum[...] * scale).astype(dkv_ref.dtype)
            dkv_ref[:, columns:] = value_sum[...].astype(dkv_ref.dtype)

    row = lambda i, s: (i, 0)
    lane = lambda i, s: (0, i)
    wide = pl.BlockSpec((block_q, columns), row)
    extra = [] if before is None else [before]
    out = [
        jax.ShapeDtypeStruct((tokens, columns), F32),
        jax.ShapeDtypeStruct((keys, 2 * columns), F32 if own else BF16),
    ]
    return kernel_call(
        body,
        begins,
        [queries, key_values, starts, mixed, logs, mixed_grad, *extra],
        [
            wide,
            full(key_values),
            pl.BlockSpec((1, block_q), lane),
            wide,
            pl.BlockSpec((heads, block_q), lane),
            wide,
        ]
        + [wide] * len(extra),
        out,
        [wide, full(out[1])],
        [
            pltpu.VMEM((columns, keys), BF16),
            pltpu.VMEM((keys, columns), F32),
            pltpu.VMEM((keys, columns), F32),
        ],
        "attend_backward",
        grid=(steps,),
    )


def join_qkv_grads(table, query_grad, own_pairs, far_pairs, tables):
    tokens, columns = query_grad.shape
    rows = math.gcd(tokens, 512)

    def body(table_ref, q_ref, own_ref, *rest):
        far_refs, (cos_ref, low_ref, up_ref, out_ref, sum_ref) = rest[: len(far_pairs)], rest[len(far_pairs) :]

        @pl.when(pl.program_id(0) == 0)
        def _():
            sum_ref[...] = jnp.zeros_like(sum_ref)

        cosine, lower, upper = cos_ref[...], -low_ref[...], -up_ref[...]
        for tile in range(3 * columns // LANES):
            here = slice(tile * LANES, (tile + 1) * LANES)
            if tile < columns // LANES:
                value = q_ref[:, here]
            else:
                there = slice(tile * LANES - columns, (tile + 1) * LANES - columns)
                value = own_ref[:, there]
                for ref in far_refs:
                    value = value + ref[:, there].astype(F32)
            if tile < 2 * columns // LANES:
                value = rope(value, cosine, lower, upper)
            low = value.astype(BF16)
            out_ref[:, here] = low
            sum_ref[:, here] += jnp.sum(low.astype(F32), axis=0, keepdims=True)

    row = lambda i, s: (i, 0)
    spec = lambda array: pl.BlockSpec((rows, array.shape[1]), row)
    out = [
        jax.ShapeDtypeStruct((tokens, 3 * columns), BF16),
        jax.ShapeDtypeStruct((1, 3 * columns), F32),
    ]
    inputs = [query_grad, own_pairs, *far_pairs, *tables]
    return kernel_call(
        body,
        table,
        inputs,
        [spec(array) for array in inputs],
        out,
        [spec(out[0]), full(out[1])],
        [],
        "join_qkv_grads",
        grid=(tokens // rows,),
    )


def core_half(value, axis, which):
    size = value.shape[axis] // lax.axis_size("core")
    return lax.dynamic_slice_in_dim(value, which * size, size, axis)


def in_core_order(own, other, axis):
    core = lax.axis_index("core")
    return jnp.where(
        core == 0,
        jnp.concatenate([own, other], axis=axis),
        jnp.concatenate([other, own], axis=axis),
    )


class Gather:
    def __init__(self, order, block, first, second):
        self.order, self.first, self.second = order, first, second
        self.n1, self.n2 = lax.axis_size(first), lax.axis_size(second)
        self.found = {(0, 0): block}

    def near(self, depth=1):
        for i in range(1, self.n1):
            self.found[i, 0] = self.order.send(self.found[0, 0], self.first, i, depth)

    def side(self, depth=1):
        for j in range(1, self.n2):
            self.found[0, j] = self.order.send(self.found[0, 0], self.second, j, depth)

    def cross(self, depth=1):
        for i in range(1, self.n1):
            for j in range(1, self.n2):
                self.found[i, j] = self.order.send(self.found[i, 0], self.second, j, depth)

    def blocks(self):
        if self.first == "x":
            return [self.found[b, a] for a in range(self.n2) for b in range(self.n1)]
        return [self.found[a, b] for a in range(self.n1) for b in range(self.n2)]


class ScatterIn:
    def __init__(self, order, layout, table, features, right):
        self.order, self.layout, self.table = order, layout, table
        self.features, self.right = features, right

    parts = None

    def compute(self):
        layout, n_x = self.layout, self.layout.n_x
        which = [a * n_x + b for a in range(1, layout.n_y) for b in range(n_x)]
        (self.parts,) = self.order.run(
            lambda f, r: grad_in(layout, self.table, f, r, which), self.features, self.right
        )

    def begin(self, depth=1):
        if self.parts is None:
            self.compute()
        size = self.layout.n_x * self.layout.block
        self.received = [
            self.order.send(self.parts[(a - 1) * size : a * size], "dp", -a, depth)
            for a in range(1, self.layout.n_y)
        ]

    def middle(self):
        layout = self.layout
        self.first, self.others, away, others_away = self.order.run(
            lambda f, r, d: grad_in(layout, self.table, f, r, range(layout.n_x), d),
            self.features,
            self.right,
            self.received,
        )
        self.others_away = self.order.send(others_away, "core", 1, 1)
        self.away = self.order.send(away, "core", 1, 2)

    def finish(self, depth=1):
        place = self.layout.place
        near, cross = [], []
        for b in range(1, self.layout.n_x):
            here = slice((b - 1) * place, b * place)
            near.append(self.order.send(self.others[here], "x", -b, depth))
            cross.append(self.order.send(self.others_away[here], "x", -b, depth + 1))
        self.sums = ([self.first, *near], [self.away, *cross])


class ScatterOut:
    def __init__(self, order, layout, table, lefts, grad):
        self.order, self.layout, self.table = order, layout, table
        self.lefts, self.grad = lefts, grad
        self.received = [[] for _ in range(layout.n_y)]

    def compute(self):
        layout, n_x = self.layout, self.layout.n_x
        which = [a * n_x + b for a in range(layout.n_y) for b in range(1, n_x)]
        self.parts = self.order.run(
            lambda l, g: grad_out(layout, self.table, l, g, which), self.lefts, self.grad
        )

    def begin(self, a, depth=1):
        n_x = self.layout.n_x
        for b in range(1, n_x):
            part = self.parts[a * (n_x - 1) + b - 1]
            self.received[a].append(self.order.send(part, "x", -b, depth))

    def middle(self):
        layout = self.layout
        which = [a * layout.n_x for a in range(layout.n_y)]
        self.first, self.others, away, others_away = self.order.run(
            lambda l, g, d: grad_out(layout, self.table, l, g, which, d),
            self.lefts,
            self.grad,
            self.received,
        )
        self.others_away = self.order.send(others_away, "core", 1, 1)
        self.away = self.order.send(away, "core", 1, 2)

    def finish(self, depth=1):
        near, cross = [], []
        for a in range(1, self.layout.n_y):
            near.append(self.order.send(self.others[a - 1], "dp", -a, depth))
            cross.append(self.order.send(self.others_away[a - 1], "dp", -a, depth + 1))
        self.sums = ([self.first, *near], [self.away, *cross])


def per_device(
    layer_input,
    segment_ids,
    positions,
    norm_gain,
    norm_bias,
    qkv_weight,
    qkv_bias,
    dense_weight,
    dense_bias,
    up_weight,
    up_bias,
    down_weight,
    down_bias,
    output_cotangent,
):
    layer_count = qkv_weight.shape[0]
    last = layer_count - 1
    core, x = lax.axis_index("core"), lax.axis_index("x")
    z, n_z = lax.axis_index("col"), lax.axis_size("col")
    layout = Layout(*layer_input.shape)
    n_x = layout.n_x
    tokens, width = layout.tokens, layout.width
    columns = qkv_weight.shape[3] // layout.n_c
    hidden = up_weight.shape[2] // layout.n_c
    table = width_table(layout)
    query_begin = x * tokens
    begins = [
        jnp.stack([query_begin, (x - b + n_x) % n_x * tokens]).astype(jnp.int32) for b in range(n_x)
    ]
    order = Order()


    def pieces_of(layer, group):
        which = order.after([core])[0]
        pieces = []
        for half in (which, 1 - which):
            if group == "out":
                parts = [core_half(w[layer], 0, half) for w in (dense_weight, down_weight)]
                pieces.append(jnp.concatenate(parts, axis=0))
                continue
            parts = []
            if group in ("qkv", "in"):
                parts.append(core_half(qkv_weight[layer], 2, half).reshape(-1, 3 * columns))
            if group in ("up", "in"):
                parts.append(core_half(up_weight[layer], 1, half))
            pieces.append(parts[0] if len(parts) == 1 else jnp.concatenate(parts, axis=1))
        return (*pieces, 1 if group == "out" else 0)

    def make_ready(layer, groups):
        pieces = [pieces_of(layer, group) for group in groups]
        swapped = [swap_core(other) for _, other, _ in pieces]
        blocks = [
            jnp.concatenate([own, other], axis=axis)
            for (own, _, axis), other in zip(pieces, swapped)
        ]
        for group, block in zip(groups, order.wait(*blocks)):
            ways = ("dp", "x") if group == "out" else ("x", "dp")
            gathers[layer, group] = Gather(order, block, *ways)

    def blocks_of(layer, group):
        if (layer, group) not in gathers:
            group = "in"
        return gathers[layer, group].blocks()


    def gather_features(block):
        return lax.all_gather(order.after([block])[0], ("core", "col"), axis=0, tiled=False)

    def scatter_features(summed):
        return lax.psum_scatter(order.after([summed])[0], "col", scatter_dimension=1, tiled=True)

    def to_owner(lefts, weights, transposed, name):
        *away, own = order.run(
            lambda *a: project_back(layout, table, a[0], a[1], transposed, name), lefts, weights
        )
        received = [order.send(piece, "core", 1, 2) for piece in away]
        return order.run(lambda a, b: merge_cores(layout, table, a, b), own, received)

    def moments(value, axes):
        mean = jnp.sum(value, axis=axes) / width
        return mean, jnp.sum(value * value, axis=axes) / width

    def inverse_of(mean, square):
        return lax.rsqrt(square - mean * mean + EPSILON)

    def normalise(residual, layer):
        stats = jnp.stack([jnp.sum(residual, axis=1), jnp.sum(residual * residual, axis=1)])
        stats = sum_over(stats, "col") / width
        inverse = inverse_of(stats[0], stats[1])
        centred = (residual - stats[0][:, None]) * inverse[:, None]
        return (centred * norm_gain[layer] + norm_bias[layer]).astype(BF16), centred, inverse

    def qkv_shift(layer):
        return core_half(qkv_bias[layer], 1, core).reshape(1, -1)

    def up_shift(layer):
        return core_half(up_bias[layer], 0, core).reshape(1, -1)

    def send_pairs(k, pairs):
        k["pairs"] = [pairs] + [order.send(pairs, "x", b) for b in range(1, n_x)]

    def project_q(layer):
        k = kept[layer]
        k["q"], pairs = order.run(
            lambda f, w, b, t: project_qkv(layout, table, f, w, b, t),
            k["features"],
            blocks_of(layer, "qkv"),
            qkv_shift(layer),
            tables,
        )
        send_pairs(k, pairs)

    def own_attention(layer):
        k = kept[layer]
        k["found"] = order.run(attend, begins[0], k["q"], k["pairs"][0], starts)

    def far_attention(layer):
        k = kept[layer]
        for b in range(1, n_x):
            k["found"] = order.run(
                attend, begins[b], k["q"], k["pairs"][b], starts, k["found"][1:]
            )
        k["mixed_low"], k["mixed"], k["logs"] = k["found"]

    def far_gradients(layer):
        k = kept[layer]
        query_grad, k["away_pairs"] = [], []
        for b in range(1, n_x):
            found, pair_grad = order.run(
                lambda *a: attend_backward(*a[:7], False, *a[7:]),
                begins[b],
                k["q"],
                k["pairs"][b],
                starts,
                k["mixed"],
                k["logs"],
                k["mixed_grad"],
                *query_grad,
            )
            query_grad = [found]
            k["away_pairs"].append(order.send(pair_grad, "x", -b))
        k["query_grad"] = query_grad

    def own_gradients(layer):
        k = kept[layer]
        k["query_grad"], k["own_pairs"] = order.run(
            lambda *a: attend_backward(*a[:7], True, *a[7:]),
            begins[0],
            k["q"],
            k["pairs"][0],
            starts,
            k["mixed"],
            k["logs"],
            k["mixed_grad"],
            *k["query_grad"],
        )

    def join_gradients(layer):
        k = kept[layer]
        k["qkv_low"], k["qkv_sum"] = order.run(
            lambda *a: join_qkv_grads(table, *a),
            k["query_grad"],
            k["own_pairs"],
            k["away_pairs"],
            tables,
        )

    gathers = {}
    kept = [dict() for _ in range(layer_count)]
    outputs = [None] * layer_count

    def out_pairs(layer):
        return [(block,) for block in gathers[layer, "out"].blocks()]

    def in_pairs(layer):
        if (layer, "in") in gathers:
            return [(block,) for block in gathers[layer, "in"].blocks()]
        return list(zip(gathers[layer, "qkv"].blocks(), gathers[layer, "up"].blocks()))


    def arrived(*transfers):
        order.wait(*transfers)

    residual = layer_input.astype(F32)
    raw = gather_features(layer_input)
    make_ready(0, ["qkv"])
    qkv, up, out = [None] * 3
    gathers[0, "qkv"].near()
    gathers[0, "qkv"].side()
    grad_features = gather_features(output_cotangent)
    make_ready(0, ["up", "out"])
    qkv, up, out = (gathers[0, group] for group in ("qkv", "up", "out"))
    arrived(qkv.found[1, 0], qkv.found[0, 1])
    up.near()
    qkv.cross()
    query_segments = lax.dynamic_slice_in_dim(segment_ids, query_begin, tokens, 0)
    starts = jnp.sum(
        (segment_ids[:, None] < query_segments[None, :]).astype(jnp.int32), axis=0, keepdims=True
    )
    places = lax.dynamic_slice_in_dim(positions, query_begin, tokens, 0)
    tables = rope_tables(order.after([places])[0])
    starts, *tables = order.wait(starts, *tables)
    affine = order.after([jnp.stack([norm_gain[0], norm_bias[0]])])[0]
    spread = [affine] + [shift(affine, "col", k) for k in range(1, n_z)]
    spread = jnp.stack(spread)[(z - jnp.arange(n_z) + n_z) % n_z]
    (spread,) = order.wait(spread)
    arrived(up.found[1, 0], *qkv.blocks()[1:])
    out.near()
    out.side()
    (raw,) = order.wait(raw)
    blocks = raw.reshape(layout.n_c, n_z, layout.own_tokens, layout.part).astype(F32)
    mean, square = moments(blocks, (1, 3))
    inverse = inverse_of(mean, square)
    gain, bias = (spread[:, i][None, :, None, :] for i in range(2))
    normed = (blocks - mean[:, None, :, None]) * inverse[:, None, :, None] * gain + bias
    kept[0]["features"] = normed.astype(BF16).reshape(raw.shape)
    kept[0]["inverse"] = lax.dynamic_index_in_dim(inverse, core, 0, keepdims=False)
    own_mean = lax.dynamic_index_in_dim(mean, core, 0, keepdims=False)
    (kept[0]["features"],) = order.wait(kept[0]["features"])
    for layer in range(last):
        k = kept[layer]
        project_q(layer)
        if layer == 0:
            up.side(2)
        own_attention(layer)
        arrived(*k["pairs"][1:])
        if layer == 0:
            arrived(up.found[0, 1], out.found[1, 0], out.found[0, 1])
            out.cross()
            up.cross()
        far_attention(layer)
        make_ready(layer + 1, ["in", "out"])
        in_next, out_next = gathers[layer + 1, "in"], gathers[layer + 1, "out"]
        if layer == 0:
            arrived(grad_features, *up.blocks()[1:])
        out_next.near()
        k["active"], k["slope"] = order.run(
            lambda f, w, b: project_up(layout, table, f, w, b),
            k["features"],
            blocks_of(layer, "up"),
            up_shift(layer),
        )
        arrived(*blocks_of(layer, "out")[1:])
        summed = to_owner([k["mixed_low"], k["active"]], out_pairs(layer), False, "project_out")
        arrived(*[out_next.found[a, 0] for a in range(1, layout.n_y)])
        branch = scatter_features(summed)
        order.wait(summed)
        in_next.near()
        in_next.side()
        arrived(*[v for at, v in in_next.found.items() if at != (0, 0)])
        (branch,) = order.wait(branch)
        residual = residual + branch.astype(F32) + dense_bias[layer] + down_bias[layer]
        outputs[layer] = residual
        normed, kept[layer + 1]["centred"], kept[layer + 1]["inverse"] = normalise(residual, layer + 1)
        (normed,) = order.wait(normed)
        kept[layer + 1]["features"] = gather_features(normed)
        order.wait(normed)
        out_next.side(1)
        out_next.cross(2)
        in_next.cross()
        arrived(*in_next.blocks()[1:])
        order.wait(kept[layer + 1]["features"])


    k = kept[last]
    project_q(last)
    k["mixed_grad"], k["active_grad"] = order.run(
        lambda g, w: branch_grads(layout, table, g, w, columns),
        grad_features,
        blocks_of(last, "out"),
    )
    k["active"], k["up_low"] = order.run(
        lambda f, w, b, g: project_up(layout, table, f, w, b, g),
        k["features"],
        blocks_of(last, "up"),
        up_shift(last),
        k["active_grad"],
    )
    arrived(*k["pairs"][1:])
    gradient = output_cotangent.astype(F32)
    sums = [None] * layer_count
    held = {"up": None, "qkv": None, "out": None}
    shapes = {
        "up": (layer_count, layout.place, layout.n_c * hidden),
        "qkv": (layer_count, layout.place, 3, layout.n_c * columns),
        "out": [
            (layer_count, layout.n_c * columns, layout.place),
            (layer_count, layout.n_c * hidden, layout.place),
        ],
    }

    def place(layer, group, scatter):
        if group == "out":
            held[group] = order.run(
                lambda a, b, h: place_out(layout, table, layer, a, b, shapes[group], h),
                *scatter.sums,
                held[group],
            )
        else:
            held[group] = order.run(
                lambda a, b, h: place_in(
                    layout, table, layer, a, b, shapes[group], h, 3 if group == "qkv" else 1
                ),
                *scatter.sums,
                held[group],
            )

    def norm_backward(layer, normed_grad, gradient):
        k = kept[layer]
        normed_grad = normed_grad.astype(F32)
        scaled_grad = normed_grad * norm_gain[layer]
        means = jnp.stack(
            [jnp.sum(scaled_grad, axis=1), jnp.sum(scaled_grad * k["centred"], axis=1)]
        )
        means = sum_over(means, "col") / width
        new = gradient + k["inverse"][:, None] * (
            scaled_grad - means[0][:, None] - k["centred"] * means[1][:, None]
        )

        def to_both(value):
            return in_core_order(value, jnp.zeros_like(value), value.ndim - 1).reshape(-1)

        sums[layer] = jnp.concatenate(
            [
                jnp.sum(normed_grad * k["centred"], axis=0),
                jnp.sum(normed_grad, axis=0),
                to_both(k["qkv_sum"].reshape(3, columns)),
                jnp.sum(gradient, axis=0),
                to_both(jnp.sum(k["up_low"], axis=0, dtype=F32)),
            ]
        )
        return new

    kept[0]["centred"] = (layer_input.astype(F32) - own_mean[:, None]) * kept[0]["inverse"][:, None]

    for layer in reversed(range(layer_count)):
        k = kept[layer]
        if layer < last:
            (grad_features,) = order.wait(grad_features)
            if layer + 1 == last:
                branch = scatter_features(out_summed)
                outputs[last] = residual + branch.astype(F32) + dense_bias[last] + down_bias[last]
            k["mixed_grad"], k["up_low"] = order.run(
                lambda g, w, s: branch_grads(layout, table, g, w, columns, s),
                grad_features,
                blocks_of(layer, "out"),
                k["slope"],
            )
        up = ScatterIn(order, layout, table, k["features"], k["up_low"])
        out_lefts = lambda: [k["mixed_low"], k["active"]]
        if layer == last:
            up.begin()
            own_attention(last)
            far_attention(last)
            out = ScatterOut(order, layout, table, out_lefts(), grad_features)
        else:
            out = ScatterOut(order, layout, table, out_lefts(), grad_features)
            out.compute()
            out.begin(layout.n_y - 1)
            up.begin()
        far_gradients(layer)
        own_gradients(layer)
        if layer == last:
            out.compute()
            arrived(*up.received)
            up.middle()
        arrived(*k["away_pairs"])
        join_gradients(layer)
        qkv = ScatterIn(order, layout, table, k["features"], k["qkv_low"])
        if layer == last:
            summed = to_owner([k["qkv_low"], k["up_low"]], in_pairs(layer), True, "feature_grads")
            normed_grad = scatter_features(summed)
            order.wait(summed)
            for a in range(layout.n_y):
                out.begin(a, 1)
            qkv.begin()
            out_summed = to_owner([k["mixed_low"], k["active"]], out_pairs(layer), False, "project_out")
            arrived(*qkv.received)
            qkv.middle()
            (normed_grad,) = order.wait(normed_grad)
            gradient = norm_backward(layer, normed_grad, gradient)
            (low,) = order.wait(gradient.astype(BF16))
            arrived(*[v for row in out.received for v in row])
            grad_features = gather_features(low)
            order.wait(low)
            up.finish()
            qkv.finish(2)
            out.middle()
            out.finish()
            place(layer, "up", up)
            place(layer, "qkv", qkv)
            place(layer, "out", out)
        else:
            for a in range(layout.n_y - 1):
                out.begin(a, 2)
            qkv.compute()
            qkv.begin(2)
            summed = to_owner([k["qkv_low"], k["up_low"]], in_pairs(layer), True, "feature_grads")
            arrived(*up.received, *qkv.received, *[v for row in out.received for v in row])
            normed_grad = scatter_features(summed)
            order.wait(summed)
            up.middle()
            up.finish(2)
            out.middle()
            out.finish(2)
            qkv.middle()
            qkv.finish(2)
            (normed_grad,) = order.wait(normed_grad)
            gradient = norm_backward(layer, normed_grad, gradient)
            if layer == 0:
                small = jnp.stack(sums)
                for axis in ("core", "x", "dp"):
                    small = sum_over(small, axis)
            place(layer, "up", up)
            place(layer, "out", out)
            place(layer, "qkv", qkv)

    small, gradient, outputs = order.now((small, gradient, outputs))
    held = order.now(held)
    part, both = layout.part, layout.n_c * columns
    ends = [0]
    for size in (part, part, 3 * both, part, layout.n_c * hidden):
        ends.append(ends[-1] + size)
    gain_grad, shift_grad, qkv_grad, out_bias_grad, up_grad = [
        small[:, begin:end] for begin, end in zip(ends[:-1], ends[1:])
    ]
    return (
        jnp.stack(outputs),
        gradient,
        gain_grad,
        shift_grad,
        held["qkv"],
        qkv_grad.reshape(layer_count, 3, both),
        held["out"][0],
        out_bias_grad,
        held["up"],
        up_grad,
        held["out"][1],
        out_bias_grad,
    )


def solution(mesh):
    n_y, n_row, n_z = (mesh.shape[name] for name in ("dp", "row", "col"))
    split = Mesh(mesh.devices.reshape(n_y, n_row // 2, 2, n_z), ("dp", "x", "core", "col"))
    rows = ("dp", "x", "core")
    placed = (
        P(rows, "col"),
        P("dp"),
        P("dp"),
        P(None, "col"),
        P(None, "col"),
        P(None, rows, None, "col"),
        P(None, None, "col"),
        P(None, "col", rows),
        P(None, "col"),
        P(None, rows, "col"),
        P(None, "col"),
        P(None, "col", rows),
        P(None, "col"),
        P(rows, "col"),
    )
    return jax.shard_map(
        per_device,
        mesh=split,
        in_specs=placed,
        out_specs=(
            P(None, rows, "col"),
            P(rows, "col"),
            P(None, "col"),
            P(None, "col"),
            P(None, rows, None, "col"),
            P(None, None, "col"),
            P(None, "col", rows),
            P(None, "col"),
            P(None, rows, "col"),
            P(None, "col"),
            P(None, "col", rows),
            P(None, "col"),
        ),
        check_vma=False,
    )
```

```python
import math
from types import SimpleNamespace

import jax
import jax.numpy as jnp
from jax import lax
from jax.experimental import pallas as pl
from jax.experimental.pallas import tpu as pltpu
from jax.sharding import Mesh
from jax.sharding import PartitionSpec as P

HEAD_DIM = 64
ROT = 32
EPSILON = 1e-05
NEGATIVE = -1e30
LANES = 128
HEADS_TILE = LANES // HEAD_DIM
MEBI = 1024 * 1024
PIECES = 4
VMEM_MEBI = 40
MORE_MEBI = 40
F32 = jnp.float32
BF16 = jnp.bfloat16
ANY = pl.BlockSpec(memory_space=pl.ANY)
HBM = pl.BlockSpec(memory_space=pltpu.HBM)
Y, X, C, Z = "dp", "x", "core", "col"
QKV, UP, OUT, IN = range(4)
COST = pl.CostEstimate(flops=1, bytes_accessed=1, transcendentals=0)


def contract(left, right, left_dim, right_dim):
    return lax.dot_general(
        left, right, (((left_dim,), (right_dim,)), ((), ())), preferred_element_type=F32
    )


def shift(value, axis, step):
    size = lax.axis_size(axis)
    return lax.ppermute(value, axis, [(i, (i + step) % size) for i in range(size)])


class Order:
    def __init__(self):
        self.last = []
        self.links = {}
        self.newest = {}

    def now(self, values):
        def one(value):
            while id(value) in self.newest:
                value = self.newest[id(value)][1]
            return value

        return jax.tree.map(one, values)

    def after(self, values, *others):
        leaves, tree = jax.tree.flatten(self.now(values))
        held = self.now([other for other in (*self.last, *others) if other is not None])
        every = {id(value): value for value in (*leaves, *held)}
        if held:
            for old, new in zip(every.values(), lax.optimization_barrier(tuple(every.values()))):
                self.newest[id(old)] = (old, new)
        return self.now(jax.tree.unflatten(tree, leaves))

    def run(self, function, *values):
        out = function(*self.after(values))
        self.last = jax.tree.leaves(out)
        return out

    def send(self, value, axis, step, depth=2):
        queue = self.links.setdefault(axis, [])
        held = queue[-depth] if len(queue) >= depth else None
        out = shift(self.after([value], held)[0], axis, step)
        queue.append(out)
        return out

    def wait(self, *values):
        out = self.after(list(values))
        self.last = [*self.last, *out]
        return out


def sum_over(value, axis):
    size = lax.axis_size(axis)
    if size & (size - 1):
        return value + sum(shift(value, axis, k) for k in range(1, size))
    step = 1
    while step < size:
        value = value + lax.ppermute(value, axis, [(i, i ^ step) for i in range(size)])
        step *= 2
    return value


def width_table(layout):
    n_y, n_x, n_c = lax.axis_size(Y), lax.axis_size(X), lax.axis_size(C)
    y, x, c = lax.axis_index(Y), lax.axis_index(X), lax.axis_index(C)
    begins = jnp.stack(
        [
            ((((y - a + n_y) % n_y) * n_x + (x - b + n_x) % n_x) * n_c + (c - k + n_c) % n_c)
            * layout.place
            for a in range(n_y)
            for b in range(n_x)
            for k in range(n_c)
        ]
    )
    return jnp.concatenate(
        [begins // layout.part, begins % layout.part, c[None], begins]
    ).astype(jnp.int32)


class Layout:
    def __init__(self, own_tokens, part):
        self.n_y, self.n_x, self.n_c, self.n_z = (
            lax.axis_size(name) for name in (Y, X, C, Z)
        )
        self.own_tokens = own_tokens
        self.tokens = own_tokens * self.n_c
        self.part = part
        self.width = part * self.n_z
        self.places = self.n_y * self.n_x * self.n_c
        self.place = self.width // self.places
        self.block = self.place * self.n_c
        self.blocks = self.n_y * self.n_x

    def fetch(self, table, gathered, core, places, target, sems, first):
        copies = []
        for slot, at in enumerate(places):
            begin = pl.multiple_of(table[self.places + at], self.place)
            copies.append(
                pltpu.make_async_copy(
                    gathered.at[core * self.n_z + table[at], :, pl.ds(begin, self.place)],
                    target.at[:, slot * self.place : (slot + 1) * self.place],
                    sems.at[first + slot],
                )
            )
        return copies


def kernel_call(body, table, inputs, in_specs, out_shape, out_specs, scratch, name, grid=(1,), aliases=None, mebi=VMEM_MEBI):
    return pl.pallas_call(
        body,
        grid_spec=pltpu.PrefetchScalarGridSpec(
            num_scalar_prefetch=1,
            grid=grid,
            in_specs=in_specs,
            out_specs=out_specs,
            scratch_shapes=scratch,
        ),
        out_shape=out_shape,
        input_output_aliases=aliases or {},
        compiler_params=pltpu.CompilerParams(vmem_limit_bytes=mebi * MEBI),
        cost_estimate=COST,
        name=name,
    )(table, *inputs)


def full(array_or_shape):
    shape = getattr(array_or_shape, "shape", array_or_shape)
    return pl.BlockSpec(tuple(shape), lambda i, t: (0,) * len(shape))


def start_all(copies):
    for copy in copies:
        copy.start()


def wait_all(copies):
    for copy in copies:
        copy.wait()


def rope(value, cosine, lower, upper):
    half = ROT // 2
    return (
        value * cosine
        + pltpu.roll(value, LANES - half, 1) * lower
        + pltpu.roll(value, half, 1) * upper
    )


def rope_tables(place_values):
    half = ROT // 2
    freq_table = 1.0 / 10000.0 ** (jnp.arange(half, dtype=F32) * 2.0 / ROT)
    angles = place_values.astype(F32)[:, None] * freq_table
    cosine, sine = jnp.cos(angles), jnp.sin(angles)
    rest = jnp.ones((angles.shape[0], HEAD_DIM - ROT), F32)
    none = jnp.zeros_like(sine)
    pair = lambda *pieces: jnp.concatenate(pieces * HEADS_TILE, axis=1)
    return jnp.stack(
        [
            pair(cosine, cosine, rest),
            pair(-sine, none, 0.0 * rest),
            pair(none, sine, 0.0 * rest),
        ]
    )


class Stream:
    def __init__(self, layout, table, gathered, weights, features, buffers, sems, w_sems, window=None):
        self.layout, self.features, self.buffers = layout, features, buffers
        if window is not None:
            weights = [ref.at[:, window] for ref in weights]
        n_c = layout.n_c
        self.pieces = [
            [
                layout.fetch(
                    table,
                    gathered,
                    core,
                    range(b * n_c, (b + 1) * n_c),
                    features.at[core, b],
                    sems.at[core, b],
                    0,
                )
                for b in range(layout.blocks)
            ]
            for core in range(n_c)
        ]
        self.weights = [
            pltpu.make_async_copy(ref, buffer, w_sems.at[b])
            for b, (ref, buffer) in enumerate(zip(weights, buffers))
        ]
        for core in range(n_c):
            for b in range(layout.blocks):
                if core == 0:
                    self.weights[b].start()
                start_all(self.pieces[core][b])

    def run(self, total, parts, product, finish):
        last = self.layout.blocks - 1
        for core in range(self.layout.n_c):
            for b in range(last + 1):
                if core == 0:
                    self.weights[b].wait()
                wait_all(self.pieces[core][b])
                for part in parts:
                    term = product(self.features[core, b], self.buffers[b], part)
                    if 0 < b:
                        term = total[:, part] + term
                    if b < last:
                        total[:, part] = term
                    else:
                        finish(core, part, term)

    @staticmethod
    def scratch(layout, shape, outputs):
        n_c, count = layout.n_c, layout.blocks
        return [
            pltpu.VMEM((n_c, count, layout.own_tokens, layout.block), BF16),
            *[pltpu.VMEM(shape, BF16) for _ in range(count)],
            pltpu.SemaphoreType.DMA((n_c, count, n_c)),
            pltpu.SemaphoreType.DMA((count,)),
            pltpu.VMEM((layout.own_tokens, outputs), F32),
        ]


def chunks(size, step=256):
    step = math.gcd(size, step)
    return [slice(begin, begin + step) for begin in range(0, size, step)]


def project_qkv(layout, table, gathered, blocks, bias, tables):
    columns = bias.shape[1] // 3
    rows, count = layout.own_tokens, layout.blocks

    def body(table_ref, g_ref, *rest):
        w_refs, rest = rest[:count], rest[count:]
        bias_ref, tables_ref, q_ref, kv_ref, features = rest[:5]
        buffers, (sems, w_sems, total, turns, turn_sem) = rest[5 : 5 + count], rest[5 + count :]
        window = slice(0, 3 * columns)
        stream = Stream(layout, table_ref, g_ref, w_refs, features, buffers, sems, w_sems, window)
        turn = pltpu.make_async_copy(tables_ref, turns, turn_sem)
        turn.start()

        def finish(core, part, value):
            if core == 0 and part.start == 0:
                turn.wait()
            here = slice(core * rows, (core + 1) * rows)
            value = value + bias_ref[:, part]
            for lanes in chunks(columns, LANES):
                piece = value[:, lanes]
                if part.start < 2 * columns:
                    piece = rope(piece, *(turns[i, here, :] for i in range(3)))
                begin = part.start + lanes.start
                if part.start < columns:
                    q_ref[here, begin : begin + LANES] = piece.astype(BF16)
                else:
                    kv_ref[here, begin - columns : begin - columns + LANES] = piece.astype(BF16)

        stream.run(
            total,
            [slice(i * columns, (i + 1) * columns) for i in range(3)],
            lambda f, w, part: jnp.dot(f, w[:, part], preferred_element_type=F32),
            finish,
        )

    out = [
        jax.ShapeDtypeStruct((layout.tokens, columns), BF16),
        jax.ShapeDtypeStruct((layout.tokens, 2 * columns), BF16),
    ]
    return kernel_call(
        body,
        table,
        [gathered, *blocks, bias, tables],
        [HBM] * (1 + count) + [full(bias), HBM],
        out,
        [full(o) for o in out],
        Stream.scratch(layout, (layout.block, 3 * columns), 3 * columns)
        + [pltpu.VMEM(tables.shape, F32), pltpu.SemaphoreType.DMA],
        "project_qkv",
        mebi=MORE_MEBI,
    )


def gelu_and_slope(v):
    inner = math.sqrt(2 / math.pi) * v * (1.0 + 0.044715 * v * v)
    curve = jnp.tanh(inner)
    slope = 0.5 * (1.0 + curve) + 0.5 * v * (1.0 - curve * curve) * math.sqrt(2 / math.pi) * (
        1.0 + 3 * 0.044715 * v * v
    )
    return 0.5 * v * (1.0 + curve), slope


def project_up(layout, table, gathered, blocks, bias, active_grad=None):
    hidden = bias.shape[1]
    window = slice(blocks[0].shape[1] - hidden, blocks[0].shape[1])
    rows, count = layout.own_tokens, layout.blocks
    known = active_grad is not None

    def body(table_ref, g_ref, *rest):
        w_refs, rest = rest[:count], rest[count:]
        if known:
            grad_ref, rest = rest[0], rest[1:]
        bias_ref, act_ref, slope_ref, features = rest[:4]
        buffers, (sems, w_sems, total, act_buf, slope_buf, out_sems) = rest[4 : 4 + count], rest[4 + count :]
        stream = Stream(layout, table_ref, g_ref, w_refs, features, buffers, sems, w_sems, window)
        outs = []
        parts = chunks(hidden)

        def finish(core, part, value):
            here = slice(core * rows, (core + 1) * rows)
            active, slope = gelu_and_slope(value + bias_ref[:, part])
            act_buf[here, part] = active.astype(BF16)
            if known:
                slope = slope * grad_ref[here, part].astype(F32)
            slope_buf[here, part] = slope.astype(BF16)
            if part.stop == hidden:
                for i, (buffer, ref) in enumerate(((act_buf, act_ref), (slope_buf, slope_ref))):
                    outs.append(
                        pltpu.make_async_copy(buffer.at[here], ref.at[here], out_sems.at[core, i])
                    )
                    outs[-1].start()

        stream.run(
            total,
            parts,
            lambda f, w, part: jnp.dot(f, w[:, part], preferred_element_type=F32),
            finish,
        )
        wait_all(outs)

    out = [jax.ShapeDtypeStruct((layout.tokens, hidden), BF16)] * 2
    extra = [active_grad] if known else []
    return kernel_call(
        body,
        table,
        [gathered, *blocks, *extra, bias],
        [HBM] * (1 + count) + [full(e) for e in extra] + [full(bias)],
        out,
        [ANY, ANY],
        Stream.scratch(layout, (layout.block, hidden), hidden)
        + [pltpu.VMEM((layout.tokens, hidden), BF16)] * 2
        + [pltpu.SemaphoreType.DMA((layout.n_c, 2))],
        "project_up",
        mebi=MORE_MEBI,
    )


def branch_grads(layout, table, gathered, blocks, columns, slope=None):
    rows, count = layout.own_tokens, layout.blocks
    height = blocks[0].shape[0]
    hidden = height - columns
    known = slope is not None

    def body(table_ref, g_ref, *rest):
        w_refs, rest = rest[:count], rest[count:]
        if known:
            slope_ref, rest = rest[0], rest[1:]
        mixed_ref, hidden_ref, features = rest[:3]
        buffers, (sems, w_sems, total, mixed_buf, hidden_buf, out_sems) = (
            rest[3 : 3 + count],
            rest[3 + count :],
        )
        stream = Stream(layout, table_ref, g_ref, w_refs, features, buffers, sems, w_sems)
        outs = []

        def finish(core, part, value):
            here = slice(core * rows, (core + 1) * rows)
            if part.start < columns:
                mixed_buf[here, part] = value.astype(BF16)
            else:
                to = slice(part.start - columns, part.stop - columns)
                if known:
                    value = value * slope_ref[here, to].astype(F32)
                hidden_buf[here, to] = value.astype(BF16)
            if part.stop == height:
                for i, (buffer, ref) in enumerate(((mixed_buf, mixed_ref), (hidden_buf, hidden_ref))):
                    outs.append(
                        pltpu.make_async_copy(buffer.at[here], ref.at[here], out_sems.at[core, i])
                    )
                    outs[-1].start()

        stream.run(
            total,
            chunks(height, math.gcd(columns, 256)),
            lambda f, w, part: contract(f, w[part, :], 1, 1),
            finish,
        )
        wait_all(outs)

    out = [
        jax.ShapeDtypeStruct((layout.tokens, columns), BF16),
        jax.ShapeDtypeStruct((layout.tokens, hidden), BF16),
    ]
    extra = [slope] if known else []
    return kernel_call(
        body,
        table,
        [gathered, *blocks, *extra],
        [HBM] * (1 + count) + [full(e) for e in extra],
        out,
        [ANY, ANY],
        Stream.scratch(layout, blocks[0].shape, height)
        + [pltpu.VMEM(o.shape, BF16) for o in out]
        + [pltpu.SemaphoreType.DMA((layout.n_c, 2))],
        "branch_grads",
        mebi=MORE_MEBI,
    )


def project_back(layout, table, lefts, weights, transposed, name):
    rows, count = layout.own_tokens, len(weights)
    per_block = len(weights[0])
    sizes = [left.shape[1] for left in lefts]
    flat = [w for block in weights for w in block]
    n = len(lefts)
    step = rows // PIECES

    def body(table_ref, *rest):
        left_refs, rest = rest[:n], rest[n:]
        w_refs, rest = rest[: len(flat)], rest[len(flat) :]
        out_refs, rest = rest[: PIECES + 1], rest[PIECES + 1 :]
        left_bufs, rest = rest[:n], rest[n:]
        w_bufs, (out_buf, sems, w_sems, out_sems) = rest[: len(flat)], rest[len(flat) :]
        core = table_ref[2 * layout.places]
        copies = []
        for half, which in enumerate((lax.rem(core + 1, layout.n_c), core)):
            begin = pl.multiple_of(which * rows, rows)
            copies.append(
                [
                    pltpu.make_async_copy(
                        ref.at[pl.ds(begin, rows), :], buf.at[half], sems.at[half, i]
                    )
                    for i, (ref, buf) in enumerate(zip(left_refs, left_bufs))
                ]
            )
        w_copies = [
            pltpu.make_async_copy(ref, buf, w_sems.at[i])
            for i, (ref, buf) in enumerate(zip(w_refs, w_bufs))
        ]
        start_all(copies[0] + w_copies)
        start_all(copies[1])
        outs = []
        for half in range(2):
            wait_all(copies[half])
            for b in range(count):
                if half == 0:
                    wait_all(w_copies[b * per_block : (b + 1) * per_block])
                total = None
                at = 0
                for i, buf in enumerate(left_bufs):
                    if per_block == 1:
                        here = slice(at, at + sizes[i])
                        w = w_bufs[b][:, here] if transposed else w_bufs[b][here, :]
                        at += sizes[i]
                    else:
                        w = w_bufs[b * per_block + i][...]
                    term = contract(buf[half], w, 1, 1 if transposed else 0)
                    total = term if total is None else total + term
                out_buf[half, :, b * layout.block : (b + 1) * layout.block] = total.astype(BF16)
            pieces = [out_buf.at[0, i * step : (i + 1) * step] for i in range(PIECES)]
            pieces = pieces if half == 0 else [out_buf.at[1]]
            for piece in pieces:
                at = len(outs)
                outs.append(pltpu.make_async_copy(piece, out_refs[at], out_sems.at[at]))
                outs[-1].start()
        wait_all(outs)

    out = [jax.ShapeDtypeStruct((size, layout.width), BF16) for size in [step] * PIECES + [rows]]
    return kernel_call(
        body,
        table,
        [*lefts, *flat],
        [ANY] * n + [HBM] * len(flat),
        out,
        [ANY] * (PIECES + 1),
        [pltpu.VMEM((2, rows, size), BF16) for size in sizes]
        + [pltpu.VMEM(w.shape, BF16) for w in flat]
        + [
            pltpu.VMEM((2, rows, layout.width), BF16),
            pltpu.SemaphoreType.DMA((2, n)),
            pltpu.SemaphoreType.DMA((len(flat),)),
            pltpu.SemaphoreType.DMA((PIECES + 1,)),
        ],
        name,
        mebi=MORE_MEBI,
    )


def merge_cores(layout, table, own, received):
    rows = layout.own_tokens // PIECES
    place, places, n_c = layout.place, layout.places, layout.n_c

    def body(table_ref, own_ref, *refs):
        out_ref = refs[PIECES]

        def write(other_ref):
            for at in range(places):
                begin = pl.multiple_of(table_ref[2 * places + 1 + at], place)
                there = at // n_c * n_c + (n_c - at % n_c) % n_c if n_c != 2 else at ^ 1
                total = own_ref[:, at * place : (at + 1) * place].astype(F32)
                total = total + other_ref[:, there * place : (there + 1) * place].astype(F32)
                out_ref[:, pl.ds(begin, place)] = total.astype(BF16)

        for i in range(PIECES):
            pl.when(pl.program_id(0) == i)(lambda i=i: write(refs[i]))

    spec = pl.BlockSpec((rows, layout.width), lambda i, t: (i, 0))
    return kernel_call(
        body,
        table,
        [own, *received],
        [spec] + [full(piece) for piece in received],
        jax.ShapeDtypeStruct((layout.own_tokens, layout.width), BF16),
        spec,
        [],
        "merge_cores",
        grid=(PIECES,),
    )


def fetch_blocks(layout, table, gathered, which, features, sems):
    n_c, rows = layout.n_c, layout.own_tokens
    return [
        [
            layout.fetch(
                table,
                gathered,
                core,
                range(b * n_c, (b + 1) * n_c),
                features.at[i, pl.ds(core * rows, rows), :],
                sems.at[i, core],
                0,
            )
            for core in range(n_c)
        ]
        for i, b in enumerate(which)
    ]


def grad_in(layout, table, gathered, right, which, added=None):
    n = right.shape[1]
    count, place, n_c, block = len(which), layout.place, layout.n_c, layout.block
    final = added is not None
    extra = list(added or [])

    def body(table_ref, g_ref, right_ref, *rest):
        add_refs, rest = rest[: len(extra)], rest[len(extra) :]
        outs, rest = rest[: len(out)], rest[len(out) :]
        features, right_buf, sems, right_sem, rest = *rest[:4], rest[4:]
        pieces = fetch_blocks(layout, table_ref, g_ref, which, features, sems)
        right_copy = pltpu.make_async_copy(right_ref, right_buf, right_sem)
        right_copy.start()
        for group in pieces:
            for piece in group:
                start_all(piece)
        add_bufs, rest = rest[: len(extra)], rest[len(extra) :]
        if final:
            add_sems, rest = rest[0], rest[1:]
            add_copies = [
                pltpu.make_async_copy(ref, buf, add_sems.at[i])
                for i, (ref, buf) in enumerate(zip(add_refs, add_bufs))
            ]
            start_all(add_copies)
        right_copy.wait()
        if not final:
            out_buf, out_sems = rest
        copies = []
        for i in range(count):
            for piece in pieces[i]:
                wait_all(piece)
            if final and i == 0:
                wait_all(add_copies)
            for k in range(n_c):
                value = contract(features[i, :, k * place : (k + 1) * place], right_buf[...], 0, 0)
                begin = i * block + k * place
                if not final:
                    out_buf[begin : begin + place, :] = value.astype(BF16)
                    continue
                for buf in add_bufs:
                    value = value + buf[begin : begin + place, :].astype(F32)
                if i > 0:
                    outs[2][begin - block : begin - block + place, :] = value.astype(BF16)
                elif k > 0:
                    outs[1][(k - 1) * place : k * place, :] = value.astype(BF16)
                else:
                    outs[0][...] = value
            if not final:
                here = slice(i * block, (i + 1) * block)
                copies.append(pltpu.make_async_copy(out_buf.at[here], outs[0].at[here], out_sems.at[i]))
                copies[-1].start()
        wait_all(copies)

    if final:
        out = [
            jax.ShapeDtypeStruct((place, n), F32),
            jax.ShapeDtypeStruct((block - place, n), BF16),
            jax.ShapeDtypeStruct(((count - 1) * block, n), BF16),
        ]
        more = [pltpu.VMEM(e.shape, BF16) for e in extra]
        more.append(pltpu.SemaphoreType.DMA((len(extra),)))
    else:
        out = [jax.ShapeDtypeStruct((count * block, n), BF16)]
        more = [pltpu.VMEM(out[0].shape, BF16), pltpu.SemaphoreType.DMA((count,))]
    return kernel_call(
        body,
        table,
        [gathered, right, *extra],
        [HBM] + [ANY] * (1 + len(extra)),
        out,
        [full(o) for o in out] if final else [ANY],
        [
            pltpu.VMEM((count, layout.tokens, block), BF16),
            pltpu.VMEM(right.shape, BF16),
            pltpu.SemaphoreType.DMA((count, n_c, n_c)),
            pltpu.SemaphoreType.DMA,
        ]
        + more,
        "grad_in",
        mebi=MORE_MEBI,
    )


def grad_out(layout, table, lefts, gathered, which, added=None):
    sizes = [left.shape[1] for left in lefts]
    m, n = sum(sizes), len(lefts)
    count, place, n_c, block = len(which), layout.place, layout.n_c, layout.block
    final = added is not None
    extra = [e for block_added in added for e in block_added] if final else []
    per_block = len(extra) // count

    def body(table_ref, g_ref, *rest):
        left_refs, rest = rest[:n], rest[n:]
        add_refs, rest = rest[: len(extra)], rest[len(extra) :]
        outs, rest = rest[: len(out)], rest[len(out) :]
        features, sems, left_sems, rest = *rest[:3], rest[3:]
        left_bufs, rest = rest[:n], rest[n:]
        left_copies = [
            pltpu.make_async_copy(ref, buf, left_sems.at[i])
            for i, (ref, buf) in enumerate(zip(left_refs, left_bufs))
        ]
        pieces = fetch_blocks(layout, table_ref, g_ref, which, features, sems)
        start_all(left_copies[:1])
        for piece in pieces[0]:
            start_all(piece)
        start_all(left_copies[1:])
        for group in pieces[1:]:
            for piece in group:
                start_all(piece)
        add_bufs, rest = rest[: len(extra)], rest[len(extra) :]
        if final:
            add_sems, rest = rest[0], rest[1:]
            add_copies = [
                pltpu.make_async_copy(ref, buf, add_sems.at[i])
                for i, (ref, buf) in enumerate(zip(add_refs, add_bufs))
            ]
            start_all(add_copies)
        if not final:
            out_buf, out_sems = rest
        copies = []
        for i in range(count):
            for piece in pieces[i]:
                wait_all(piece)
            if final:
                wait_all(add_copies[i * per_block : (i + 1) * per_block])
            at = 0
            for j, (left_buf, size) in enumerate(zip(left_bufs, sizes)):
                if i == 0:
                    left_copies[j].wait()
                for part in chunks(size):
                    rows = slice(at + part.start, at + part.stop)
                    value = contract(left_buf[:, part], features[i], 0, 0)
                    if not final:
                        out_buf[i, rows, :] = value.astype(BF16)
                        continue
                    for buf in add_bufs[i * per_block : (i + 1) * per_block]:
                        value = value + buf[rows, :].astype(F32)
                    if i == 0:
                        outs[0][rows, :] = value[:, :place]
                        outs[1][rows, :] = value[:, place:].astype(BF16)
                    else:
                        outs[1 + i][rows, :] = value.astype(BF16)
                at += size
            if not final:
                copies.append(pltpu.make_async_copy(out_buf.at[i], outs[i], out_sems.at[i]))
                copies[-1].start()
        wait_all(copies)

    if final:
        out = [
            jax.ShapeDtypeStruct((m, place), F32),
            jax.ShapeDtypeStruct((m, block - place), BF16),
            *[jax.ShapeDtypeStruct((m, block), BF16)] * (count - 1),
        ]
        more = [pltpu.VMEM(e.shape, BF16) for e in extra]
        more.append(pltpu.SemaphoreType.DMA((len(extra),)))
    else:
        out = [jax.ShapeDtypeStruct((m, block), BF16)] * count
        more = [pltpu.VMEM((count, m, block), BF16), pltpu.SemaphoreType.DMA((count,))]
    return kernel_call(
        body,
        table,
        [gathered, *lefts, *extra],
        [HBM] + [ANY] * (n + len(extra)),
        out,
        [full(o) for o in out] if final else [ANY] * count,
        [
            pltpu.VMEM((count, layout.tokens, block), BF16),
            pltpu.SemaphoreType.DMA((count, n_c, n_c)),
            pltpu.SemaphoreType.DMA((n,)),
        ]
        + [pltpu.VMEM(left.shape, BF16) for left in lefts]
        + more,
        "grad_out",
        mebi=MORE_MEBI,
    )


def fold(table, away, near, rows):
    m, n = away.shape
    spec = pl.BlockSpec((m, n), lambda i, t: (1, 0) if rows else (0, 1))

    def body(table_ref, away_ref, *refs):
        near_refs, out_ref = refs[:-1], refs[-1]
        total = away_ref[...].astype(F32)
        for ref in near_refs:
            total = total + ref[...].astype(F32)
        out_ref[...] = total.astype(BF16)

    return kernel_call(
        body,
        table,
        [away, *near],
        [full(away)] + [spec] * len(near),
        jax.ShapeDtypeStruct((m, n), BF16),
        full(away),
        [],
        "fold",
    )


def place_in(layout, table, layer, owns, others, shape, held, parts):
    rows, n = owns[0].shape
    step = n // parts
    inputs = [*owns, *others]

    def body(table_ref, *refs):
        refs, out_ref = refs[: len(inputs)], refs[-1]

        def write(sources):
            value = sum(ref[...].astype(F32) for ref in sources)
            if parts == 1:
                out_ref[...] = value
            else:
                for i in range(parts):
                    out_ref[i] = value[:, i * step : (i + 1) * step]

        pl.when(pl.program_id(0) == 0)(lambda: write(refs[: len(owns)]))
        pl.when(pl.program_id(0) == 1)(lambda: write(refs[len(owns) :]))

    half = lambda i, t: lax.rem(t[2 * layout.places] + i, layout.n_c)
    if parts == 1:
        spec = pl.BlockSpec((None, rows, n), lambda i, t: (layer, 0, half(i, t)))
    else:
        spec = pl.BlockSpec((None, parts, rows, step), lambda i, t: (layer, 0, 0, half(i, t)))
    more = [] if held is None else [held]
    return kernel_call(
        body,
        table,
        inputs + more,
        [pl.BlockSpec((rows, n), lambda i, t: (0, 0)) for v in inputs] + [ANY] * len(more),
        jax.ShapeDtypeStruct(shape, F32),
        spec,
        [],
        "place_in",
        grid=(2,),
        aliases={1 + len(inputs): 0} if more else None,
    )


def place_out(layout, table, layer, owns, others, shapes, held):
    m, place = owns[0].shape
    inputs = [*owns, *others]
    sizes = [shape[1] // layout.n_c for shape in shapes]
    more = [] if held is None else list(held)

    def body(table_ref, *refs):
        refs, out_refs = refs[: len(inputs)], refs[len(inputs) + len(more) :]

        def write(sources):
            at = 0
            for ref, size in zip(out_refs, sizes):
                ref[...] = sum(source[at : at + size, :].astype(F32) for source in sources)
                at += size

        pl.when(pl.program_id(0) == 0)(lambda: write(refs[: len(owns)]))
        pl.when(pl.program_id(0) == 1)(lambda: write(refs[len(owns) :]))

    half = lambda i, t: lax.rem(t[2 * layout.places] + i, layout.n_c)
    return kernel_call(
        body,
        table,
        inputs + more,
        [pl.BlockSpec((m, place), lambda i, t: (0, 0)) for v in inputs] + [ANY] * len(more),
        [jax.ShapeDtypeStruct(shape, F32) for shape in shapes],
        [pl.BlockSpec((None, size, place), lambda i, t: (layer, half(i, t), 0)) for size in sizes],
        [],
        "place_out",
        grid=(2,),
        aliases={1 + len(inputs) + i: i for i in range(len(more))} or None,
    )


def head_part(value, head):
    lane = lax.broadcasted_iota(jnp.int32, value.shape, 1)
    keep = (lane >= head * HEAD_DIM) & (lane < (head + 1) * HEAD_DIM)
    return jnp.where(keep, value, jnp.zeros_like(value))


def mask_bias(query_begin, key_begin, starts, shape, key_axis):
    key_place = key_begin + lax.broadcasted_iota(jnp.int32, shape, key_axis)
    query_place = query_begin + lax.broadcasted_iota(jnp.int32, shape, 1 - key_axis)
    allowed = (key_place >= starts) & (key_place <= query_place)
    return jnp.where(allowed, 0.0, NEGATIVE).astype(F32)


def attend(begins, queries, key_values, starts, before=None):
    tokens, columns = queries.shape
    own = before is None
    block_q = math.gcd(tokens, 256 if own else 512)
    heads, pairs = columns // HEAD_DIM, columns // LANES
    keys = key_values.shape[0]
    steps = tokens // block_q
    tall = LANES + 16

    def body(begin_ref, q_ref, kv_ref, start_ref, *rest):
        if not own:
            (old_ref, old_log_ref), rest = rest[:2], rest[2:]
        low_ref, mixed_ref, log_ref, turned = rest
        step = pl.program_id(0)

        @pl.when(step == 0)
        def _():
            for pair in range(pairs):
                there = slice(columns + pair * LANES, columns + (pair + 1) * LANES)
                turned[pair * tall : pair * tall + LANES, :] = kv_ref[:, there].T
                turned[pair * tall + LANES : (pair + 1) * tall, :] = jnp.ones((16, keys), BF16)

        def work(count, at):
            bias = mask_bias(
                begin_ref[0] + at * block_q, begin_ref[1], start_ref[...], (count, block_q), 0
            )
            for pair in range(pairs):
                here = slice(pair * LANES, (pair + 1) * LANES)
                q = q_ref[:, here] * jnp.asarray(HEAD_DIM**-0.5, BF16)
                shares, terms = [], []
                for head in range(HEADS_TILE):
                    index = HEADS_TILE * pair + head
                    score = contract(kv_ref[:count, here], head_part(q, head), 1, 1) + bias
                    top = jnp.max(score, axis=0, keepdims=True)
                    weight = jnp.exp(score - top).astype(BF16)
                    found = jnp.dot(
                        turned[pair * tall : (pair + 1) * tall, :count],
                        weight,
                        preferred_element_type=F32,
                    )
                    value = found[head * HEAD_DIM : (head + 1) * HEAD_DIM]
                    total = found[LANES : LANES + 1]
                    joined = top + jnp.log(total)
                    if own:
                        value = value * (1.0 / total)
                    else:
                        old = old_log_ref[index : index + 1, :]
                        most = jnp.maximum(old, joined)
                        joined = most + jnp.log(jnp.exp(old - most) + jnp.exp(joined - most))
                        value = value * jnp.exp(top - joined)
                        shares.append(jnp.broadcast_to(jnp.exp(old - joined), value.shape))
                    log_ref[index : index + 1, :] = joined
                    terms.append(value)
                value = jnp.concatenate(terms, axis=0).T
                if not own:
                    value = value + old_ref[:, here] * jnp.concatenate(shares, axis=0).T
                mixed_ref[:, here] = value
                low_ref[:, here] = value.astype(BF16)

        if own:
            for at in range(steps):
                pl.when(step == at)(lambda at=at: work((at + 1) * block_q, at))
        else:
            work(keys, step)

    row = lambda i, s: (i, 0)
    lane = lambda i, s: (0, i)
    wide = pl.BlockSpec((block_q, columns), row)
    slim = pl.BlockSpec((heads, block_q), lane)
    extra = [] if own else list(before)
    return kernel_call(
        body,
        begins,
        [queries, key_values, starts, *extra],
        [wide, full(key_values), pl.BlockSpec((1, block_q), lane)] + ([] if own else [wide, slim]),
        [
            jax.ShapeDtypeStruct((tokens, columns), BF16),
            jax.ShapeDtypeStruct((tokens, columns), F32),
            jax.ShapeDtypeStruct((heads, tokens), F32),
        ],
        [wide, wide, slim],
        [pltpu.VMEM((pairs * tall, keys), BF16)],
        "attend_own" if own else "attend_far",
        grid=(steps,),
    )


def attend_backward(begins, queries, key_values, starts, mixed, logs, mixed_grad, own, before=None):
    tokens, columns = queries.shape
    block_q = math.gcd(tokens, 256)
    heads = columns // HEAD_DIM
    keys = key_values.shape[0]
    steps = tokens // block_q
    scale = HEAD_DIM**-0.5
    pairs = columns // LANES

    def body(begin_ref, q_ref, kv_ref, start_ref, mixed_ref, log_ref, grad_ref, *rest):
        if before is not None:
            before_ref, rest = rest[0], rest[1:]
        dq_ref, dkv_ref, turned, key_sum, value_sum = rest
        step = pl.program_id(0)

        @pl.when(step == 0)
        def _():
            key_sum[...] = jnp.zeros_like(key_sum)
            value_sum[...] = jnp.zeros_like(value_sum)
            for pair in range(pairs):
                here = slice(pair * LANES, (pair + 1) * LANES)
                turned[here, :] = kv_ref[:, here].T

        def work(count, at):
            bias = mask_bias(
                begin_ref[0] + at * block_q, begin_ref[1], start_ref[...], (count, block_q), 0
            )
            for pair in range(pairs):
                here = slice(pair * LANES, (pair + 1) * LANES)
                there = slice(columns + pair * LANES, columns + (pair + 1) * LANES)
                q, grad = q_ref[:, here], grad_ref[:, here]
                product = (mixed_ref[:, here] * grad.astype(F32)).T
                k, v = kv_ref[:count, here], kv_ref[:count, there]
                key_terms, value_terms, query_terms = [], [], []
                for head in range(HEADS_TILE):
                    q_head, grad_head = head_part(q, head), head_part(grad, head)
                    inner = slice(head * HEAD_DIM, (head + 1) * HEAD_DIM)
                    delta = jnp.sum(product[inner], axis=0, keepdims=True)
                    index = HEADS_TILE * pair + head
                    score = contract(k, q_head, 1, 1) * scale + bias
                    weight = jnp.exp(score - log_ref[index : index + 1, :])
                    weight_grad = contract(v, grad_head, 1, 1)
                    score_grad = (weight * (weight_grad - delta)).astype(BF16)
                    value_terms.append(
                        jnp.dot(weight.astype(BF16), grad_head, preferred_element_type=F32)
                    )
                    key_terms.append(jnp.dot(score_grad, q_head, preferred_element_type=F32))
                    begin = pair * LANES + head * HEAD_DIM
                    query_terms.append(
                        jnp.dot(
                            turned[begin : begin + HEAD_DIM, :count],
                            score_grad,
                            preferred_element_type=F32,
                        )
                    )
                value_sum[:count, here] += value_terms[0] + value_terms[1]
                key_sum[:count, here] += key_terms[0] + key_terms[1]
                found = jnp.concatenate(query_terms, axis=0).T * scale
                if before is not None:
                    found = found + before_ref[:, here]
                dq_ref[:, here] = found

        if own:
            for at in range(steps):
                pl.when(step == at)(lambda at=at: work((at + 1) * block_q, at))
        else:
            work(keys, step)

        @pl.when(step == steps - 1)
        def _():
            dkv_ref[:, :columns] = (key_sum[...] * scale).astype(dkv_ref.dtype)
            dkv_ref[:, columns:] = value_sum[...].astype(dkv_ref.dtype)

    row = lambda i, s: (i, 0)
    lane = lambda i, s: (0, i)
    wide = pl.BlockSpec((block_q, columns), row)
    extra = [] if before is None else [before]
    out = [
        jax.ShapeDtypeStruct((tokens, columns), F32),
        jax.ShapeDtypeStruct((keys, 2 * columns), F32 if own else BF16),
    ]
    return kernel_call(
        body,
        begins,
        [queries, key_values, starts, mixed, logs, mixed_grad, *extra],
        [
            wide,
            full(key_values),
            pl.BlockSpec((1, block_q), lane),
            wide,
            pl.BlockSpec((heads, block_q), lane),
            wide,
        ]
        + [wide] * len(extra),
        out,
        [wide, full(out[1])],
        [
            pltpu.VMEM((columns, keys), BF16),
            pltpu.VMEM((keys, columns), F32),
            pltpu.VMEM((keys, columns), F32),
        ],
        "attend_backward",
        grid=(steps,),
    )


def join_qkv_grads(table, query_grad, own_pairs, far_pairs, tables):
    tokens, columns = query_grad.shape
    rows = math.gcd(tokens, 512)

    def body(table_ref, q_ref, own_ref, *rest):
        far_refs, (turn_ref, out_ref, sum_ref) = rest[: len(far_pairs)], rest[len(far_pairs) :]

        @pl.when(pl.program_id(0) == 0)
        def _():
            sum_ref[...] = jnp.zeros_like(sum_ref)

        cosine, lower, upper = turn_ref[0], -turn_ref[1], -turn_ref[2]
        for tile in range(3 * columns // LANES):
            here = slice(tile * LANES, (tile + 1) * LANES)
            if tile < columns // LANES:
                value = q_ref[:, here]
            else:
                there = slice(tile * LANES - columns, (tile + 1) * LANES - columns)
                value = own_ref[:, there]
                for ref in far_refs:
                    value = value + ref[:, there].astype(F32)
            if tile < 2 * columns // LANES:
                value = rope(value, cosine, lower, upper)
            low = value.astype(BF16)
            out_ref[:, here] = low
            sum_ref[:, here] += jnp.sum(low.astype(F32), axis=0, keepdims=True)

    row = lambda i, s: (i, 0)
    spec = lambda array: pl.BlockSpec((rows, array.shape[1]), row)
    out = [
        jax.ShapeDtypeStruct((tokens, 3 * columns), BF16),
        jax.ShapeDtypeStruct((1, 3 * columns), F32),
    ]
    inputs = [query_grad, own_pairs, *far_pairs]
    return kernel_call(
        body,
        table,
        [*inputs, tables],
        [spec(array) for array in inputs]
        + [pl.BlockSpec((3, rows, LANES), lambda i, s: (0, i, 0))],
        out,
        [spec(out[0]), full(out[1])],
        [],
        "join_qkv_grads",
        grid=(tokens // rows,),
    )


def cut_weights(layout, table, sources):
    n = len(sources)
    pieces = [source.pieces for source in sources]

    def body(table_ref, *rest):
        refs, outs, sems = rest[:n], rest[n : 3 * n], rest[3 * n]
        core = table_ref[2 * layout.places]
        copies = []
        for i, source in enumerate(sources):
            for j in range(pieces[i]):
                for k, half in enumerate((core, 1 - core)):
                    copies.append(
                        pltpu.make_async_copy(
                            source.read(refs[i], half, j),
                            source.part(outs[2 * i + k], j),
                            sems.at[i, j, k],
                        )
                    )
        start_all(copies)
        wait_all(copies)

    return kernel_call(
        body,
        table,
        [source.array for source in sources],
        [HBM] * n,
        [jax.ShapeDtypeStruct(source.shape, BF16) for source in sources for _ in range(2)],
        [HBM] * (2 * n),
        [pltpu.SemaphoreType.DMA((n, max(pieces), 2))],
        "cut_weights",
    )


def join_weights(table, sources, shape, owns, received):
    n = len(sources)

    def body(table_ref, *rest):
        refs, out_ref = rest[: 2 * n], rest[2 * n]
        for i, source in enumerate(sources):
            out_ref[source.place()] = refs[i][...]
            out_ref[source.other()] = refs[n + i][...]

    out = jax.ShapeDtypeStruct(shape, BF16)
    arrays = [*owns, *received]
    return kernel_call(
        body, table, arrays, [full(a) for a in arrays], out, full(out), [], "join_weights"
    )


class RowSource:
    def __init__(self, array, layer, begin):
        self.array, self.layer, self.begin = array, layer, begin
        self.split = array.ndim == 4
        self.pieces = array.shape[1] if self.split else 1
        self.rows = array.shape[-2]
        self.size = array.shape[-1] // 2
        self.shape = (self.rows, self.pieces * self.size)

    def read(self, ref, core, piece):
        here = pl.ds(pl.multiple_of(core * self.size, self.size), self.size)
        return ref.at[self.layer, piece, :, here] if self.split else ref.at[self.layer, :, here]

    def place(self):
        return slice(0, self.rows), slice(self.begin, self.begin + self.shape[1])

    def other(self):
        return slice(self.rows, 2 * self.rows), slice(self.begin, self.begin + self.shape[1])

    def part(self, target, piece):
        return target.at[:, piece * self.size : (piece + 1) * self.size]


class ColumnSource:
    pieces = 1

    def __init__(self, array, layer, begin):
        self.array, self.layer, self.begin = array, layer, begin
        self.size, self.columns = array.shape[1] // 2, array.shape[2]
        self.shape = (self.size, self.columns)

    def read(self, ref, core, piece):
        return ref.at[self.layer, pl.ds(pl.multiple_of(core * self.size, self.size), self.size), :]

    def place(self):
        return slice(self.begin, self.begin + self.size), slice(0, self.columns)

    def other(self):
        return slice(self.begin, self.begin + self.size), slice(self.columns, 2 * self.columns)

    def part(self, target, piece):
        return target


def core_half(value, axis, which):
    size = value.shape[axis] // lax.axis_size(C)
    return lax.dynamic_slice_in_dim(value, which * size, size, axis)


def in_core_order(own, other, axis):
    return jnp.where(
        lax.axis_index(C) == 0,
        jnp.concatenate([own, other], axis=axis),
        jnp.concatenate([other, own], axis=axis),
    )


class Gather:
    def __init__(self, order, block, first, second):
        self.order, self.first, self.second = order, first, second
        self.n1, self.n2 = lax.axis_size(first), lax.axis_size(second)
        self.found = {(0, 0): block}

    def near(self, depth=1):
        for i in range(1, self.n1):
            self.found[i, 0] = self.order.send(self.found[0, 0], self.first, i, depth)
        return [self.found[i, 0] for i in range(1, self.n1)]

    def side(self, depth=1):
        for j in range(1, self.n2):
            self.found[0, j] = self.order.send(self.found[0, 0], self.second, j, depth)
        return [self.found[0, j] for j in range(1, self.n2)]

    def cross(self, depth=1):
        found = []
        for i in range(1, self.n1):
            for j in range(1, self.n2):
                self.found[i, j] = self.order.send(self.found[i, 0], self.second, j, depth)
                found.append(self.found[i, j])
        return found

    def blocks(self):
        if self.first == X:
            return [self.found[b, a] for a in range(self.n2) for b in range(self.n1)]
        return [self.found[a, b] for a in range(self.n1) for b in range(self.n2)]


class ScatterIn:
    def __init__(self, order, layout, table, features, right):
        self.order, self.layout, self.table = order, layout, table
        self.features, self.right = features, right

    def compute(self):
        layout, n_x = self.layout, self.layout.n_x
        which = [a * n_x + b for a in range(1, layout.n_y) for b in range(n_x)]
        (self.parts,) = self.order.run(
            lambda f, r: grad_in(layout, self.table, f, r, which), self.features, self.right
        )

    def begin(self, depth=1):
        size = self.layout.n_x * self.layout.block
        self.received = [
            self.order.send(self.parts[(a - 1) * size : a * size], Y, -a, depth)
            for a in range(1, self.layout.n_y)
        ]

    def middle(self):
        layout = self.layout
        self.first, self.away, self.others = self.order.run(
            lambda f, r, d: grad_in(layout, self.table, f, r, range(layout.n_x), d),
            self.features,
            self.right,
            self.received,
        )

    def finish(self, depth=2):
        block = self.layout.block
        self.near = [
            self.order.send(self.others[(b - 1) * block : b * block], X, -b, depth)
            for b in range(1, self.layout.n_x)
        ]

    def swap(self):
        away = self.order.run(
            lambda a, b: fold(self.table, a, b, True), self.away, self.near
        )
        self.sums = ([self.first, *self.near], [self.order.send(away, C, 1, 3)])


class ScatterOut:
    def __init__(self, order, layout, table, lefts, grad):
        self.order, self.layout, self.table = order, layout, table
        self.lefts, self.grad = lefts, grad
        self.received = [[] for _ in range(layout.n_y)]

    def compute(self):
        layout, n_x = self.layout, self.layout.n_x
        which = [a * n_x + b for a in range(layout.n_y) for b in range(1, n_x)]
        self.parts = self.order.run(
            lambda l, g: grad_out(layout, self.table, l, g, which), self.lefts, self.grad
        )

    def begin(self, a, depth=1):
        n_x = self.layout.n_x
        for b in range(1, n_x):
            part = self.parts[a * (n_x - 1) + b - 1]
            self.received[a].append(self.order.send(part, X, -b, depth))

    def all_received(self):
        return [value for row in self.received for value in row]

    def middle(self):
        layout = self.layout
        which = [a * layout.n_x for a in range(layout.n_y)]
        self.first, self.away, *self.others = self.order.run(
            lambda l, g, d: grad_out(layout, self.table, l, g, which, d),
            self.lefts,
            self.grad,
            self.received,
        )

    def finish(self, depth=2):
        self.near = [
            self.order.send(self.others[a - 1], Y, -a, depth) for a in range(1, self.layout.n_y)
        ]

    def swap(self):
        away = self.order.run(
            lambda a, b: fold(self.table, a, b, False), self.away, self.near
        )
        self.sums = ([self.first, *self.near], [self.order.send(away, C, 1, 3)])


def per_device(
    layer_input,
    segment_ids,
    positions,
    norm_gain,
    norm_bias,
    qkv_weight,
    qkv_bias,
    dense_weight,
    dense_bias,
    up_weight,
    up_bias,
    down_weight,
    down_bias,
    output_cotangent,
):
    layer_count = qkv_weight.shape[0]
    last = layer_count - 1
    core, x = lax.axis_index(C), lax.axis_index(X)
    z, n_z = lax.axis_index(Z), lax.axis_size(Z)
    layout = Layout(*layer_input.shape)
    n_x = layout.n_x
    tokens, width = layout.tokens, layout.width
    columns = qkv_weight.shape[3] // layout.n_c
    hidden = up_weight.shape[2] // layout.n_c
    table = width_table(layout)
    query_begin = x * tokens
    begins = [
        jnp.stack([query_begin, (x - b + n_x) % n_x * tokens]).astype(jnp.int32) for b in range(n_x)
    ]
    order = Order()
    gathers = {}
    kept = [SimpleNamespace(layer=layer) for layer in range(layer_count)]
    outputs = [None] * layer_count
    sums = [None] * layer_count

    def arrived(*transfers):
        order.wait(*transfers)


    def sources_of(layer, group):
        if group == OUT:
            shape = (columns + hidden, layout.block)
            return shape, [
                ColumnSource(dense_weight, layer, 0),
                ColumnSource(down_weight, layer, columns),
            ]
        sources = []
        if group != UP:
            sources.append(RowSource(qkv_weight.transpose(0, 2, 1, 3), layer, 0))
        if group != QKV:
            begin = 3 * columns if group == IN else 0
            sources.append(RowSource(up_weight, layer, begin))
        return (layout.block, sum(source.shape[1] for source in sources)), sources

    def make_ready(layer, groups):
        found = []
        for group in groups:
            shape, sources = sources_of(layer, group)

            def cut(arrays, sources=sources):
                for source, array in zip(sources, arrays):
                    source.array = array
                return cut_weights(layout, table, sources)

            parts = order.run(cut, [source.array for source in sources])
            found.append((sources, shape, parts[::2], parts[1::2]))
        swapped = [[shift(value, C, 1) for value in order.after(away)] for *_, away in found]
        for group, (sources, shape, owns, _), received in zip(groups, found, swapped):
            block = order.run(
                lambda o, r, s=sources, h=shape: join_weights(table, s, h, o, r), owns, received
            )
            ways = (Y, X) if group == OUT else (X, Y)
            gathers[layer, group] = Gather(order, block, *ways)

    def blocks_of(layer, group):
        if (layer, group) not in gathers:
            group = IN
        return gathers[layer, group].blocks()


    def gather_features(block):
        return lax.all_gather(order.after([block])[0], (C, Z), axis=0, tiled=False)

    def scatter_features(summed):
        return lax.psum_scatter(order.after([summed])[0], Z, scatter_dimension=1, tiled=True)

    def to_owner(lefts, weights, transposed, name, awaited=()):
        *away, own = order.run(
            lambda *a: project_back(layout, table, a[0], a[1], transposed, name), lefts, weights
        )
        received = [order.send(piece, C, 1, PIECES) for piece in away]
        if awaited:
            order.wait(*awaited)
        return order.run(lambda a, b: merge_cores(layout, table, a, b), own, received)

    def moments(value, axes):
        mean = jnp.sum(value, axis=axes) / width
        return mean, jnp.sum(value * value, axis=axes) / width

    def inverse_of(mean, square):
        return lax.rsqrt(square - mean * mean + EPSILON)

    def normalise(k, residual):
        stats = jnp.stack([jnp.sum(residual, axis=1), jnp.sum(residual * residual, axis=1)])
        stats = sum_over(stats, Z) / width
        k.inverse = inverse_of(stats[0], stats[1])
        k.centred = (residual - stats[0][:, None]) * k.inverse[:, None]
        normed = (k.centred * norm_gain[k.layer] + norm_bias[k.layer]).astype(BF16)
        (normed,) = order.wait(normed)
        k.features = gather_features(normed)
        order.wait(normed)

    def qkv_shift(layer):
        return core_half(qkv_bias[layer], 1, core).reshape(1, -1)

    def up_shift(layer):
        return core_half(up_bias[layer], 0, core).reshape(1, -1)

    def project_q(k):
        k.q, pairs = order.run(
            lambda f, w, b, t: project_qkv(layout, table, f, w, b, t),
            k.features,
            blocks_of(k.layer, QKV),
            qkv_shift(k.layer),
            tables,
        )
        k.pairs = [pairs] + [order.send(pairs, X, b) for b in range(1, n_x)]

    def project_hidden(k, *grad):
        k.active, k.slope = order.run(
            lambda f, w, b, *g: project_up(layout, table, f, w, b, *g),
            k.features,
            blocks_of(k.layer, UP),
            up_shift(k.layer),
            *grad,
        )

    def grads_of_branch(k, grad_features, *slope):
        k.mixed_grad, k.hidden_grad = order.run(
            lambda g, w, *s: branch_grads(layout, table, g, w, columns, *s),
            grad_features,
            blocks_of(k.layer, OUT),
            *slope,
        )

    def own_attention(k):
        k.found = order.run(attend, begins[0], k.q, k.pairs[0], starts)

    def far_attention(k):
        for b in range(1, n_x):
            k.found = order.run(attend, begins[b], k.q, k.pairs[b], starts, k.found[1:])
        k.mixed_low, k.mixed, k.logs = k.found

    def far_gradients(k):
        k.query_grad, k.away_pairs = [], []
        for b in range(1, n_x):
            found, pair_grad = order.run(
                lambda *a: attend_backward(*a[:7], False, *a[7:]),
                *(begins[b], k.q, k.pairs[b], starts, k.mixed, k.logs, k.mixed_grad),
                *k.query_grad,
            )
            k.query_grad = [found]
            k.away_pairs.append(order.send(pair_grad, X, -b))

    def own_gradients(k):
        k.query_grad, k.own_pairs = order.run(
            lambda *a: attend_backward(*a[:7], True, *a[7:]),
            *(begins[0], k.q, k.pairs[0], starts, k.mixed, k.logs, k.mixed_grad),
            *k.query_grad,
        )

    def join_gradients(k):
        k.qkv_low, k.qkv_sum = order.run(
            lambda *a: join_qkv_grads(table, *a), k.query_grad, k.own_pairs, k.away_pairs, tables
        )

    def branch_sum(k):
        lefts = [k.mixed_low, k.active]
        pairs = [(block,) for block in blocks_of(k.layer, OUT)]
        return to_owner(lefts, pairs, False, "project_out")

    def feature_sum(k, *awaited):
        if (k.layer, IN) in gathers:
            pairs = [(block,) for block in blocks_of(k.layer, IN)]
        else:
            pairs = list(zip(blocks_of(k.layer, QKV), blocks_of(k.layer, UP)))
        return to_owner([k.qkv_low, k.up_low], pairs, True, "feature_grads", awaited)

    def add_branch(residual, branch, layer):
        return residual + branch.astype(F32) + dense_bias[layer] + down_bias[layer]


    residual = layer_input.astype(F32)
    raw = gather_features(layer_input)
    make_ready(0, [QKV])
    qkv = gathers[0, QKV]
    first_near, first_side = qkv.near(), qkv.side()
    grad_features = gather_features(output_cotangent)
    make_ready(0, [UP, OUT])
    up, out = gathers[0, UP], gathers[0, OUT]
    arrived(*first_near, *first_side)
    up_near, qkv_cross = up.near(), qkv.cross()
    query_segments = lax.dynamic_slice_in_dim(segment_ids, query_begin, tokens, 0)
    starts = jnp.sum(
        (segment_ids[:, None] < query_segments[None, :]).astype(jnp.int32), axis=0, keepdims=True
    )
    places = lax.dynamic_slice_in_dim(positions, query_begin, tokens, 0)
    tables = rope_tables(order.after([places])[0])
    starts, tables = order.wait(starts, tables)
    affine = order.after([jnp.stack([norm_gain[0], norm_bias[0]])])[0]
    spread = [affine] + [shift(affine, Z, k) for k in range(1, n_z)]
    spread = jnp.stack(spread)[(z - jnp.arange(n_z) + n_z) % n_z]
    (spread,) = order.wait(spread)
    arrived(*up_near, *qkv_cross)
    out_near, out_side = out.near(), out.side()
    (raw,) = order.wait(raw)
    blocks = raw.reshape(layout.n_c, n_z, layout.own_tokens, layout.part).astype(F32)
    mean, square = moments(blocks, (1, 3))
    inverse = inverse_of(mean, square)
    gain, bias = (spread[:, i][None, :, None, :] for i in range(2))
    normed = (blocks - mean[:, None, :, None]) * inverse[:, None, :, None] * gain + bias
    kept[0].inverse = lax.dynamic_index_in_dim(inverse, core, 0, keepdims=False)
    own_mean = lax.dynamic_index_in_dim(mean, core, 0, keepdims=False)
    (kept[0].features,) = order.wait(normed.astype(BF16).reshape(raw.shape))
    for k in kept[:-1]:
        layer = k.layer
        project_q(k)
        if layer == 0:
            up_side = up.side(2)
        own_attention(k)
        arrived(*k.pairs[1:])
        if layer == 0:
            arrived(*up_side, *out_near, *out_side)
            out_cross, up_cross = out.cross(), up.cross()
        far_attention(k)
        make_ready(layer + 1, [IN, OUT])
        in_next, out_next = gathers[layer + 1, IN], gathers[layer + 1, OUT]
        if layer == 0:
            arrived(grad_features, *up_cross, *out_cross)
        next_near, next_side = out_next.near(), out_next.side()
        project_hidden(k)
        summed = branch_sum(k)
        arrived(*next_near, *next_side)
        branch = scatter_features(summed)
        order.wait(summed)
        arrived(*in_next.near(), *in_next.side())
        (branch,) = order.wait(branch)
        residual = outputs[layer] = add_branch(residual, branch, layer)
        k = kept[layer + 1]
        normalise(k, residual)
        next_cross, in_cross = out_next.cross(), in_next.cross()
        if k.layer == last:
            arrived(*next_cross)
            grads_of_branch(k, grad_features)
        arrived(*in_cross)
        order.wait(k.features)


    k = kept[last]
    project_q(k)
    project_hidden(k, k.hidden_grad)
    k.up_low = k.slope
    gradient = output_cotangent.astype(F32)
    held = {UP: None, QKV: None, OUT: None}
    shapes = {
        UP: (layer_count, layout.place, layout.n_c * hidden),
        QKV: (layer_count, 3, layout.place, layout.n_c * columns),
        OUT: [
            (layer_count, layout.n_c * columns, layout.place),
            (layer_count, layout.n_c * hidden, layout.place),
        ],
    }

    def place(layer, group, scatter):
        def write(owns, others, before):
            if group == OUT:
                return place_out(layout, table, layer, owns, others, shapes[group], before)
            parts = 3 if group == QKV else 1
            return place_in(layout, table, layer, owns, others, shapes[group], before, parts)

        held[group] = order.run(write, *scatter.sums, held[group])

    def norm_backward(k, normed_grad, gradient):
        normed_grad = normed_grad.astype(F32)
        scaled_grad = normed_grad * norm_gain[k.layer]
        means = jnp.stack([jnp.sum(scaled_grad, axis=1), jnp.sum(scaled_grad * k.centred, axis=1)])
        means = sum_over(means, Z) / width
        new = gradient + k.inverse[:, None] * (
            scaled_grad - means[0][:, None] - k.centred * means[1][:, None]
        )

        def to_both(value):
            return in_core_order(value, jnp.zeros_like(value), value.ndim - 1).reshape(-1)

        sums[k.layer] = jnp.concatenate(
            [
                jnp.sum(normed_grad * k.centred, axis=0),
                jnp.sum(normed_grad, axis=0),
                to_both(k.qkv_sum.reshape(3, columns)),
                jnp.sum(gradient, axis=0),
                to_both(jnp.sum(k.up_low, axis=0, dtype=F32)),
            ]
        )
        return new

    kept[0].centred = (layer_input.astype(F32) - own_mean[:, None]) * kept[0].inverse[:, None]
    before = None

    for k in reversed(kept):
        layer = k.layer
        scatter_in = lambda right: ScatterIn(order, layout, table, k.features, right)
        if layer == last:
            own_attention(k)
            arrived(*k.pairs[1:])
            up = scatter_in(k.up_low)
            up.compute()
            up.begin()
            far_attention(k)
        else:
            (grad_features,) = order.wait(grad_features)
            branch = None
            if layer + 1 == last:
                branch = scatter_features(out_summed)
            grads_of_branch(k, grad_features, k.slope)
            k.up_low = k.hidden_grad
            up = scatter_in(k.up_low)
        out = ScatterOut(order, layout, table, [k.mixed_low, k.active], grad_features)
        far_gradients(k)
        if layer < last:
            up.compute()
            up.begin()
        own_gradients(k)
        out.compute()
        if layer < last:
            arrived(*k.away_pairs)
            out.begin(layout.n_y - 1, 1)
        else:
            arrived(*k.away_pairs, *up.received)
        join_gradients(k)
        qkv = scatter_in(k.qkv_low)
        awaited = [] if layer == last else [*up.received, *out.received[-1]]
        summed = feature_sum(k, *awaited)
        normed_grad = scatter_features(summed)
        order.wait(summed)
        for a in reversed(range(layout.n_y - (layer < last))):
            out.begin(a, 1)
        qkv.compute()
        qkv.begin()
        up.middle()
        if layer == last:
            (normed_grad,) = order.wait(normed_grad)
            gradient = norm_backward(k, normed_grad, gradient)
            (low,) = order.wait(gradient.astype(BF16))
            arrived(*out.all_received(), *qkv.received)
            grad_features = gather_features(low)
            order.wait(low)
            up.finish(1)
            out.middle()
            out.finish(1)
            qkv.middle()
            qkv.finish(1)
            out_summed = branch_sum(k)
            arrived(*up.near, *qkv.near, *out.near)
        else:
            for scatter in before:
                scatter.swap()
            for group, scatter in zip((UP, QKV, OUT), before):
                place(layer + 1, group, scatter)
            if branch is not None:
                outputs[last] = add_branch(residual, branch, last)
                (outputs[last],) = order.wait(outputs[last])
            arrived(*out.all_received())
            up.finish(1)
            out.middle()
            out.finish(1)
            (normed_grad,) = order.wait(normed_grad)
            gradient = norm_backward(k, normed_grad, gradient)
            (gradient,) = order.wait(gradient)
            arrived(*qkv.received)
            qkv.middle()
            qkv.finish(1)
        before = (up, qkv, out)

    up, qkv, out = before
    small = sum_over(jnp.stack(order.after(sums)), C)
    up.swap()
    place(0, UP, up)
    (small,) = order.wait(small)
    small = sum_over(small, X)
    out.swap()
    place(0, OUT, out)
    (small,) = order.wait(small)
    small = sum_over(small, Y)
    qkv.swap()
    place(0, QKV, qkv)

    small, gradient, outputs = order.now((small, gradient, outputs))
    held = order.now(held)
    part, both = layout.part, layout.n_c * columns
    ends = [0]
    for size in (part, part, 3 * both, part, layout.n_c * hidden):
        ends.append(ends[-1] + size)
    gain_grad, shift_grad, qkv_grad, out_bias_grad, up_grad = [
        small[:, begin:end] for begin, end in zip(ends[:-1], ends[1:])
    ]
    return (
        jnp.stack(outputs),
        gradient,
        gain_grad,
        shift_grad,
        held[QKV].transpose(0, 2, 1, 3),
        qkv_grad.reshape(layer_count, 3, both),
        held[OUT][0],
        out_bias_grad,
        held[UP],
        up_grad,
        held[OUT][1],
        out_bias_grad,
    )


def solution(mesh):
    n_y, n_row, n_z = (mesh.shape[name] for name in mesh.axis_names)
    split = Mesh(mesh.devices.reshape(n_y, n_row // 2, 2, n_z), (Y, X, C, Z))
    rows = (Y, X, C)
    placed = (
        P(rows, Z),
        P(Y),
        P(Y),
        P(None, Z),
        P(None, Z),
        P(None, rows, None, Z),
        P(None, None, Z),
        P(None, Z, rows),
        P(None, Z),
        P(None, rows, Z),
        P(None, Z),
        P(None, Z, rows),
        P(None, Z),
        P(rows, Z),
    )
    return jax.shard_map(
        per_device,
        mesh=split,
        in_specs=placed,
        out_specs=(
            P(None, rows, Z),
            P(rows, Z),
            P(None, Z),
            P(None, Z),
            P(None, rows, None, Z),
            P(None, None, Z),
            P(None, Z, rows),
            P(None, Z),
            P(None, rows, Z),
            P(None, Z),
            P(None, Z, rows),
            P(None, Z),
        ),
        check_vma=False,
    )
```

```python
import math
from types import SimpleNamespace

import jax
import jax.numpy as jnp
from jax import lax
from jax.experimental import pallas as pl
from jax.experimental.pallas import tpu as pltpu
from jax.sharding import Mesh
from jax.sharding import PartitionSpec as P

HEAD_DIM = 64
ROT = 32
EPSILON = 1e-05
NEGATIVE = -1e30
LANES = 128
HEADS_TILE = LANES // HEAD_DIM
MEBI = 1024 * 1024
PIECES = 2
VMEM_MEBI = 40
MORE_MEBI = 40
F32 = jnp.float32
BF16 = jnp.bfloat16
ANY = pl.BlockSpec(memory_space=pl.ANY)
HBM = pl.BlockSpec(memory_space=pltpu.HBM)
Y, X, C, Z = "dp", "x", "core", "col"
QKV, UP, OUT, IN = range(4)
COST = pl.CostEstimate(flops=1, bytes_accessed=1, transcendentals=0)


def contract(left, right, left_dim, right_dim):
    return lax.dot_general(
        left, right, (((left_dim,), (right_dim,)), ((), ())), preferred_element_type=F32
    )


def shift(value, axis, step):
    size = lax.axis_size(axis)
    return lax.ppermute(value, axis, [(i, (i + step) % size) for i in range(size)])


class Order:
    def __init__(self):
        self.last = []
        self.links = {}
        self.newest = {}

    def now(self, values):
        def one(value):
            while id(value) in self.newest:
                value = self.newest[id(value)][1]
            return value

        return jax.tree.map(one, values)

    def after(self, values, *others):
        leaves, tree = jax.tree.flatten(self.now(values))
        held = self.now([other for other in (*self.last, *others) if other is not None])
        every = {id(value): value for value in (*leaves, *held)}
        if held:
            for old, new in zip(every.values(), lax.optimization_barrier(tuple(every.values()))):
                self.newest[id(old)] = (old, new)
        return self.now(jax.tree.unflatten(tree, leaves))

    def run(self, function, *values):
        out = function(*self.after(values))
        self.last = jax.tree.leaves(out)
        return out

    def send(self, value, axis, step, depth=2):
        queue = self.links.setdefault(axis, [])
        held = queue[-depth] if len(queue) >= depth else None
        out = shift(self.after([value], held)[0], axis, step)
        queue.append(out)
        return out

    def wait(self, *values):
        out = self.after(list(values))
        self.last = [*self.last, *out]
        return out


def sum_over(value, axis):
    return value + sum(shift(value, axis, k) for k in range(1, lax.axis_size(axis)))


def width_table(layout):
    n_y, n_x, n_c = lax.axis_size(Y), lax.axis_size(X), lax.axis_size(C)
    y, x, c = lax.axis_index(Y), lax.axis_index(X), lax.axis_index(C)
    begins = jnp.stack(
        [
            ((((y - a + n_y) % n_y) * n_x + (x - b + n_x) % n_x) * n_c + (c - k + n_c) % n_c)
            * layout.place
            for a in range(n_y)
            for b in range(n_x)
            for k in range(n_c)
        ]
    )
    return jnp.concatenate(
        [begins // layout.part, begins % layout.part, c[None], begins]
    ).astype(jnp.int32)


class Layout:
    def __init__(self, own_tokens, part):
        self.n_y, self.n_x, self.n_c, self.n_z = (
            lax.axis_size(name) for name in (Y, X, C, Z)
        )
        self.own_tokens = own_tokens
        self.tokens = own_tokens * self.n_c
        self.part = part
        self.width = part * self.n_z
        self.places = self.n_y * self.n_x * self.n_c
        self.place = self.width // self.places
        self.block = self.place * self.n_c
        self.blocks = self.n_y * self.n_x

    def fetch(self, table, gathered, core, places, target, sems, first):
        copies = []
        for slot, at in enumerate(places):
            begin = pl.multiple_of(table[self.places + at], self.place)
            copies.append(
                pltpu.make_async_copy(
                    gathered.at[core * self.n_z + table[at], :, pl.ds(begin, self.place)],
                    target.at[:, slot * self.place : (slot + 1) * self.place],
                    sems.at[first + slot],
                )
            )
        return copies


def kernel_call(body, table, inputs, in_specs, out_shape, out_specs, scratch, name, grid=(1,), aliases=None, mebi=VMEM_MEBI):
    return pl.pallas_call(
        body,
        grid_spec=pltpu.PrefetchScalarGridSpec(
            num_scalar_prefetch=1,
            grid=grid,
            in_specs=in_specs,
            out_specs=out_specs,
            scratch_shapes=scratch,
        ),
        out_shape=out_shape,
        input_output_aliases=aliases or {},
        compiler_params=pltpu.CompilerParams(vmem_limit_bytes=mebi * MEBI),
        cost_estimate=COST,
        name=name,
    )(table, *inputs)


def full(array_or_shape):
    shape = getattr(array_or_shape, "shape", array_or_shape)
    return pl.BlockSpec(tuple(shape), lambda i, t: (0,) * len(shape))


def start_all(copies):
    for copy in copies:
        copy.start()


def wait_all(copies):
    for copy in copies:
        copy.wait()


def rope(value, cosine, lower, upper):
    half = ROT // 2
    return (
        value * cosine
        + pltpu.roll(value, LANES - half, 1) * lower
        + pltpu.roll(value, half, 1) * upper
    )


def rope_tables(place_values):
    half = ROT // 2
    freq_table = 1.0 / 10000.0 ** (jnp.arange(half, dtype=F32) * 2.0 / ROT)
    angles = place_values.astype(F32)[:, None] * freq_table
    cosine, sine = jnp.cos(angles), jnp.sin(angles)
    rest = jnp.ones((angles.shape[0], HEAD_DIM - ROT), F32)
    none = jnp.zeros_like(sine)
    pair = lambda *pieces: jnp.concatenate(pieces * HEADS_TILE, axis=1)
    return jnp.stack(
        [
            pair(cosine, cosine, rest),
            pair(-sine, none, 0.0 * rest),
            pair(none, sine, 0.0 * rest),
        ]
    )


class Stream:
    def __init__(self, layout, table, gathered, weights, features, buffers, sems, w_sems, window=None):
        self.layout, self.features, self.buffers = layout, features, buffers
        if window is not None:
            weights = [ref.at[:, window] for ref in weights]
        n_c = layout.n_c
        self.pieces = [
            [
                layout.fetch(
                    table,
                    gathered,
                    core,
                    range(b * n_c, (b + 1) * n_c),
                    features.at[core, b],
                    sems.at[core, b],
                    0,
                )
                for b in range(layout.blocks)
            ]
            for core in range(n_c)
        ]
        self.weights = [
            pltpu.make_async_copy(ref, buffer, w_sems.at[b])
            for b, (ref, buffer) in enumerate(zip(weights, buffers))
        ]
        for core in range(n_c):
            for b in range(layout.blocks):
                if core == 0:
                    self.weights[b].start()
                start_all(self.pieces[core][b])

    def run(self, total, parts, product, finish):
        last = self.layout.blocks - 1
        for core in range(self.layout.n_c):
            for b in range(last + 1):
                if core == 0:
                    self.weights[b].wait()
                wait_all(self.pieces[core][b])
                for part in parts:
                    term = product(self.features[core, b], self.buffers[b], part)
                    if 0 < b:
                        term = total[:, part] + term
                    if b < last:
                        total[:, part] = term
                    else:
                        finish(core, part, term)

    @staticmethod
    def scratch(layout, shape, outputs):
        n_c, count = layout.n_c, layout.blocks
        return [
            pltpu.VMEM((n_c, count, layout.own_tokens, layout.block), BF16),
            *[pltpu.VMEM(shape, BF16) for _ in range(count)],
            pltpu.SemaphoreType.DMA((n_c, count, n_c)),
            pltpu.SemaphoreType.DMA((count,)),
            pltpu.VMEM((layout.own_tokens, outputs), F32),
        ]


def chunks(size, step=256):
    step = math.gcd(size, step)
    return [slice(begin, begin + step) for begin in range(0, size, step)]


def project_qkv(layout, table, gathered, blocks, bias, tables):
    columns = bias.shape[1] // 3
    rows, count = layout.own_tokens, layout.blocks

    def body(table_ref, g_ref, *rest):
        w_refs, rest = rest[:count], rest[count:]
        bias_ref, tables_ref, q_ref, kv_ref, features = rest[:5]
        buffers, (sems, w_sems, total, turns, turn_sem) = rest[5 : 5 + count], rest[5 + count :]
        window = slice(0, 3 * columns)
        stream = Stream(layout, table_ref, g_ref, w_refs, features, buffers, sems, w_sems, window)
        turn = pltpu.make_async_copy(tables_ref, turns, turn_sem)
        turn.start()

        def finish(core, part, value):
            if core == 0 and part.start == 0:
                turn.wait()
            here = slice(core * rows, (core + 1) * rows)
            value = value + bias_ref[:, part]
            for lanes in chunks(columns, LANES):
                piece = value[:, lanes]
                if part.start < 2 * columns:
                    piece = rope(piece, *(turns[i, here, :] for i in range(3)))
                begin = part.start + lanes.start
                if part.start < columns:
                    q_ref[here, begin : begin + LANES] = piece.astype(BF16)
                else:
                    kv_ref[here, begin - columns : begin - columns + LANES] = piece.astype(BF16)

        stream.run(
            total,
            [slice(i * columns, (i + 1) * columns) for i in range(3)],
            lambda f, w, part: jnp.dot(f, w[:, part], preferred_element_type=F32),
            finish,
        )

    out = [
        jax.ShapeDtypeStruct((layout.tokens, columns), BF16),
        jax.ShapeDtypeStruct((layout.tokens, 2 * columns), BF16),
    ]
    return kernel_call(
        body,
        table,
        [gathered, *blocks, bias, tables],
        [HBM] * (1 + count) + [full(bias), HBM],
        out,
        [full(o) for o in out],
        Stream.scratch(layout, (layout.block, 3 * columns), 3 * columns)
        + [pltpu.VMEM(tables.shape, F32), pltpu.SemaphoreType.DMA],
        "project_qkv",
        mebi=MORE_MEBI,
    )


def gelu_and_slope(v):
    inner = math.sqrt(2 / math.pi) * v * (1.0 + 0.044715 * v * v)
    curve = jnp.tanh(inner)
    slope = 0.5 * (1.0 + curve) + 0.5 * v * (1.0 - curve * curve) * math.sqrt(2 / math.pi) * (
        1.0 + 3 * 0.044715 * v * v
    )
    return 0.5 * v * (1.0 + curve), slope


def project_up(layout, table, gathered, blocks, bias, active_grad=None):
    hidden = bias.shape[1]
    window = slice(blocks[0].shape[1] - hidden, blocks[0].shape[1])
    rows, count = layout.own_tokens, layout.blocks
    known = active_grad is not None

    def body(table_ref, g_ref, *rest):
        w_refs, rest = rest[:count], rest[count:]
        if known:
            grad_ref, rest = rest[0], rest[1:]
        bias_ref, act_ref, slope_ref, features = rest[:4]
        buffers, (sems, w_sems, total, act_buf, slope_buf, out_sems) = rest[4 : 4 + count], rest[4 + count :]
        stream = Stream(layout, table_ref, g_ref, w_refs, features, buffers, sems, w_sems, window)
        outs = []
        parts = chunks(hidden)

        def finish(core, part, value):
            here = slice(core * rows, (core + 1) * rows)
            active, slope = gelu_and_slope(value + bias_ref[:, part])
            act_buf[here, part] = active.astype(BF16)
            if known:
                slope = slope * grad_ref[here, part].astype(F32)
            slope_buf[here, part] = slope.astype(BF16)
            if part.stop == hidden:
                for i, (buffer, ref) in enumerate(((act_buf, act_ref), (slope_buf, slope_ref))):
                    outs.append(
                        pltpu.make_async_copy(buffer.at[here], ref.at[here], out_sems.at[core, i])
                    )
                    outs[-1].start()

        stream.run(
            total,
            parts,
            lambda f, w, part: jnp.dot(f, w[:, part], preferred_element_type=F32),
            finish,
        )
        wait_all(outs)

    out = [jax.ShapeDtypeStruct((layout.tokens, hidden), BF16)] * 2
    extra = [active_grad] if known else []
    return kernel_call(
        body,
        table,
        [gathered, *blocks, *extra, bias],
        [HBM] * (1 + count) + [full(e) for e in extra] + [full(bias)],
        out,
        [ANY, ANY],
        Stream.scratch(layout, (layout.block, hidden), hidden)
        + [pltpu.VMEM((layout.tokens, hidden), BF16)] * 2
        + [pltpu.SemaphoreType.DMA((layout.n_c, 2))],
        "project_up",
        mebi=MORE_MEBI,
    )


def branch_grads(layout, table, gathered, blocks, columns, slope=None):
    rows, count = layout.own_tokens, layout.blocks
    height = blocks[0].shape[0]
    hidden = height - columns
    known = slope is not None

    def body(table_ref, g_ref, *rest):
        w_refs, rest = rest[:count], rest[count:]
        if known:
            slope_ref, rest = rest[0], rest[1:]
        mixed_ref, hidden_ref, features = rest[:3]
        buffers, (sems, w_sems, total, mixed_buf, hidden_buf, out_sems) = (
            rest[3 : 3 + count],
            rest[3 + count :],
        )
        stream = Stream(layout, table_ref, g_ref, w_refs, features, buffers, sems, w_sems)
        outs = []

        def finish(core, part, value):
            here = slice(core * rows, (core + 1) * rows)
            if part.start < columns:
                mixed_buf[here, part] = value.astype(BF16)
            else:
                to = slice(part.start - columns, part.stop - columns)
                if known:
                    value = value * slope_ref[here, to].astype(F32)
                hidden_buf[here, to] = value.astype(BF16)
            if part.stop == height:
                for i, (buffer, ref) in enumerate(((mixed_buf, mixed_ref), (hidden_buf, hidden_ref))):
                    outs.append(
                        pltpu.make_async_copy(buffer.at[here], ref.at[here], out_sems.at[core, i])
                    )
                    outs[-1].start()

        stream.run(
            total,
            chunks(height, math.gcd(columns, 256)),
            lambda f, w, part: contract(f, w[part, :], 1, 1),
            finish,
        )
        wait_all(outs)

    out = [
        jax.ShapeDtypeStruct((layout.tokens, columns), BF16),
        jax.ShapeDtypeStruct((layout.tokens, hidden), BF16),
    ]
    extra = [slope] if known else []
    return kernel_call(
        body,
        table,
        [gathered, *blocks, *extra],
        [HBM] * (1 + count) + [full(e) for e in extra],
        out,
        [ANY, ANY],
        Stream.scratch(layout, blocks[0].shape, height)
        + [pltpu.VMEM(o.shape, BF16) for o in out]
        + [pltpu.SemaphoreType.DMA((layout.n_c, 2))],
        "branch_grads",
        mebi=MORE_MEBI,
    )


def project_back(layout, table, lefts, weights, transposed, away, name):
    rows, count = layout.own_tokens, len(weights)
    per_block = len(weights[0])
    sizes = [left.shape[1] for left in lefts]
    flat = [w for block in weights for w in block]
    n = len(lefts)
    pieces = PIECES if away else 1
    step = rows // pieces

    def body(table_ref, *rest):
        left_refs, rest = rest[:n], rest[n:]
        w_refs, rest = rest[: len(flat)], rest[len(flat) :]
        out_refs, rest = rest[:pieces], rest[pieces:]
        left_bufs, rest = rest[:n], rest[n:]
        w_bufs, (sems, w_sems) = rest[: len(flat)], rest[len(flat) :]
        core = table_ref[2 * layout.places]
        begin = pl.multiple_of((lax.rem(core + 1, layout.n_c) if away else core) * rows, rows)
        copies = [
            pltpu.make_async_copy(ref.at[pl.ds(begin, rows), :], buf, sems.at[i])
            for i, (ref, buf) in enumerate(zip(left_refs, left_bufs))
        ]
        w_copies = [
            pltpu.make_async_copy(ref, buf, w_sems.at[i])
            for i, (ref, buf) in enumerate(zip(w_refs, w_bufs))
        ]
        start_all(copies + w_copies)
        wait_all(copies)
        for b in range(count):
            wait_all(w_copies[b * per_block : (b + 1) * per_block])
            total = None
            at = 0
            for i, buf in enumerate(left_bufs):
                if per_block == 1:
                    here = slice(at, at + sizes[i])
                    w = w_bufs[b][:, here] if transposed else w_bufs[b][here, :]
                    at += sizes[i]
                else:
                    w = w_bufs[b * per_block + i][...]
                term = contract(buf[...], w, 1, 1 if transposed else 0)
                total = term if total is None else total + term
            for i in range(pieces):
                out_refs[i][:, b * layout.block : (b + 1) * layout.block] = total[
                    i * step : (i + 1) * step
                ].astype(BF16)

    out = [jax.ShapeDtypeStruct((step, layout.width), BF16)] * pieces
    return kernel_call(
        body,
        table,
        [*lefts, *flat],
        [ANY] * n + [HBM] * len(flat),
        out,
        [full(o) for o in out],
        [pltpu.VMEM((rows, size), BF16) for size in sizes]
        + [pltpu.VMEM(w.shape, BF16) for w in flat]
        + [
            pltpu.SemaphoreType.DMA((n,)),
            pltpu.SemaphoreType.DMA((len(flat),)),
        ],
        name,
        mebi=MORE_MEBI,
    )


def merge_cores(layout, table, own, received):
    rows = layout.own_tokens // PIECES
    place, places, n_c = layout.place, layout.places, layout.n_c

    def body(table_ref, own_ref, *refs):
        out_ref = refs[PIECES]

        def write(other_ref):
            for at in range(places):
                begin = pl.multiple_of(table_ref[2 * places + 1 + at], place)
                there = at // n_c * n_c + (n_c - at % n_c) % n_c if n_c != 2 else at ^ 1
                total = own_ref[:, at * place : (at + 1) * place].astype(F32)
                total = total + other_ref[:, there * place : (there + 1) * place].astype(F32)
                out_ref[:, pl.ds(begin, place)] = total.astype(BF16)

        for i in range(PIECES):
            pl.when(pl.program_id(0) == i)(lambda i=i: write(refs[i]))

    spec = pl.BlockSpec((rows, layout.width), lambda i, t: (i, 0))
    return kernel_call(
        body,
        table,
        [own, *received],
        [spec] + [full(piece) for piece in received],
        jax.ShapeDtypeStruct((layout.own_tokens, layout.width), BF16),
        spec,
        [],
        "merge_cores",
        grid=(PIECES,),
    )


def fetch_blocks(layout, table, gathered, which, features, sems):
    n_c, rows = layout.n_c, layout.own_tokens
    return [
        [
            layout.fetch(
                table,
                gathered,
                core,
                range(b * n_c, (b + 1) * n_c),
                features.at[i, pl.ds(core * rows, rows), :],
                sems.at[i, core],
                0,
            )
            for core in range(n_c)
        ]
        for i, b in enumerate(which)
    ]


def grad_in(layout, table, gathered, right, which, added=None):
    n = right.shape[1]
    count, place, n_c, block = len(which), layout.place, layout.n_c, layout.block
    final = added is not None
    extra = list(added or [])

    def body(table_ref, g_ref, right_ref, *rest):
        add_refs, rest = rest[: len(extra)], rest[len(extra) :]
        outs, rest = rest[: len(out)], rest[len(out) :]
        features, right_buf, sems, right_sem, rest = *rest[:4], rest[4:]
        pieces = fetch_blocks(layout, table_ref, g_ref, which, features, sems)
        right_copy = pltpu.make_async_copy(right_ref, right_buf, right_sem)
        right_copy.start()
        for group in pieces:
            for piece in group:
                start_all(piece)
        add_bufs, rest = rest[: len(extra)], rest[len(extra) :]
        if final:
            add_sems, rest = rest[0], rest[1:]
            add_copies = [
                pltpu.make_async_copy(ref, buf, add_sems.at[i])
                for i, (ref, buf) in enumerate(zip(add_refs, add_bufs))
            ]
            start_all(add_copies)
        right_copy.wait()
        if not final:
            out_buf, out_sems = rest
        copies = []
        for i in range(count):
            for piece in pieces[i]:
                wait_all(piece)
            if final and i == 0:
                wait_all(add_copies)
            for k in range(n_c):
                value = contract(features[i, :, k * place : (k + 1) * place], right_buf[...], 0, 0)
                begin = i * block + k * place
                if not final:
                    out_buf[begin : begin + place, :] = value.astype(BF16)
                    continue
                for buf in add_bufs:
                    value = value + buf[begin : begin + place, :].astype(F32)
                if i > 0:
                    outs[2][begin - block : begin - block + place, :] = value.astype(BF16)
                elif k > 0:
                    outs[1][(k - 1) * place : k * place, :] = value.astype(BF16)
                else:
                    outs[0][...] = value
            if not final:
                here = slice(i * block, (i + 1) * block)
                copies.append(pltpu.make_async_copy(out_buf.at[here], outs[0].at[here], out_sems.at[i]))
                copies[-1].start()
        wait_all(copies)

    if final:
        out = [
            jax.ShapeDtypeStruct((place, n), F32),
            jax.ShapeDtypeStruct((block - place, n), BF16),
            jax.ShapeDtypeStruct(((count - 1) * block, n), BF16),
        ]
        more = [pltpu.VMEM(e.shape, BF16) for e in extra]
        more.append(pltpu.SemaphoreType.DMA((len(extra),)))
    else:
        out = [jax.ShapeDtypeStruct((count * block, n), BF16)]
        more = [pltpu.VMEM(out[0].shape, BF16), pltpu.SemaphoreType.DMA((count,))]
    return kernel_call(
        body,
        table,
        [gathered, right, *extra],
        [HBM] + [ANY] * (1 + len(extra)),
        out,
        [full(o) for o in out] if final else [ANY],
        [
            pltpu.VMEM((count, layout.tokens, block), BF16),
            pltpu.VMEM(right.shape, BF16),
            pltpu.SemaphoreType.DMA((count, n_c, n_c)),
            pltpu.SemaphoreType.DMA,
        ]
        + more,
        "grad_in",
        mebi=MORE_MEBI,
    )


def grad_out(layout, table, lefts, gathered, which, added=None):
    sizes = [left.shape[1] for left in lefts]
    m, n = sum(sizes), len(lefts)
    count, place, n_c, block = len(which), layout.place, layout.n_c, layout.block
    final = added is not None
    extra = [e for block_added in added for e in block_added] if final else []
    per_block = len(extra) // count

    def body(table_ref, g_ref, *rest):
        left_refs, rest = rest[:n], rest[n:]
        add_refs, rest = rest[: len(extra)], rest[len(extra) :]
        outs, rest = rest[: len(out)], rest[len(out) :]
        features, sems, left_sems, rest = *rest[:3], rest[3:]
        left_bufs, rest = rest[:n], rest[n:]
        left_copies = [
            pltpu.make_async_copy(ref, buf, left_sems.at[i])
            for i, (ref, buf) in enumerate(zip(left_refs, left_bufs))
        ]
        pieces = fetch_blocks(layout, table_ref, g_ref, which, features, sems)
        start_all(left_copies[:1])
        for piece in pieces[0]:
            start_all(piece)
        start_all(left_copies[1:])
        for group in pieces[1:]:
            for piece in group:
                start_all(piece)
        add_bufs, rest = rest[: len(extra)], rest[len(extra) :]
        if final:
            add_sems, rest = rest[0], rest[1:]
            add_copies = [
                pltpu.make_async_copy(ref, buf, add_sems.at[i])
                for i, (ref, buf) in enumerate(zip(add_refs, add_bufs))
            ]
            start_all(add_copies)
        if not final:
            out_buf, out_sems = rest
        copies = []
        for i in range(count):
            for piece in pieces[i]:
                wait_all(piece)
            if final:
                wait_all(add_copies[i * per_block : (i + 1) * per_block])
            at = 0
            for j, (left_buf, size) in enumerate(zip(left_bufs, sizes)):
                if i == 0:
                    left_copies[j].wait()
                for part in chunks(size):
                    rows = slice(at + part.start, at + part.stop)
                    value = contract(left_buf[:, part], features[i], 0, 0)
                    if not final:
                        out_buf[i, rows, :] = value.astype(BF16)
                        continue
                    for buf in add_bufs[i * per_block : (i + 1) * per_block]:
                        value = value + buf[rows, :].astype(F32)
                    if i == 0:
                        outs[0][rows, :] = value[:, :place]
                        outs[1][rows, :] = value[:, place:].astype(BF16)
                    else:
                        outs[1 + i][rows, :] = value.astype(BF16)
                at += size
            if not final:
                copies.append(pltpu.make_async_copy(out_buf.at[i], outs[i], out_sems.at[i]))
                copies[-1].start()
        wait_all(copies)

    if final:
        out = [
            jax.ShapeDtypeStruct((m, place), F32),
            jax.ShapeDtypeStruct((m, block - place), BF16),
            *[jax.ShapeDtypeStruct((m, block), BF16)] * (count - 1),
        ]
        more = [pltpu.VMEM(e.shape, BF16) for e in extra]
        more.append(pltpu.SemaphoreType.DMA((len(extra),)))
    else:
        out = [jax.ShapeDtypeStruct((m, block), BF16)] * count
        more = [pltpu.VMEM((count, m, block), BF16), pltpu.SemaphoreType.DMA((count,))]
    return kernel_call(
        body,
        table,
        [gathered, *lefts, *extra],
        [HBM] + [ANY] * (n + len(extra)),
        out,
        [full(o) for o in out] if final else [ANY] * count,
        [
            pltpu.VMEM((count, layout.tokens, block), BF16),
            pltpu.SemaphoreType.DMA((count, n_c, n_c)),
            pltpu.SemaphoreType.DMA((n,)),
        ]
        + [pltpu.VMEM(left.shape, BF16) for left in lefts]
        + more,
        "grad_out",
        mebi=MORE_MEBI,
    )


def fold(table, away, near, rows):
    m, n = away.shape
    spec = pl.BlockSpec((m, n), lambda i, t: (1, 0) if rows else (0, 1))

    def body(table_ref, away_ref, *refs):
        near_refs, out_ref = refs[:-1], refs[-1]
        total = away_ref[...].astype(F32)
        for ref in near_refs:
            total = total + ref[...].astype(F32)
        out_ref[...] = total.astype(BF16)

    return kernel_call(
        body,
        table,
        [away, *near],
        [full(away)] + [spec] * len(near),
        jax.ShapeDtypeStruct((m, n), BF16),
        full(away),
        [],
        "fold",
    )


def place_in(layout, table, layer, owns, others, shape, held, parts):
    rows, n = owns[0].shape
    step = n // parts
    inputs = [*owns, *others]

    def body(table_ref, *refs):
        refs, out_ref = refs[: len(inputs)], refs[-1]

        def write(sources):
            value = sum(ref[...].astype(F32) for ref in sources)
            if parts == 1:
                out_ref[...] = value
            else:
                for i in range(parts):
                    out_ref[i] = value[:, i * step : (i + 1) * step]

        pl.when(pl.program_id(0) == 0)(lambda: write(refs[: len(owns)]))
        pl.when(pl.program_id(0) == 1)(lambda: write(refs[len(owns) :]))

    half = lambda i, t: lax.rem(t[2 * layout.places] + i, layout.n_c)
    if parts == 1:
        spec = pl.BlockSpec((None, rows, n), lambda i, t: (layer, 0, half(i, t)))
    else:
        spec = pl.BlockSpec((None, parts, rows, step), lambda i, t: (layer, 0, 0, half(i, t)))
    more = [] if held is None else [held]
    return kernel_call(
        body,
        table,
        inputs + more,
        [pl.BlockSpec((rows, n), lambda i, t: (0, 0)) for v in inputs] + [ANY] * len(more),
        jax.ShapeDtypeStruct(shape, F32),
        spec,
        [],
        "place_in",
        grid=(2,),
        aliases={1 + len(inputs): 0} if more else None,
    )


def place_out(layout, table, layer, owns, others, shapes, held):
    m, place = owns[0].shape
    inputs = [*owns, *others]
    sizes = [shape[1] // layout.n_c for shape in shapes]
    more = [] if held is None else list(held)

    def body(table_ref, *refs):
        refs, out_refs = refs[: len(inputs)], refs[len(inputs) + len(more) :]

        def write(sources):
            at = 0
            for ref, size in zip(out_refs, sizes):
                ref[...] = sum(source[at : at + size, :].astype(F32) for source in sources)
                at += size

        pl.when(pl.program_id(0) == 0)(lambda: write(refs[: len(owns)]))
        pl.when(pl.program_id(0) == 1)(lambda: write(refs[len(owns) :]))

    half = lambda i, t: lax.rem(t[2 * layout.places] + i, layout.n_c)
    return kernel_call(
        body,
        table,
        inputs + more,
        [pl.BlockSpec((m, place), lambda i, t: (0, 0)) for v in inputs] + [ANY] * len(more),
        [jax.ShapeDtypeStruct(shape, F32) for shape in shapes],
        [pl.BlockSpec((None, size, place), lambda i, t: (layer, half(i, t), 0)) for size in sizes],
        [],
        "place_out",
        grid=(2,),
        aliases={1 + len(inputs) + i: i for i in range(len(more))} or None,
    )


def head_part(value, head):
    lane = lax.broadcasted_iota(jnp.int32, value.shape, 1)
    keep = (lane >= head * HEAD_DIM) & (lane < (head + 1) * HEAD_DIM)
    return jnp.where(keep, value, jnp.zeros_like(value))


def mask_bias(query_begin, key_begin, starts, shape, key_axis):
    key_place = key_begin + lax.broadcasted_iota(jnp.int32, shape, key_axis)
    query_place = query_begin + lax.broadcasted_iota(jnp.int32, shape, 1 - key_axis)
    allowed = (key_place >= starts) & (key_place <= query_place)
    return jnp.where(allowed, 0.0, NEGATIVE).astype(F32)


def attend(begins, queries, key_values, starts, before=None):
    tokens, columns = queries.shape
    own = before is None
    block_q = math.gcd(tokens, 512)
    heads, pairs = columns // HEAD_DIM, columns // LANES
    keys = key_values.shape[0]
    steps = tokens // block_q
    tall = LANES + 16

    def body(begin_ref, q_ref, kv_ref, start_ref, *rest):
        if not own:
            (old_ref, old_log_ref), rest = rest[:2], rest[2:]
        low_ref, mixed_ref, log_ref, turned = rest
        step = pl.program_id(0)

        @pl.when(step == 0)
        def _():
            for pair in range(pairs):
                there = slice(columns + pair * LANES, columns + (pair + 1) * LANES)
                turned[pair * tall : pair * tall + LANES, :] = kv_ref[:, there].T
                turned[pair * tall + LANES : (pair + 1) * tall, :] = jnp.ones((16, keys), BF16)

        def work(count, at):
            bias = mask_bias(
                begin_ref[0] + at * block_q, begin_ref[1], start_ref[...], (count, block_q), 0
            )
            for pair in range(pairs):
                here = slice(pair * LANES, (pair + 1) * LANES)
                q = q_ref[:, here] * jnp.asarray(HEAD_DIM**-0.5, BF16)
                shares, terms = [], []
                for head in range(HEADS_TILE):
                    index = HEADS_TILE * pair + head
                    score = contract(kv_ref[:count, here], head_part(q, head), 1, 1) + bias
                    top = jnp.max(score, axis=0, keepdims=True)
                    weight = jnp.exp(score - top).astype(BF16)
                    found = jnp.dot(
                        turned[pair * tall : (pair + 1) * tall, :count],
                        weight,
                        preferred_element_type=F32,
                    )
                    value = found[head * HEAD_DIM : (head + 1) * HEAD_DIM]
                    total = found[LANES : LANES + 1]
                    joined = top + jnp.log(total)
                    if own:
                        value = value * (1.0 / total)
                    else:
                        old = old_log_ref[index : index + 1, :]
                        most = jnp.maximum(old, joined)
                        joined = most + jnp.log(jnp.exp(old - most) + jnp.exp(joined - most))
                        value = value * jnp.exp(top - joined)
                        shares.append(jnp.broadcast_to(jnp.exp(old - joined), value.shape))
                    log_ref[index : index + 1, :] = joined
                    terms.append(value)
                value = jnp.concatenate(terms, axis=0).T
                if not own:
                    value = value + old_ref[:, here] * jnp.concatenate(shares, axis=0).T
                mixed_ref[:, here] = value
                low_ref[:, here] = value.astype(BF16)

        if own:
            for at in range(steps):
                pl.when(step == at)(lambda at=at: work((at + 1) * block_q, at))
        else:
            work(keys, step)

    row = lambda i, s: (i, 0)
    lane = lambda i, s: (0, i)
    wide = pl.BlockSpec((block_q, columns), row)
    slim = pl.BlockSpec((heads, block_q), lane)
    extra = [] if own else list(before)
    return kernel_call(
        body,
        begins,
        [queries, key_values, starts, *extra],
        [wide, full(key_values), pl.BlockSpec((1, block_q), lane)] + ([] if own else [wide, slim]),
        [
            jax.ShapeDtypeStruct((tokens, columns), BF16),
            jax.ShapeDtypeStruct((tokens, columns), F32),
            jax.ShapeDtypeStruct((heads, tokens), F32),
        ],
        [wide, wide, slim],
        [pltpu.VMEM((pairs * tall, keys), BF16)],
        "attend_own" if own else "attend_far",
        grid=(steps,),
    )


def attend_backward(begins, queries, key_values, starts, mixed, logs, mixed_grad, own, before=None):
    tokens, columns = queries.shape
    block_q = math.gcd(tokens, 256)
    heads = columns // HEAD_DIM
    keys = key_values.shape[0]
    steps = tokens // block_q
    scale = HEAD_DIM**-0.5
    pairs = columns // LANES

    def body(begin_ref, q_ref, kv_ref, start_ref, mixed_ref, log_ref, grad_ref, *rest):
        if before is not None:
            before_ref, rest = rest[0], rest[1:]
        dq_ref, dkv_ref, turned, key_sum, value_sum = rest
        step = pl.program_id(0)

        @pl.when(step == 0)
        def _():
            key_sum[...] = jnp.zeros_like(key_sum)
            value_sum[...] = jnp.zeros_like(value_sum)
            for pair in range(pairs):
                here = slice(pair * LANES, (pair + 1) * LANES)
                turned[here, :] = kv_ref[:, here].T

        def work(count, at):
            bias = mask_bias(
                begin_ref[0] + at * block_q, begin_ref[1], start_ref[...], (count, block_q), 0
            )
            for pair in range(pairs):
                here = slice(pair * LANES, (pair + 1) * LANES)
                there = slice(columns + pair * LANES, columns + (pair + 1) * LANES)
                q, grad = q_ref[:, here], grad_ref[:, here]
                product = (mixed_ref[:, here] * grad.astype(F32)).T
                k, v = kv_ref[:count, here], kv_ref[:count, there]
                key_terms, value_terms, query_terms = [], [], []
                for head in range(HEADS_TILE):
                    q_head, grad_head = head_part(q, head), head_part(grad, head)
                    inner = slice(head * HEAD_DIM, (head + 1) * HEAD_DIM)
                    delta = jnp.sum(product[inner], axis=0, keepdims=True)
                    index = HEADS_TILE * pair + head
                    score = contract(k, q_head, 1, 1) * scale + bias
                    weight = jnp.exp(score - log_ref[index : index + 1, :])
                    weight_grad = contract(v, grad_head, 1, 1)
                    score_grad = (weight * (weight_grad - delta)).astype(BF16)
                    value_terms.append(
                        jnp.dot(weight.astype(BF16), grad_head, preferred_element_type=F32)
                    )
                    key_terms.append(jnp.dot(score_grad, q_head, preferred_element_type=F32))
                    begin = pair * LANES + head * HEAD_DIM
                    query_terms.append(
                        jnp.dot(
                            turned[begin : begin + HEAD_DIM, :count],
                            score_grad,
                            preferred_element_type=F32,
                        )
                    )
                value_sum[:count, here] += value_terms[0] + value_terms[1]
                key_sum[:count, here] += key_terms[0] + key_terms[1]
                found = jnp.concatenate(query_terms, axis=0).T * scale
                if before is not None:
                    found = found + before_ref[:, here]
                dq_ref[:, here] = found

        if own:
            for at in range(steps):
                pl.when(step == at)(lambda at=at: work((at + 1) * block_q, at))
        else:
            work(keys, step)

        @pl.when(step == steps - 1)
        def _():
            dkv_ref[:, :columns] = (key_sum[...] * scale).astype(dkv_ref.dtype)
            dkv_ref[:, columns:] = value_sum[...].astype(dkv_ref.dtype)

    row = lambda i, s: (i, 0)
    lane = lambda i, s: (0, i)
    wide = pl.BlockSpec((block_q, columns), row)
    extra = [] if before is None else [before]
    out = [
        jax.ShapeDtypeStruct((tokens, columns), F32),
        jax.ShapeDtypeStruct((keys, 2 * columns), F32 if own else BF16),
    ]
    return kernel_call(
        body,
        begins,
        [queries, key_values, starts, mixed, logs, mixed_grad, *extra],
        [
            wide,
            full(key_values),
            pl.BlockSpec((1, block_q), lane),
            wide,
            pl.BlockSpec((heads, block_q), lane),
            wide,
        ]
        + [wide] * len(extra),
        out,
        [wide, full(out[1])],
        [
            pltpu.VMEM((columns, keys), BF16),
            pltpu.VMEM((keys, columns), F32),
            pltpu.VMEM((keys, columns), F32),
        ],
        "attend_backward",
        grid=(steps,),
    )


def join_qkv_grads(table, query_grad, own_pairs, far_pairs, tables):
    tokens, columns = query_grad.shape
    rows = math.gcd(tokens, 512)

    def body(table_ref, q_ref, own_ref, *rest):
        far_refs, (turn_ref, out_ref, sum_ref) = rest[: len(far_pairs)], rest[len(far_pairs) :]

        @pl.when(pl.program_id(0) == 0)
        def _():
            sum_ref[...] = jnp.zeros_like(sum_ref)

        cosine, lower, upper = turn_ref[0], -turn_ref[1], -turn_ref[2]
        for tile in range(3 * columns // LANES):
            here = slice(tile * LANES, (tile + 1) * LANES)
            if tile < columns // LANES:
                value = q_ref[:, here]
            else:
                there = slice(tile * LANES - columns, (tile + 1) * LANES - columns)
                value = own_ref[:, there]
                for ref in far_refs:
                    value = value + ref[:, there].astype(F32)
            if tile < 2 * columns // LANES:
                value = rope(value, cosine, lower, upper)
            low = value.astype(BF16)
            out_ref[:, here] = low
            sum_ref[:, here] += jnp.sum(low.astype(F32), axis=0, keepdims=True)

    row = lambda i, s: (i, 0)
    spec = lambda array: pl.BlockSpec((rows, array.shape[1]), row)
    out = [
        jax.ShapeDtypeStruct((tokens, 3 * columns), BF16),
        jax.ShapeDtypeStruct((1, 3 * columns), F32),
    ]
    inputs = [query_grad, own_pairs, *far_pairs]
    return kernel_call(
        body,
        table,
        [*inputs, tables],
        [spec(array) for array in inputs]
        + [pl.BlockSpec((3, rows, LANES), lambda i, s: (0, i, 0))],
        out,
        [spec(out[0]), full(out[1])],
        [],
        "join_qkv_grads",
        grid=(tokens // rows,),
    )


def cut_weights(layout, table, sources):
    n = len(sources)
    pieces = [source.pieces for source in sources]

    def body(table_ref, *rest):
        refs, outs, sems = rest[:n], rest[n : 3 * n], rest[3 * n]
        core = table_ref[2 * layout.places]
        copies = []
        for i, source in enumerate(sources):
            for j in range(pieces[i]):
                for k, half in enumerate((core, 1 - core)):
                    copies.append(
                        pltpu.make_async_copy(
                            source.read(refs[i], half, j),
                            source.part(outs[2 * i + k], j),
                            sems.at[i, j, k],
                        )
                    )
        start_all(copies)
        wait_all(copies)

    return kernel_call(
        body,
        table,
        [source.array for source in sources],
        [HBM] * n,
        [jax.ShapeDtypeStruct(source.shape, BF16) for source in sources for _ in range(2)],
        [HBM] * (2 * n),
        [pltpu.SemaphoreType.DMA((n, max(pieces), 2))],
        "cut_weights",
    )


def join_weights(table, sources, shape, owns, received):
    n = len(sources)

    def body(table_ref, *rest):
        refs, out_ref = rest[: 2 * n], rest[2 * n]
        for i, source in enumerate(sources):
            out_ref[source.place()] = refs[i][...]
            out_ref[source.other()] = refs[n + i][...]

    out = jax.ShapeDtypeStruct(shape, BF16)
    arrays = [*owns, *received]
    return kernel_call(
        body, table, arrays, [full(a) for a in arrays], out, full(out), [], "join_weights"
    )


class RowSource:
    def __init__(self, array, layer, begin):
        self.array, self.layer, self.begin = array, layer, begin
        self.split = array.ndim == 4
        self.pieces = array.shape[1] if self.split else 1
        self.rows = array.shape[-2]
        self.size = array.shape[-1] // 2
        self.shape = (self.rows, self.pieces * self.size)

    def read(self, ref, core, piece):
        here = pl.ds(pl.multiple_of(core * self.size, self.size), self.size)
        return ref.at[self.layer, piece, :, here] if self.split else ref.at[self.layer, :, here]

    def place(self):
        return slice(0, self.rows), slice(self.begin, self.begin + self.shape[1])

    def other(self):
        return slice(self.rows, 2 * self.rows), slice(self.begin, self.begin + self.shape[1])

    def part(self, target, piece):
        return target.at[:, piece * self.size : (piece + 1) * self.size]


class ColumnSource:
    pieces = 1

    def __init__(self, array, layer, begin):
        self.array, self.layer, self.begin = array, layer, begin
        self.size, self.columns = array.shape[1] // 2, array.shape[2]
        self.shape = (self.size, self.columns)

    def read(self, ref, core, piece):
        return ref.at[self.layer, pl.ds(pl.multiple_of(core * self.size, self.size), self.size), :]

    def place(self):
        return slice(self.begin, self.begin + self.size), slice(0, self.columns)

    def other(self):
        return slice(self.begin, self.begin + self.size), slice(self.columns, 2 * self.columns)

    def part(self, target, piece):
        return target


def core_half(value, axis, which):
    size = value.shape[axis] // lax.axis_size(C)
    return lax.dynamic_slice_in_dim(value, which * size, size, axis)


def in_core_order(own, other, axis):
    return jnp.where(
        lax.axis_index(C) == 0,
        jnp.concatenate([own, other], axis=axis),
        jnp.concatenate([other, own], axis=axis),
    )


class Gather:
    def __init__(self, order, block, first, second):
        self.order, self.first, self.second = order, first, second
        self.n1, self.n2 = lax.axis_size(first), lax.axis_size(second)
        self.found = {(0, 0): block}

    def near(self, depth=1):
        for i in range(1, self.n1):
            self.found[i, 0] = self.order.send(self.found[0, 0], self.first, i, depth)
        return [self.found[i, 0] for i in range(1, self.n1)]

    def side(self, depth=1):
        for j in range(1, self.n2):
            self.found[0, j] = self.order.send(self.found[0, 0], self.second, j, depth)
        return [self.found[0, j] for j in range(1, self.n2)]

    def cross(self, depth=1):
        found = []
        for i in range(1, self.n1):
            for j in range(1, self.n2):
                self.found[i, j] = self.order.send(self.found[i, 0], self.second, j, depth)
                found.append(self.found[i, j])
        return found

    def blocks(self):
        if self.first == X:
            return [self.found[b, a] for a in range(self.n2) for b in range(self.n1)]
        return [self.found[a, b] for a in range(self.n1) for b in range(self.n2)]


class ScatterIn:
    def __init__(self, order, layout, table, features, right):
        self.order, self.layout, self.table = order, layout, table
        self.features, self.right = features, right

    def compute(self):
        layout, n_x = self.layout, self.layout.n_x
        which = [a * n_x + b for a in range(1, layout.n_y) for b in range(n_x)]
        (self.parts,) = self.order.run(
            lambda f, r: grad_in(layout, self.table, f, r, which), self.features, self.right
        )

    def begin(self, depth=1):
        size = self.layout.n_x * self.layout.block
        self.received = [
            self.order.send(self.parts[(a - 1) * size : a * size], Y, -a, depth)
            for a in range(1, self.layout.n_y)
        ]

    def middle(self):
        layout = self.layout
        self.first, self.away, self.others = self.order.run(
            lambda f, r, d: grad_in(layout, self.table, f, r, range(layout.n_x), d),
            self.features,
            self.right,
            self.received,
        )

    def finish(self, depth=2):
        block = self.layout.block
        self.near = [
            self.order.send(self.others[(b - 1) * block : b * block], X, -b, depth)
            for b in range(1, self.layout.n_x)
        ]

    def swap(self):
        away = self.order.run(
            lambda a, b: fold(self.table, a, b, True), self.away, self.near
        )
        self.sums = ([self.first, *self.near], [self.order.send(away, C, 1, 3)])


class ScatterOut:
    def __init__(self, order, layout, table, lefts, grad):
        self.order, self.layout, self.table = order, layout, table
        self.lefts, self.grad = lefts, grad
        self.received = [[] for _ in range(layout.n_y)]

    def compute(self):
        layout, n_x = self.layout, self.layout.n_x
        which = [a * n_x + b for a in range(layout.n_y) for b in range(1, n_x)]
        self.parts = self.order.run(
            lambda l, g: grad_out(layout, self.table, l, g, which), self.lefts, self.grad
        )

    def begin(self, a, depth=1):
        n_x = self.layout.n_x
        for b in range(1, n_x):
            part = self.parts[a * (n_x - 1) + b - 1]
            self.received[a].append(self.order.send(part, X, -b, depth))

    def all_received(self):
        return [value for row in self.received for value in row]

    def middle(self):
        layout = self.layout
        which = [a * layout.n_x for a in range(layout.n_y)]
        self.first, self.away, *self.others = self.order.run(
            lambda l, g, d: grad_out(layout, self.table, l, g, which, d),
            self.lefts,
            self.grad,
            self.received,
        )

    def finish(self, depth=2):
        self.near = [
            self.order.send(self.others[a - 1], Y, -a, depth) for a in range(1, self.layout.n_y)
        ]

    def swap(self):
        away = self.order.run(
            lambda a, b: fold(self.table, a, b, False), self.away, self.near
        )
        self.sums = ([self.first, *self.near], [self.order.send(away, C, 1, 3)])


def per_device(
    layer_input,
    segment_ids,
    positions,
    norm_gain,
    norm_bias,
    qkv_weight,
    qkv_bias,
    dense_weight,
    dense_bias,
    up_weight,
    up_bias,
    down_weight,
    down_bias,
    output_cotangent,
):
    layer_count = qkv_weight.shape[0]
    last = layer_count - 1
    core, x = lax.axis_index(C), lax.axis_index(X)
    z, n_z = lax.axis_index(Z), lax.axis_size(Z)
    layout = Layout(*layer_input.shape)
    n_x = layout.n_x
    tokens, width = layout.tokens, layout.width
    columns = qkv_weight.shape[3] // layout.n_c
    hidden = up_weight.shape[2] // layout.n_c
    table = width_table(layout)
    query_begin = x * tokens
    begins = [
        jnp.stack([query_begin, (x - b + n_x) % n_x * tokens]).astype(jnp.int32) for b in range(n_x)
    ]
    order = Order()
    gathers = {}
    kept = [SimpleNamespace(layer=layer) for layer in range(layer_count)]
    outputs = [None] * layer_count
    sums = [None] * layer_count

    def arrived(*transfers):
        order.wait(*transfers)


    def sources_of(layer, group):
        if group == OUT:
            shape = (columns + hidden, layout.block)
            return shape, [
                ColumnSource(dense_weight, layer, 0),
                ColumnSource(down_weight, layer, columns),
            ]
        sources = []
        if group != UP:
            sources.append(RowSource(qkv_weight.transpose(0, 2, 1, 3), layer, 0))
        if group != QKV:
            begin = 3 * columns if group == IN else 0
            sources.append(RowSource(up_weight, layer, begin))
        return (layout.block, sum(source.shape[1] for source in sources)), sources

    def make_ready(layer, groups):
        found = []
        for group in groups:
            shape, sources = sources_of(layer, group)

            def cut(arrays, sources=sources):
                for source, array in zip(sources, arrays):
                    source.array = array
                return cut_weights(layout, table, sources)

            parts = order.run(cut, [source.array for source in sources])
            found.append((sources, shape, parts[::2], parts[1::2]))
        swapped = [[shift(value, C, 1) for value in order.after(away)] for *_, away in found]
        for group, (sources, shape, owns, _), received in zip(groups, found, swapped):
            block = order.run(
                lambda o, r, s=sources, h=shape: join_weights(table, s, h, o, r), owns, received
            )
            ways = (Y, X) if group == OUT else (X, Y)
            gathers[layer, group] = Gather(order, block, *ways)

    def blocks_of(layer, group):
        if (layer, group) not in gathers:
            group = IN
        return gathers[layer, group].blocks()


    def gather_features(block):
        return lax.all_gather(order.after([block])[0], (C, Z), axis=0, tiled=False)

    def scatter_features(summed):
        return lax.psum_scatter(order.after([summed])[0], Z, scatter_dimension=1, tiled=True)

    def to_owner(lefts, weights, transposed, name, awaited=()):
        away = order.run(
            lambda *a: project_back(layout, table, a[0], a[1], transposed, True, name), lefts, weights
        )
        received = [order.send(piece, C, 1, PIECES) for piece in away]
        (own,) = order.run(
            lambda *a: project_back(layout, table, a[0], a[1], transposed, False, name), lefts, weights
        )
        if awaited:
            order.wait(*awaited)
        return order.run(lambda a, b: merge_cores(layout, table, a, b), own, received)

    def moments(value, axes):
        mean = jnp.sum(value, axis=axes) / width
        return mean, jnp.sum(value * value, axis=axes) / width

    def inverse_of(mean, square):
        return lax.rsqrt(square - mean * mean + EPSILON)

    def normalise(k, residual):
        stats = jnp.stack([jnp.sum(residual, axis=1), jnp.sum(residual * residual, axis=1)])
        stats = sum_over(stats, Z) / width
        k.inverse = inverse_of(stats[0], stats[1])
        k.centred = (residual - stats[0][:, None]) * k.inverse[:, None]
        normed = (k.centred * norm_gain[k.layer] + norm_bias[k.layer]).astype(BF16)
        (normed,) = order.wait(normed)
        k.features = gather_features(normed)
        order.wait(normed)

    def qkv_shift(layer):
        return core_half(qkv_bias[layer], 1, core).reshape(1, -1)

    def up_shift(layer):
        return core_half(up_bias[layer], 0, core).reshape(1, -1)

    def project_q(k):
        k.q, pairs = order.run(
            lambda f, w, b, t: project_qkv(layout, table, f, w, b, t),
            k.features,
            blocks_of(k.layer, QKV),
            qkv_shift(k.layer),
            tables,
        )
        k.pairs = [pairs] + [order.send(pairs, X, b) for b in range(1, n_x)]

    def project_hidden(k, *grad):
        k.active, k.slope = order.run(
            lambda f, w, b, *g: project_up(layout, table, f, w, b, *g),
            k.features,
            blocks_of(k.layer, UP),
            up_shift(k.layer),
            *grad,
        )

    def grads_of_branch(k, grad_features, *slope):
        k.mixed_grad, k.hidden_grad = order.run(
            lambda g, w, *s: branch_grads(layout, table, g, w, columns, *s),
            grad_features,
            blocks_of(k.layer, OUT),
            *slope,
        )

    def own_attention(k):
        k.found = order.run(attend, begins[0], k.q, k.pairs[0], starts)

    def far_attention(k):
        for b in range(1, n_x):
            k.found = order.run(attend, begins[b], k.q, k.pairs[b], starts, k.found[1:])
        k.mixed_low, k.mixed, k.logs = k.found

    def far_gradients(k):
        k.query_grad, k.away_pairs = [], []
        for b in range(1, n_x):
            found, pair_grad = order.run(
                lambda *a: attend_backward(*a[:7], False, *a[7:]),
                *(begins[b], k.q, k.pairs[b], starts, k.mixed, k.logs, k.mixed_grad),
                *k.query_grad,
            )
            k.query_grad = [found]
            k.away_pairs.append(order.send(pair_grad, X, -b))

    def own_gradients(k):
        k.query_grad, k.own_pairs = order.run(
            lambda *a: attend_backward(*a[:7], True, *a[7:]),
            *(begins[0], k.q, k.pairs[0], starts, k.mixed, k.logs, k.mixed_grad),
            *k.query_grad,
        )

    def join_gradients(k):
        k.qkv_low, k.qkv_sum = order.run(
            lambda *a: join_qkv_grads(table, *a), k.query_grad, k.own_pairs, k.away_pairs, tables
        )

    def branch_sum(k):
        lefts = [k.mixed_low, k.active]
        pairs = [(block,) for block in blocks_of(k.layer, OUT)]
        return to_owner(lefts, pairs, False, "project_out")

    def feature_sum(k, *awaited):
        if (k.layer, IN) in gathers:
            pairs = [(block,) for block in blocks_of(k.layer, IN)]
        else:
            pairs = list(zip(blocks_of(k.layer, QKV), blocks_of(k.layer, UP)))
        return to_owner([k.qkv_low, k.up_low], pairs, True, "feature_grads", awaited)

    def add_branch(residual, branch, layer):
        return residual + branch.astype(F32) + dense_bias[layer] + down_bias[layer]


    residual = layer_input.astype(F32)
    raw = gather_features(layer_input)
    make_ready(0, [QKV])
    qkv = gathers[0, QKV]
    first_near, first_side = qkv.near(), qkv.side()
    grad_features = gather_features(output_cotangent)
    make_ready(0, [UP, OUT])
    up, out = gathers[0, UP], gathers[0, OUT]
    arrived(*first_near, *first_side)
    up_near, qkv_cross = up.near(), qkv.cross()
    query_segments = lax.dynamic_slice_in_dim(segment_ids, query_begin, tokens, 0)
    starts = jnp.sum(
        (segment_ids[:, None] < query_segments[None, :]).astype(jnp.int32), axis=0, keepdims=True
    )
    places = lax.dynamic_slice_in_dim(positions, query_begin, tokens, 0)
    tables = rope_tables(order.after([places])[0])
    starts, tables = order.wait(starts, tables)
    affine = order.after([jnp.stack([norm_gain[0], norm_bias[0]])])[0]
    spread = [affine] + [shift(affine, Z, k) for k in range(1, n_z)]
    spread = jnp.stack(spread)[(z - jnp.arange(n_z) + n_z) % n_z]
    (spread,) = order.wait(spread)
    arrived(*up_near, *qkv_cross)
    out_near, out_side = out.near(), out.side()
    (raw,) = order.wait(raw)
    blocks = raw.reshape(layout.n_c, n_z, layout.own_tokens, layout.part).astype(F32)
    mean, square = moments(blocks, (1, 3))
    inverse = inverse_of(mean, square)
    gain, bias = (spread[:, i][None, :, None, :] for i in range(2))
    normed = (blocks - mean[:, None, :, None]) * inverse[:, None, :, None] * gain + bias
    kept[0].inverse = lax.dynamic_index_in_dim(inverse, core, 0, keepdims=False)
    own_mean = lax.dynamic_index_in_dim(mean, core, 0, keepdims=False)
    (kept[0].features,) = order.wait(normed.astype(BF16).reshape(raw.shape))
    for k in kept[:-1]:
        layer = k.layer
        project_q(k)
        if layer == 0:
            up_side = up.side(2)
        own_attention(k)
        arrived(*k.pairs[1:])
        if layer == 0:
            arrived(*up_side, *out_near, *out_side)
            out_cross, up_cross = out.cross(), up.cross()
        far_attention(k)
        make_ready(layer + 1, [IN, OUT])
        in_next, out_next = gathers[layer + 1, IN], gathers[layer + 1, OUT]
        if layer == 0:
            arrived(grad_features, *up_cross, *out_cross)
        next_near, next_side = out_next.near(), out_next.side()
        project_hidden(k)
        summed = branch_sum(k)
        arrived(*next_near, *next_side)
        branch = scatter_features(summed)
        order.wait(summed)
        arrived(*in_next.near(), *in_next.side())
        (branch,) = order.wait(branch)
        residual = outputs[layer] = add_branch(residual, branch, layer)
        k = kept[layer + 1]
        normalise(k, residual)
        next_cross, in_cross = out_next.cross(), in_next.cross()
        if k.layer == last:
            arrived(*next_cross)
            grads_of_branch(k, grad_features)
        arrived(*in_cross)
        order.wait(k.features)


    k = kept[last]
    project_q(k)
    project_hidden(k, k.hidden_grad)
    k.up_low = k.slope
    gradient = output_cotangent.astype(F32)
    held = {UP: None, QKV: None, OUT: None}
    shapes = {
        UP: (layer_count, layout.place, layout.n_c * hidden),
        QKV: (layer_count, 3, layout.place, layout.n_c * columns),
        OUT: [
            (layer_count, layout.n_c * columns, layout.place),
            (layer_count, layout.n_c * hidden, layout.place),
        ],
    }

    def place(layer, group, scatter):
        def write(owns, others, before):
            if group == OUT:
                return place_out(layout, table, layer, owns, others, shapes[group], before)
            parts = 3 if group == QKV else 1
            return place_in(layout, table, layer, owns, others, shapes[group], before, parts)

        held[group] = order.run(write, *scatter.sums, held[group])

    def norm_backward(k, normed_grad, gradient):
        normed_grad = normed_grad.astype(F32)
        scaled_grad = normed_grad * norm_gain[k.layer]
        means = jnp.stack([jnp.sum(scaled_grad, axis=1), jnp.sum(scaled_grad * k.centred, axis=1)])
        means = sum_over(means, Z) / width
        new = gradient + k.inverse[:, None] * (
            scaled_grad - means[0][:, None] - k.centred * means[1][:, None]
        )

        def to_both(value):
            return in_core_order(value, jnp.zeros_like(value), value.ndim - 1).reshape(-1)

        sums[k.layer] = jnp.concatenate(
            [
                jnp.sum(normed_grad * k.centred, axis=0),
                jnp.sum(normed_grad, axis=0),
                to_both(k.qkv_sum.reshape(3, columns)),
                jnp.sum(gradient, axis=0),
                to_both(k.up_sum),
            ]
        )
        return new

    kept[0].centred = (layer_input.astype(F32) - own_mean[:, None]) * kept[0].inverse[:, None]
    before = None

    for k in reversed(kept):
        layer = k.layer
        scatter_in = lambda right: ScatterIn(order, layout, table, k.features, right)
        if layer == last:
            own_attention(k)
            arrived(*k.pairs[1:])
            up = scatter_in(k.up_low)
            up.compute()
            up.begin()
            far_attention(k)
        else:
            (grad_features,) = order.wait(grad_features)
            branch = None
            if layer + 1 == last:
                branch = scatter_features(out_summed)
        out = ScatterOut(order, layout, table, [k.mixed_low, k.active], grad_features)
        if layer < last:
            out.compute()
            out.begin(layout.n_y - 1, 1)
            grads_of_branch(k, grad_features, k.slope)
            k.up_low = k.hidden_grad
            up = scatter_in(k.up_low)
        far_gradients(k)
        if layer < last:
            up.compute()
            up.begin()
        own_gradients(k)
        if layer < last:
            before.swap()
            place(layer + 1, QKV, before)
            arrived(*k.away_pairs, *out.received[-1])
            for a in reversed(range(layout.n_y - 1)):
                out.begin(a, 1)
        else:
            out.compute()
            arrived(*k.away_pairs, *up.received)
        join_gradients(k)
        (k.up_sum,) = order.wait(jnp.sum(order.after([k.up_low])[0], axis=0, dtype=F32))
        qkv = scatter_in(k.qkv_low)
        if layer < last:
            qkv.compute()
        awaited = [] if layer == last else [*up.received, *out.all_received()]
        summed = feature_sum(k, *awaited)
        normed_grad = scatter_features(summed)
        order.wait(summed)
        if layer == last:
            for a in reversed(range(1, layout.n_y)):
                out.begin(a, 1)
            qkv.compute()
            qkv.begin()
            up.middle()
            out_summed = branch_sum(k)
            out.begin(0, 1)
            (normed_grad,) = order.wait(normed_grad)
            gradient = norm_backward(k, normed_grad, gradient)
            (low,) = order.wait(gradient.astype(BF16))
            arrived(*out.all_received(), *qkv.received)
            grad_features = gather_features(low)
            order.wait(low)
            up.finish(1)
            out.middle()
            out.finish(1)
            qkv.middle()
            qkv.finish(1)
            arrived(*up.near)
            up.swap()
            place(layer, UP, up)
            arrived(*out.near)
            out.swap()
            place(layer, OUT, out)
            arrived(*qkv.near)
        else:
            qkv.begin()
            up.middle()
            up.finish(1)
            if branch is not None:
                outputs[last] = add_branch(residual, branch, last)
                (outputs[last],) = order.wait(outputs[last])
            out.middle()
            arrived(*qkv.received)
            out.finish(1)
            qkv.middle()
            qkv.finish(1)
            (normed_grad,) = order.wait(normed_grad)
            gradient = norm_backward(k, normed_grad, gradient)
            (gradient,) = order.wait(gradient)
            if layer > 0:
                up.swap()
                out.swap()
                place(layer, UP, up)
                place(layer, OUT, out)
        before = qkv

    small = sum_over(jnp.stack(order.after(sums)), C)
    arrived(*qkv.near, *up.near, *out.near)
    (small,) = order.wait(small)
    small = sum_over(small, X)
    qkv.swap()
    up.swap()
    out.swap()
    place(0, UP, up)
    (small,) = order.wait(small)
    small = sum_over(small, Y)
    place(0, OUT, out)
    place(0, QKV, qkv)

    small, gradient, outputs = order.now((small, gradient, outputs))
    held = order.now(held)
    part, both = layout.part, layout.n_c * columns
    ends = [0]
    for size in (part, part, 3 * both, part, layout.n_c * hidden):
        ends.append(ends[-1] + size)
    gain_grad, shift_grad, qkv_grad, out_bias_grad, up_grad = [
        small[:, begin:end] for begin, end in zip(ends[:-1], ends[1:])
    ]
    return (
        jnp.stack(outputs),
        gradient,
        gain_grad,
        shift_grad,
        held[QKV].transpose(0, 2, 1, 3),
        qkv_grad.reshape(layer_count, 3, both),
        held[OUT][0],
        out_bias_grad,
        held[UP],
        up_grad,
        held[OUT][1],
        out_bias_grad,
    )


def solution(mesh):
    n_y, n_row, n_z = (mesh.shape[name] for name in mesh.axis_names)
    split = Mesh(mesh.devices.reshape(n_y, n_row // 2, 2, n_z), (Y, X, C, Z))
    rows = (Y, X, C)
    placed = (
        P(rows, Z),
        P(Y),
        P(Y),
        P(None, Z),
        P(None, Z),
        P(None, rows, None, Z),
        P(None, None, Z),
        P(None, Z, rows),
        P(None, Z),
        P(None, rows, Z),
        P(None, Z),
        P(None, Z, rows),
        P(None, Z),
        P(rows, Z),
    )
    return jax.shard_map(
        per_device,
        mesh=split,
        in_specs=placed,
        out_specs=(
            P(None, rows, Z),
            P(rows, Z),
            P(None, Z),
            P(None, Z),
            P(None, rows, None, Z),
            P(None, None, Z),
            P(None, Z, rows),
            P(None, Z),
            P(None, rows, Z),
            P(None, Z),
            P(None, Z, rows),
            P(None, Z),
        ),
        check_vma=False,
    )
```

```python
import math
from types import SimpleNamespace

import jax
import jax.numpy as jnp
from jax import lax
from jax.experimental import pallas as pl
from jax.experimental.pallas import tpu as pltpu
from jax.sharding import Mesh
from jax.sharding import PartitionSpec as P

HEAD_DIM = 64
ROT = 32
EPSILON = 1e-05
NEGATIVE = -1e30
LANES = 128
HEADS_TILE = LANES // HEAD_DIM
MEBI = 1024 * 1024
PIECES = 2
VMEM_MEBI = 22
MORE_MEBI = 26
F32 = jnp.float32
BF16 = jnp.bfloat16
ANY = pl.BlockSpec(memory_space=pl.ANY)
HBM = pl.BlockSpec(memory_space=pltpu.HBM)
Y, X, C, Z = "dp", "x", "core", "col"
QKV, UP, OUT, IN = range(4)
COST = pl.CostEstimate(flops=1, bytes_accessed=1, transcendentals=0)


def contract(left, right, left_dim, right_dim):
    return lax.dot_general(
        left, right, (((left_dim,), (right_dim,)), ((), ())), preferred_element_type=F32
    )


def shift(value, axis, step):
    size = lax.axis_size(axis)
    return lax.ppermute(value, axis, [(i, (i + step) % size) for i in range(size)])


class Order:
    def __init__(self):
        self.last = []
        self.links = {}
        self.newest = {}

    def now(self, values):
        def one(value):
            while id(value) in self.newest:
                value = self.newest[id(value)][1]
            return value

        return jax.tree.map(one, values)

    def after(self, values, *others):
        leaves, tree = jax.tree.flatten(self.now(values))
        held = self.now([other for other in (*self.last, *others) if other is not None])
        every = {id(value): value for value in (*leaves, *held)}
        if held:
            for old, new in zip(every.values(), lax.optimization_barrier(tuple(every.values()))):
                self.newest[id(old)] = (old, new)
        return self.now(jax.tree.unflatten(tree, leaves))

    def run(self, function, *values):
        out = function(*self.after(values))
        self.last = jax.tree.leaves(out)
        return out

    def send(self, value, axis, step, depth=2):
        queue = self.links.setdefault(axis, [])
        held = queue[-depth] if len(queue) >= depth else None
        out = shift(self.after([value], held)[0], axis, step)
        queue.append(out)
        return out

    def wait(self, *values):
        out = self.after(list(values))
        self.last = [*self.last, *out]
        return out


def sum_over(value, axis):
    return value + sum(shift(value, axis, k) for k in range(1, lax.axis_size(axis)))


def width_table(layout):
    n_y, n_x, n_c = lax.axis_size(Y), lax.axis_size(X), lax.axis_size(C)
    y, x, c = lax.axis_index(Y), lax.axis_index(X), lax.axis_index(C)
    begins = jnp.stack(
        [
            ((((y - a + n_y) % n_y) * n_x + (x - b + n_x) % n_x) * n_c + (c - k + n_c) % n_c)
            * layout.place
            for a in range(n_y)
            for b in range(n_x)
            for k in range(n_c)
        ]
    )
    return jnp.concatenate(
        [begins // layout.part, begins % layout.part, c[None], begins]
    ).astype(jnp.int32)


class Layout:
    def __init__(self, own_tokens, part):
        self.n_y, self.n_x, self.n_c, self.n_z = (
            lax.axis_size(name) for name in (Y, X, C, Z)
        )
        self.own_tokens = own_tokens
        self.tokens = own_tokens * self.n_c
        self.part = part
        self.width = part * self.n_z
        self.places = self.n_y * self.n_x * self.n_c
        self.place = self.width // self.places
        self.block = self.place * self.n_c
        self.blocks = self.n_y * self.n_x

    def fetch(self, table, gathered, core, places, target, sems, first):
        copies = []
        for slot, at in enumerate(places):
            begin = pl.multiple_of(table[self.places + at], self.place)
            copies.append(
                pltpu.make_async_copy(
                    gathered.at[core * self.n_z + table[at], :, pl.ds(begin, self.place)],
                    target.at[:, slot * self.place : (slot + 1) * self.place],
                    sems.at[first + slot],
                )
            )
        return copies


def kernel_call(body, table, inputs, in_specs, out_shape, out_specs, scratch, name, grid=(1,), aliases=None, mebi=VMEM_MEBI):
    return pl.pallas_call(
        body,
        grid_spec=pltpu.PrefetchScalarGridSpec(
            num_scalar_prefetch=1,
            grid=grid,
            in_specs=in_specs,
            out_specs=out_specs,
            scratch_shapes=scratch,
        ),
        out_shape=out_shape,
        input_output_aliases=aliases or {},
        compiler_params=pltpu.CompilerParams(vmem_limit_bytes=mebi * MEBI),
        cost_estimate=COST,
        name=name,
    )(table, *inputs)


def full(array_or_shape):
    shape = getattr(array_or_shape, "shape", array_or_shape)
    return pl.BlockSpec(tuple(shape), lambda i, t: (0,) * len(shape))


def start_all(copies):
    for copy in copies:
        copy.start()


def wait_all(copies):
    for copy in copies:
        copy.wait()


def rope(value, cosine, lower, upper):
    half = ROT // 2
    return (
        value * cosine
        + pltpu.roll(value, LANES - half, 1) * lower
        + pltpu.roll(value, half, 1) * upper
    )


def rope_tables(place_values):
    half = ROT // 2
    freq_table = 1.0 / 10000.0 ** (jnp.arange(half, dtype=F32) * 2.0 / ROT)
    angles = place_values.astype(F32)[:, None] * freq_table
    cosine, sine = jnp.cos(angles), jnp.sin(angles)
    rest = jnp.ones((angles.shape[0], HEAD_DIM - ROT), F32)
    none = jnp.zeros_like(sine)
    pair = lambda *pieces: jnp.concatenate(pieces * HEADS_TILE, axis=1)
    return jnp.stack(
        [
            pair(cosine, cosine, rest),
            pair(-sine, none, 0.0 * rest),
            pair(none, sine, 0.0 * rest),
        ]
    )


class Stream:
    def __init__(self, layout, table, gathered, weights, features, buffers, sems, w_sems, window=None):
        self.layout, self.features, self.buffers = layout, features, buffers
        if window is not None:
            weights = [ref.at[:, window] for ref in weights]
        n_c = layout.n_c
        self.pieces = [
            [
                layout.fetch(
                    table,
                    gathered,
                    core,
                    range(b * n_c, (b + 1) * n_c),
                    features.at[core, b],
                    sems.at[core, b],
                    0,
                )
                for b in range(layout.blocks)
            ]
            for core in range(n_c)
        ]
        self.weights = [
            pltpu.make_async_copy(ref, buffer, w_sems.at[b])
            for b, (ref, buffer) in enumerate(zip(weights, buffers))
        ]
        for core in range(n_c):
            for b in range(layout.blocks):
                if core == 0:
                    self.weights[b].start()
                start_all(self.pieces[core][b])

    def run(self, total, parts, product, finish):
        last = self.layout.blocks - 1
        for core in range(self.layout.n_c):
            for b in range(last + 1):
                if core == 0:
                    self.weights[b].wait()
                wait_all(self.pieces[core][b])
                for part in parts:
                    term = product(self.features[core, b], self.buffers[b], part)
                    if 0 < b:
                        term = total[:, part] + term
                    if b < last:
                        total[:, part] = term
                    else:
                        finish(core, part, term)

    @staticmethod
    def scratch(layout, shape, outputs):
        n_c, count = layout.n_c, layout.blocks
        return [
            pltpu.VMEM((n_c, count, layout.own_tokens, layout.block), BF16),
            *[pltpu.VMEM(shape, BF16) for _ in range(count)],
            pltpu.SemaphoreType.DMA((n_c, count, n_c)),
            pltpu.SemaphoreType.DMA((count,)),
            pltpu.VMEM((layout.own_tokens, outputs), F32),
        ]


def chunks(size, step=256):
    step = math.gcd(size, step)
    return [slice(begin, begin + step) for begin in range(0, size, step)]


def project_qkv(layout, table, gathered, blocks, bias, tables):
    columns = bias.shape[1] // 3
    rows, count = layout.own_tokens, layout.blocks

    def body(table_ref, g_ref, *rest):
        w_refs, rest = rest[:count], rest[count:]
        bias_ref, tables_ref, q_ref, kv_ref, features = rest[:5]
        buffers, (sems, w_sems, total, turns, turn_sem) = rest[5 : 5 + count], rest[5 + count :]
        window = slice(0, 3 * columns)
        stream = Stream(layout, table_ref, g_ref, w_refs, features, buffers, sems, w_sems, window)
        turn = pltpu.make_async_copy(tables_ref, turns, turn_sem)
        turn.start()

        def finish(core, part, value):
            if core == 0 and part.start == 0:
                turn.wait()
            here = slice(core * rows, (core + 1) * rows)
            value = value + bias_ref[:, part]
            for lanes in chunks(columns, LANES):
                piece = value[:, lanes]
                if part.start < 2 * columns:
                    piece = rope(piece, *(turns[i, here, :] for i in range(3)))
                begin = part.start + lanes.start
                if part.start < columns:
                    q_ref[here, begin : begin + LANES] = piece.astype(BF16)
                else:
                    kv_ref[here, begin - columns : begin - columns + LANES] = piece.astype(BF16)

        stream.run(
            total,
            [slice(i * columns, (i + 1) * columns) for i in range(3)],
            lambda f, w, part: jnp.dot(f, w[:, part], preferred_element_type=F32),
            finish,
        )

    out = [
        jax.ShapeDtypeStruct((layout.tokens, columns), BF16),
        jax.ShapeDtypeStruct((layout.tokens, 2 * columns), BF16),
    ]
    return kernel_call(
        body,
        table,
        [gathered, *blocks, bias, tables],
        [HBM] * (1 + count) + [full(bias), HBM],
        out,
        [full(o) for o in out],
        Stream.scratch(layout, (layout.block, 3 * columns), 3 * columns)
        + [pltpu.VMEM(tables.shape, F32), pltpu.SemaphoreType.DMA],
        "project_qkv",
        mebi=MORE_MEBI,
    )


def gelu_and_slope(v):
    inner = math.sqrt(2 / math.pi) * v * (1.0 + 0.044715 * v * v)
    curve = jnp.tanh(inner)
    slope = 0.5 * (1.0 + curve) + 0.5 * v * (1.0 - curve * curve) * math.sqrt(2 / math.pi) * (
        1.0 + 3 * 0.044715 * v * v
    )
    return 0.5 * v * (1.0 + curve), slope


def project_up(layout, table, gathered, blocks, bias, active_grad=None):
    hidden = bias.shape[1]
    window = slice(blocks[0].shape[1] - hidden, blocks[0].shape[1])
    rows, count = layout.own_tokens, layout.blocks
    known = active_grad is not None

    def body(table_ref, g_ref, *rest):
        w_refs, rest = rest[:count], rest[count:]
        if known:
            grad_ref, rest = rest[0], rest[1:]
        bias_ref, act_ref, slope_ref, features = rest[:4]
        buffers, (sems, w_sems, total, act_buf, slope_buf, out_sems) = rest[4 : 4 + count], rest[4 + count :]
        stream = Stream(layout, table_ref, g_ref, w_refs, features, buffers, sems, w_sems, window)
        outs = []
        parts = chunks(hidden)

        def finish(core, part, value):
            here = slice(core * rows, (core + 1) * rows)
            active, slope = gelu_and_slope(value + bias_ref[:, part])
            act_buf[here, part] = active.astype(BF16)
            if known:
                slope = slope * grad_ref[here, part].astype(F32)
            slope_buf[here, part] = slope.astype(BF16)
            if part.stop == hidden:
                for i, (buffer, ref) in enumerate(((act_buf, act_ref), (slope_buf, slope_ref))):
                    outs.append(
                        pltpu.make_async_copy(buffer.at[here], ref.at[here], out_sems.at[core, i])
                    )
                    outs[-1].start()

        stream.run(
            total,
            parts,
            lambda f, w, part: jnp.dot(f, w[:, part], preferred_element_type=F32),
            finish,
        )
        wait_all(outs)

    out = [jax.ShapeDtypeStruct((layout.tokens, hidden), BF16)] * 2
    extra = [active_grad] if known else []
    return kernel_call(
        body,
        table,
        [gathered, *blocks, *extra, bias],
        [HBM] * (1 + count) + [full(e) for e in extra] + [full(bias)],
        out,
        [ANY, ANY],
        Stream.scratch(layout, (layout.block, hidden), hidden)
        + [pltpu.VMEM((layout.tokens, hidden), BF16)] * 2
        + [pltpu.SemaphoreType.DMA((layout.n_c, 2))],
        "project_up",
        mebi=MORE_MEBI,
    )


def branch_grads(layout, table, gathered, blocks, columns, slope=None):
    rows, count = layout.own_tokens, layout.blocks
    height = blocks[0].shape[0]
    hidden = height - columns
    known = slope is not None

    def body(table_ref, g_ref, *rest):
        w_refs, rest = rest[:count], rest[count:]
        if known:
            slope_ref, rest = rest[0], rest[1:]
        mixed_ref, hidden_ref, features = rest[:3]
        buffers, (sems, w_sems, total, mixed_buf, hidden_buf, out_sems) = (
            rest[3 : 3 + count],
            rest[3 + count :],
        )
        stream = Stream(layout, table_ref, g_ref, w_refs, features, buffers, sems, w_sems)
        outs = []

        def finish(core, part, value):
            here = slice(core * rows, (core + 1) * rows)
            if part.start < columns:
                mixed_buf[here, part] = value.astype(BF16)
            else:
                to = slice(part.start - columns, part.stop - columns)
                if known:
                    value = value * slope_ref[here, to].astype(F32)
                hidden_buf[here, to] = value.astype(BF16)
            if part.stop == height:
                for i, (buffer, ref) in enumerate(((mixed_buf, mixed_ref), (hidden_buf, hidden_ref))):
                    outs.append(
                        pltpu.make_async_copy(buffer.at[here], ref.at[here], out_sems.at[core, i])
                    )
                    outs[-1].start()

        stream.run(
            total,
            chunks(height, math.gcd(columns, 256)),
            lambda f, w, part: contract(f, w[part, :], 1, 1),
            finish,
        )
        wait_all(outs)

    out = [
        jax.ShapeDtypeStruct((layout.tokens, columns), BF16),
        jax.ShapeDtypeStruct((layout.tokens, hidden), BF16),
    ]
    extra = [slope] if known else []
    return kernel_call(
        body,
        table,
        [gathered, *blocks, *extra],
        [HBM] * (1 + count) + [full(e) for e in extra],
        out,
        [ANY, ANY],
        Stream.scratch(layout, blocks[0].shape, height)
        + [pltpu.VMEM(o.shape, BF16) for o in out]
        + [pltpu.SemaphoreType.DMA((layout.n_c, 2))],
        "branch_grads",
        mebi=MORE_MEBI,
    )


def project_back(layout, table, lefts, weights, transposed, away, name):
    rows, count = layout.own_tokens, len(weights)
    per_block = len(weights[0])
    sizes = [left.shape[1] for left in lefts]
    flat = [w for block in weights for w in block]
    n = len(lefts)
    pieces = PIECES if away else 1
    step = rows // pieces

    def body(table_ref, *rest):
        left_refs, rest = rest[:n], rest[n:]
        w_refs, rest = rest[: len(flat)], rest[len(flat) :]
        out_refs, rest = rest[:pieces], rest[pieces:]
        left_bufs, rest = rest[:n], rest[n:]
        w_bufs, (sems, w_sems) = rest[: len(flat)], rest[len(flat) :]
        core = table_ref[2 * layout.places]
        begin = pl.multiple_of((lax.rem(core + 1, layout.n_c) if away else core) * rows, rows)
        copies = [
            pltpu.make_async_copy(ref.at[pl.ds(begin, rows), :], buf, sems.at[i])
            for i, (ref, buf) in enumerate(zip(left_refs, left_bufs))
        ]
        w_copies = [
            pltpu.make_async_copy(ref, buf, w_sems.at[i])
            for i, (ref, buf) in enumerate(zip(w_refs, w_bufs))
        ]
        start_all(copies + w_copies)
        wait_all(copies)
        for b in range(count):
            wait_all(w_copies[b * per_block : (b + 1) * per_block])
            total = None
            at = 0
            for i, buf in enumerate(left_bufs):
                if per_block == 1:
                    here = slice(at, at + sizes[i])
                    w = w_bufs[b][:, here] if transposed else w_bufs[b][here, :]
                    at += sizes[i]
                else:
                    w = w_bufs[b * per_block + i][...]
                term = contract(buf[...], w, 1, 1 if transposed else 0)
                total = term if total is None else total + term
            for i in range(pieces):
                out_refs[i][:, b * layout.block : (b + 1) * layout.block] = total[
                    i * step : (i + 1) * step
                ].astype(BF16)

    out = [jax.ShapeDtypeStruct((step, layout.width), BF16)] * pieces
    return kernel_call(
        body,
        table,
        [*lefts, *flat],
        [ANY] * n + [HBM] * len(flat),
        out,
        [full(o) for o in out],
        [pltpu.VMEM((rows, size), BF16) for size in sizes]
        + [pltpu.VMEM(w.shape, BF16) for w in flat]
        + [
            pltpu.SemaphoreType.DMA((n,)),
            pltpu.SemaphoreType.DMA((len(flat),)),
        ],
        name,
        mebi=MORE_MEBI,
    )


def merge_cores(layout, table, own, received):
    rows = layout.own_tokens // PIECES
    place, places, n_c = layout.place, layout.places, layout.n_c

    def body(table_ref, own_ref, *refs):
        out_ref = refs[PIECES]

        def write(other_ref):
            for at in range(places):
                begin = pl.multiple_of(table_ref[2 * places + 1 + at], place)
                there = at // n_c * n_c + (n_c - at % n_c) % n_c if n_c != 2 else at ^ 1
                total = own_ref[:, at * place : (at + 1) * place].astype(F32)
                total = total + other_ref[:, there * place : (there + 1) * place].astype(F32)
                out_ref[:, pl.ds(begin, place)] = total.astype(BF16)

        for i in range(PIECES):
            pl.when(pl.program_id(0) == i)(lambda i=i: write(refs[i]))

    spec = pl.BlockSpec((rows, layout.width), lambda i, t: (i, 0))
    return kernel_call(
        body,
        table,
        [own, *received],
        [spec] + [full(piece) for piece in received],
        jax.ShapeDtypeStruct((layout.own_tokens, layout.width), BF16),
        spec,
        [],
        "merge_cores",
        grid=(PIECES,),
    )


def fetch_blocks(layout, table, gathered, which, features, sems):
    n_c, rows = layout.n_c, layout.own_tokens
    return [
        [
            layout.fetch(
                table,
                gathered,
                core,
                range(b * n_c, (b + 1) * n_c),
                features.at[i, pl.ds(core * rows, rows), :],
                sems.at[i, core],
                0,
            )
            for core in range(n_c)
        ]
        for i, b in enumerate(which)
    ]


def grad_in(layout, table, gathered, right, which, added=None):
    n = right.shape[1]
    count, place, n_c, block = len(which), layout.place, layout.n_c, layout.block
    final = added is not None
    extra = list(added or [])

    def body(table_ref, g_ref, right_ref, *rest):
        add_refs, rest = rest[: len(extra)], rest[len(extra) :]
        outs, rest = rest[: len(out)], rest[len(out) :]
        features, right_buf, sems, right_sem, rest = *rest[:4], rest[4:]
        pieces = fetch_blocks(layout, table_ref, g_ref, which, features, sems)
        right_copy = pltpu.make_async_copy(right_ref, right_buf, right_sem)
        right_copy.start()
        for group in pieces:
            for piece in group:
                start_all(piece)
        add_bufs, rest = rest[: len(extra)], rest[len(extra) :]
        if final:
            add_sems, rest = rest[0], rest[1:]
            add_copies = [
                pltpu.make_async_copy(ref, buf, add_sems.at[i])
                for i, (ref, buf) in enumerate(zip(add_refs, add_bufs))
            ]
            start_all(add_copies)
        right_copy.wait()
        if not final:
            out_buf, out_sems = rest
        copies = []
        for i in range(count):
            for piece in pieces[i]:
                wait_all(piece)
            if final and i == 0:
                wait_all(add_copies)
            for k in range(n_c):
                value = contract(features[i, :, k * place : (k + 1) * place], right_buf[...], 0, 0)
                begin = i * block + k * place
                if not final:
                    out_buf[begin : begin + place, :] = value.astype(BF16)
                    continue
                for buf in add_bufs:
                    value = value + buf[begin : begin + place, :].astype(F32)
                if i > 0:
                    outs[2][begin - block : begin - block + place, :] = value.astype(BF16)
                elif k > 0:
                    outs[1][(k - 1) * place : k * place, :] = value.astype(BF16)
                else:
                    outs[0][...] = value
            if not final:
                here = slice(i * block, (i + 1) * block)
                copies.append(pltpu.make_async_copy(out_buf.at[here], outs[0].at[here], out_sems.at[i]))
                copies[-1].start()
        wait_all(copies)

    if final:
        out = [
            jax.ShapeDtypeStruct((place, n), F32),
            jax.ShapeDtypeStruct((block - place, n), BF16),
            jax.ShapeDtypeStruct(((count - 1) * block, n), BF16),
        ]
        more = [pltpu.VMEM(e.shape, BF16) for e in extra]
        more.append(pltpu.SemaphoreType.DMA((len(extra),)))
    else:
        out = [jax.ShapeDtypeStruct((count * block, n), BF16)]
        more = [pltpu.VMEM(out[0].shape, BF16), pltpu.SemaphoreType.DMA((count,))]
    return kernel_call(
        body,
        table,
        [gathered, right, *extra],
        [HBM] + [ANY] * (1 + len(extra)),
        out,
        [full(o) for o in out] if final else [ANY],
        [
            pltpu.VMEM((count, layout.tokens, block), BF16),
            pltpu.VMEM(right.shape, BF16),
            pltpu.SemaphoreType.DMA((count, n_c, n_c)),
            pltpu.SemaphoreType.DMA,
        ]
        + more,
        "grad_in",
        mebi=MORE_MEBI,
    )


def grad_out(layout, table, lefts, gathered, which, added=None):
    sizes = [left.shape[1] for left in lefts]
    m, n = sum(sizes), len(lefts)
    count, place, n_c, block = len(which), layout.place, layout.n_c, layout.block
    final = added is not None
    extra = [e for block_added in added for e in block_added] if final else []
    per_block = len(extra) // count

    def body(table_ref, g_ref, *rest):
        left_refs, rest = rest[:n], rest[n:]
        add_refs, rest = rest[: len(extra)], rest[len(extra) :]
        outs, rest = rest[: len(out)], rest[len(out) :]
        features, sems, left_sems, rest = *rest[:3], rest[3:]
        left_bufs, rest = rest[:n], rest[n:]
        left_copies = [
            pltpu.make_async_copy(ref, buf, left_sems.at[i])
            for i, (ref, buf) in enumerate(zip(left_refs, left_bufs))
        ]
        pieces = fetch_blocks(layout, table_ref, g_ref, which, features, sems)
        start_all(left_copies[:1])
        for piece in pieces[0]:
            start_all(piece)
        start_all(left_copies[1:])
        for group in pieces[1:]:
            for piece in group:
                start_all(piece)
        add_bufs, rest = rest[: len(extra)], rest[len(extra) :]
        if final:
            add_sems, rest = rest[0], rest[1:]
            add_copies = [
                pltpu.make_async_copy(ref, buf, add_sems.at[i])
                for i, (ref, buf) in enumerate(zip(add_refs, add_bufs))
            ]
            start_all(add_copies)
        if not final:
            out_buf, out_sems = rest
        copies = []
        for i in range(count):
            for piece in pieces[i]:
                wait_all(piece)
            if final:
                wait_all(add_copies[i * per_block : (i + 1) * per_block])
            at = 0
            for j, (left_buf, size) in enumerate(zip(left_bufs, sizes)):
                if i == 0:
                    left_copies[j].wait()
                for part in chunks(size):
                    rows = slice(at + part.start, at + part.stop)
                    value = contract(left_buf[:, part], features[i], 0, 0)
                    if not final:
                        out_buf[i, rows, :] = value.astype(BF16)
                        continue
                    for buf in add_bufs[i * per_block : (i + 1) * per_block]:
                        value = value + buf[rows, :].astype(F32)
                    if i == 0:
                        outs[0][rows, :] = value[:, :place]
                        outs[1][rows, :] = value[:, place:].astype(BF16)
                    else:
                        outs[1 + i][rows, :] = value.astype(BF16)
                at += size
            if not final:
                copies.append(pltpu.make_async_copy(out_buf.at[i], outs[i], out_sems.at[i]))
                copies[-1].start()
        wait_all(copies)

    if final:
        out = [
            jax.ShapeDtypeStruct((m, place), F32),
            jax.ShapeDtypeStruct((m, block - place), BF16),
            *[jax.ShapeDtypeStruct((m, block), BF16)] * (count - 1),
        ]
        more = [pltpu.VMEM(e.shape, BF16) for e in extra]
        more.append(pltpu.SemaphoreType.DMA((len(extra),)))
    else:
        out = [jax.ShapeDtypeStruct((m, block), BF16)] * count
        more = [pltpu.VMEM((count, m, block), BF16), pltpu.SemaphoreType.DMA((count,))]
    return kernel_call(
        body,
        table,
        [gathered, *lefts, *extra],
        [HBM] + [ANY] * (n + len(extra)),
        out,
        [full(o) for o in out] if final else [ANY] * count,
        [
            pltpu.VMEM((count, layout.tokens, block), BF16),
            pltpu.SemaphoreType.DMA((count, n_c, n_c)),
            pltpu.SemaphoreType.DMA((n,)),
        ]
        + [pltpu.VMEM(left.shape, BF16) for left in lefts]
        + more,
        "grad_out",
        mebi=MORE_MEBI,
    )


def fold(table, away, near, rows):
    m, n = away.shape
    spec = pl.BlockSpec((m, n), lambda i, t: (1, 0) if rows else (0, 1))

    def body(table_ref, away_ref, *refs):
        near_refs, out_ref = refs[:-1], refs[-1]
        total = away_ref[...].astype(F32)
        for ref in near_refs:
            total = total + ref[...].astype(F32)
        out_ref[...] = total.astype(BF16)

    return kernel_call(
        body,
        table,
        [away, *near],
        [full(away)] + [spec] * len(near),
        jax.ShapeDtypeStruct((m, n), BF16),
        full(away),
        [],
        "fold",
    )


def place_in(layout, table, layer, owns, others, shape, held, parts):
    rows, n = owns[0].shape
    step = n // parts
    inputs = [*owns, *others]

    def body(table_ref, *refs):
        refs, out_ref = refs[: len(inputs)], refs[-1]

        def write(sources):
            value = sum(ref[...].astype(F32) for ref in sources)
            if parts == 1:
                out_ref[...] = value
            else:
                for i in range(parts):
                    out_ref[i] = value[:, i * step : (i + 1) * step]

        pl.when(pl.program_id(0) == 0)(lambda: write(refs[: len(owns)]))
        pl.when(pl.program_id(0) == 1)(lambda: write(refs[len(owns) :]))

    half = lambda i, t: lax.rem(t[2 * layout.places] + i, layout.n_c)
    if parts == 1:
        spec = pl.BlockSpec((None, rows, n), lambda i, t: (layer, 0, half(i, t)))
    else:
        spec = pl.BlockSpec((None, parts, rows, step), lambda i, t: (layer, 0, 0, half(i, t)))
    more = [] if held is None else [held]
    return kernel_call(
        body,
        table,
        inputs + more,
        [pl.BlockSpec((rows, n), lambda i, t: (0, 0)) for v in inputs] + [ANY] * len(more),
        jax.ShapeDtypeStruct(shape, F32),
        spec,
        [],
        "place_in",
        grid=(2,),
        aliases={1 + len(inputs): 0} if more else None,
    )


def place_out(layout, table, layer, owns, others, shapes, held):
    m, place = owns[0].shape
    inputs = [*owns, *others]
    sizes = [shape[1] // layout.n_c for shape in shapes]
    more = [] if held is None else list(held)

    def body(table_ref, *refs):
        refs, out_refs = refs[: len(inputs)], refs[len(inputs) + len(more) :]

        def write(sources):
            at = 0
            for ref, size in zip(out_refs, sizes):
                ref[...] = sum(source[at : at + size, :].astype(F32) for source in sources)
                at += size

        pl.when(pl.program_id(0) == 0)(lambda: write(refs[: len(owns)]))
        pl.when(pl.program_id(0) == 1)(lambda: write(refs[len(owns) :]))

    half = lambda i, t: lax.rem(t[2 * layout.places] + i, layout.n_c)
    return kernel_call(
        body,
        table,
        inputs + more,
        [pl.BlockSpec((m, place), lambda i, t: (0, 0)) for v in inputs] + [ANY] * len(more),
        [jax.ShapeDtypeStruct(shape, F32) for shape in shapes],
        [pl.BlockSpec((None, size, place), lambda i, t: (layer, half(i, t), 0)) for size in sizes],
        [],
        "place_out",
        grid=(2,),
        aliases={1 + len(inputs) + i: i for i in range(len(more))} or None,
    )


def head_part(value, head):
    lane = lax.broadcasted_iota(jnp.int32, value.shape, 1)
    keep = (lane >= head * HEAD_DIM) & (lane < (head + 1) * HEAD_DIM)
    return jnp.where(keep, value, jnp.zeros_like(value))


def mask_bias(query_begin, key_begin, starts, shape, key_axis):
    key_place = key_begin + lax.broadcasted_iota(jnp.int32, shape, key_axis)
    query_place = query_begin + lax.broadcasted_iota(jnp.int32, shape, 1 - key_axis)
    allowed = (key_place >= starts) & (key_place <= query_place)
    return jnp.where(allowed, 0.0, NEGATIVE).astype(F32)


def attend(begins, queries, key_values, starts, before=None):
    tokens, columns = queries.shape
    own = before is None
    block_q = math.gcd(tokens, 512)
    heads, pairs = columns // HEAD_DIM, columns // LANES
    keys = key_values.shape[0]
    steps = tokens // block_q
    tall = LANES + 16

    def body(begin_ref, q_ref, kv_ref, start_ref, *rest):
        if not own:
            (old_ref, old_log_ref), rest = rest[:2], rest[2:]
        low_ref, mixed_ref, log_ref, turned = rest
        step = pl.program_id(0)

        @pl.when(step == 0)
        def _():
            for pair in range(pairs):
                there = slice(columns + pair * LANES, columns + (pair + 1) * LANES)
                turned[pair * tall : pair * tall + LANES, :] = kv_ref[:, there].T
                turned[pair * tall + LANES : (pair + 1) * tall, :] = jnp.ones((16, keys), BF16)

        def work(count, at):
            bias = mask_bias(
                begin_ref[0] + at * block_q, begin_ref[1], start_ref[...], (count, block_q), 0
            )
            for pair in range(pairs):
                here = slice(pair * LANES, (pair + 1) * LANES)
                q = q_ref[:, here] * jnp.asarray(HEAD_DIM**-0.5, BF16)
                shares, terms = [], []
                for head in range(HEADS_TILE):
                    index = HEADS_TILE * pair + head
                    score = contract(kv_ref[:count, here], head_part(q, head), 1, 1) + bias
                    top = jnp.max(score, axis=0, keepdims=True)
                    weight = jnp.exp(score - top).astype(BF16)
                    found = jnp.dot(
                        turned[pair * tall : (pair + 1) * tall, :count],
                        weight,
                        preferred_element_type=F32,
                    )
                    value = found[head * HEAD_DIM : (head + 1) * HEAD_DIM]
                    total = found[LANES : LANES + 1]
                    joined = top + jnp.log(total)
                    if own:
                        value = value * (1.0 / total)
                    else:
                        old = old_log_ref[index : index + 1, :]
                        most = jnp.maximum(old, joined)
                        joined = most + jnp.log(jnp.exp(old - most) + jnp.exp(joined - most))
                        value = value * jnp.exp(top - joined)
                        shares.append(jnp.broadcast_to(jnp.exp(old - joined), value.shape))
                    log_ref[index : index + 1, :] = joined
                    terms.append(value)
                value = jnp.concatenate(terms, axis=0).T
                if not own:
                    value = value + old_ref[:, here] * jnp.concatenate(shares, axis=0).T
                mixed_ref[:, here] = value
                low_ref[:, here] = value.astype(BF16)

        if own:
            for at in range(steps):
                pl.when(step == at)(lambda at=at: work((at + 1) * block_q, at))
        else:
            work(keys, step)

    row = lambda i, s: (i, 0)
    lane = lambda i, s: (0, i)
    wide = pl.BlockSpec((block_q, columns), row)
    slim = pl.BlockSpec((heads, block_q), lane)
    extra = [] if own else list(before)
    return kernel_call(
        body,
        begins,
        [queries, key_values, starts, *extra],
        [wide, full(key_values), pl.BlockSpec((1, block_q), lane)] + ([] if own else [wide, slim]),
        [
            jax.ShapeDtypeStruct((tokens, columns), BF16),
            jax.ShapeDtypeStruct((tokens, columns), F32),
            jax.ShapeDtypeStruct((heads, tokens), F32),
        ],
        [wide, wide, slim],
        [pltpu.VMEM((pairs * tall, keys), BF16)],
        "attend_own" if own else "attend_far",
        grid=(steps,),
    )


def attend_backward(begins, queries, key_values, starts, mixed, logs, mixed_grad, own, before=None):
    tokens, columns = queries.shape
    block_q = math.gcd(tokens, 256)
    heads = columns // HEAD_DIM
    keys = key_values.shape[0]
    steps = tokens // block_q
    scale = HEAD_DIM**-0.5
    pairs = columns // LANES

    def body(begin_ref, q_ref, kv_ref, start_ref, mixed_ref, log_ref, grad_ref, *rest):
        if before is not None:
            before_ref, rest = rest[0], rest[1:]
        dq_ref, dkv_ref, turned, key_sum, value_sum = rest
        step = pl.program_id(0)

        @pl.when(step == 0)
        def _():
            key_sum[...] = jnp.zeros_like(key_sum)
            value_sum[...] = jnp.zeros_like(value_sum)
            for pair in range(pairs):
                here = slice(pair * LANES, (pair + 1) * LANES)
                turned[here, :] = kv_ref[:, here].T

        def work(count, at):
            bias = mask_bias(
                begin_ref[0] + at * block_q, begin_ref[1], start_ref[...], (count, block_q), 0
            )
            for pair in range(pairs):
                here = slice(pair * LANES, (pair + 1) * LANES)
                there = slice(columns + pair * LANES, columns + (pair + 1) * LANES)
                q, grad = q_ref[:, here], grad_ref[:, here]
                product = (mixed_ref[:, here] * grad.astype(F32)).T
                k, v = kv_ref[:count, here], kv_ref[:count, there]
                key_terms, value_terms, query_terms = [], [], []
                for head in range(HEADS_TILE):
                    q_head, grad_head = head_part(q, head), head_part(grad, head)
                    inner = slice(head * HEAD_DIM, (head + 1) * HEAD_DIM)
                    delta = jnp.sum(product[inner], axis=0, keepdims=True)
                    index = HEADS_TILE * pair + head
                    score = contract(k, q_head, 1, 1) * scale + bias
                    weight = jnp.exp(score - log_ref[index : index + 1, :])
                    weight_grad = contract(v, grad_head, 1, 1)
                    score_grad = (weight * (weight_grad - delta)).astype(BF16)
                    value_terms.append(
                        jnp.dot(weight.astype(BF16), grad_head, preferred_element_type=F32)
                    )
                    key_terms.append(jnp.dot(score_grad, q_head, preferred_element_type=F32))
                    begin = pair * LANES + head * HEAD_DIM
                    query_terms.append(
                        jnp.dot(
                            turned[begin : begin + HEAD_DIM, :count],
                            score_grad,
                            preferred_element_type=F32,
                        )
                    )
                value_sum[:count, here] += value_terms[0] + value_terms[1]
                key_sum[:count, here] += key_terms[0] + key_terms[1]
                found = jnp.concatenate(query_terms, axis=0).T * scale
                if before is not None:
                    found = found + before_ref[:, here]
                dq_ref[:, here] = found

        if own:
            for at in range(steps):
                pl.when(step == at)(lambda at=at: work((at + 1) * block_q, at))
        else:
            work(keys, step)

        @pl.when(step == steps - 1)
        def _():
            dkv_ref[:, :columns] = (key_sum[...] * scale).astype(dkv_ref.dtype)
            dkv_ref[:, columns:] = value_sum[...].astype(dkv_ref.dtype)

    row = lambda i, s: (i, 0)
    lane = lambda i, s: (0, i)
    wide = pl.BlockSpec((block_q, columns), row)
    extra = [] if before is None else [before]
    out = [
        jax.ShapeDtypeStruct((tokens, columns), F32),
        jax.ShapeDtypeStruct((keys, 2 * columns), F32 if own else BF16),
    ]
    return kernel_call(
        body,
        begins,
        [queries, key_values, starts, mixed, logs, mixed_grad, *extra],
        [
            wide,
            full(key_values),
            pl.BlockSpec((1, block_q), lane),
            wide,
            pl.BlockSpec((heads, block_q), lane),
            wide,
        ]
        + [wide] * len(extra),
        out,
        [wide, full(out[1])],
        [
            pltpu.VMEM((columns, keys), BF16),
            pltpu.VMEM((keys, columns), F32),
            pltpu.VMEM((keys, columns), F32),
        ],
        "attend_backward",
        grid=(steps,),
    )


def join_qkv_grads(table, query_grad, own_pairs, far_pairs, tables):
    tokens, columns = query_grad.shape
    rows = math.gcd(tokens, 512)

    def body(table_ref, q_ref, own_ref, *rest):
        far_refs, (turn_ref, out_ref, sum_ref) = rest[: len(far_pairs)], rest[len(far_pairs) :]

        @pl.when(pl.program_id(0) == 0)
        def _():
            sum_ref[...] = jnp.zeros_like(sum_ref)

        cosine, lower, upper = turn_ref[0], -turn_ref[1], -turn_ref[2]
        for tile in range(3 * columns // LANES):
            here = slice(tile * LANES, (tile + 1) * LANES)
            if tile < columns // LANES:
                value = q_ref[:, here]
            else:
                there = slice(tile * LANES - columns, (tile + 1) * LANES - columns)
                value = own_ref[:, there]
                for ref in far_refs:
                    value = value + ref[:, there].astype(F32)
            if tile < 2 * columns // LANES:
                value = rope(value, cosine, lower, upper)
            low = value.astype(BF16)
            out_ref[:, here] = low
            sum_ref[:, here] += jnp.sum(low.astype(F32), axis=0, keepdims=True)

    row = lambda i, s: (i, 0)
    spec = lambda array: pl.BlockSpec((rows, array.shape[1]), row)
    out = [
        jax.ShapeDtypeStruct((tokens, 3 * columns), BF16),
        jax.ShapeDtypeStruct((1, 3 * columns), F32),
    ]
    inputs = [query_grad, own_pairs, *far_pairs]
    return kernel_call(
        body,
        table,
        [*inputs, tables],
        [spec(array) for array in inputs]
        + [pl.BlockSpec((3, rows, LANES), lambda i, s: (0, i, 0))],
        out,
        [spec(out[0]), full(out[1])],
        [],
        "join_qkv_grads",
        grid=(tokens // rows,),
    )


def cut_weights(layout, table, sources):
    n = len(sources)
    pieces = [source.pieces for source in sources]

    def body(table_ref, *rest):
        refs, outs, sems = rest[:n], rest[n : 3 * n], rest[3 * n]
        core = table_ref[2 * layout.places]
        copies = []
        for i, source in enumerate(sources):
            for j in range(pieces[i]):
                for k, half in enumerate((core, 1 - core)):
                    copies.append(
                        pltpu.make_async_copy(
                            source.read(refs[i], half, j),
                            source.part(outs[2 * i + k], j),
                            sems.at[i, j, k],
                        )
                    )
        start_all(copies)
        wait_all(copies)

    return kernel_call(
        body,
        table,
        [source.array for source in sources],
        [HBM] * n,
        [jax.ShapeDtypeStruct(source.shape, BF16) for source in sources for _ in range(2)],
        [HBM] * (2 * n),
        [pltpu.SemaphoreType.DMA((n, max(pieces), 2))],
        "cut_weights",
    )


def join_weights(table, sources, shape, owns, received):
    n = len(sources)

    def body(table_ref, *rest):
        refs, out_ref = rest[: 2 * n], rest[2 * n]
        for i, source in enumerate(sources):
            out_ref[source.place()] = refs[i][...]
            out_ref[source.other()] = refs[n + i][...]

    out = jax.ShapeDtypeStruct(shape, BF16)
    arrays = [*owns, *received]
    return kernel_call(
        body, table, arrays, [full(a) for a in arrays], out, full(out), [], "join_weights"
    )


class RowSource:
    def __init__(self, array, layer, begin):
        self.array, self.layer, self.begin = array, layer, begin
        self.split = array.ndim == 4
        self.pieces = array.shape[1] if self.split else 1
        self.rows = array.shape[-2]
        self.size = array.shape[-1] // 2
        self.shape = (self.rows, self.pieces * self.size)

    def read(self, ref, core, piece):
        here = pl.ds(pl.multiple_of(core * self.size, self.size), self.size)
        return ref.at[self.layer, piece, :, here] if self.split else ref.at[self.layer, :, here]

    def place(self):
        return slice(0, self.rows), slice(self.begin, self.begin + self.shape[1])

    def other(self):
        return slice(self.rows, 2 * self.rows), slice(self.begin, self.begin + self.shape[1])

    def part(self, target, piece):
        return target.at[:, piece * self.size : (piece + 1) * self.size]


class ColumnSource:
    pieces = 1

    def __init__(self, array, layer, begin):
        self.array, self.layer, self.begin = array, layer, begin
        self.size, self.columns = array.shape[1] // 2, array.shape[2]
        self.shape = (self.size, self.columns)

    def read(self, ref, core, piece):
        return ref.at[self.layer, pl.ds(pl.multiple_of(core * self.size, self.size), self.size), :]

    def place(self):
        return slice(self.begin, self.begin + self.size), slice(0, self.columns)

    def other(self):
        return slice(self.begin, self.begin + self.size), slice(self.columns, 2 * self.columns)

    def part(self, target, piece):
        return target


def core_half(value, axis, which):
    size = value.shape[axis] // lax.axis_size(C)
    return lax.dynamic_slice_in_dim(value, which * size, size, axis)


def in_core_order(own, other, axis):
    return jnp.where(
        lax.axis_index(C) == 0,
        jnp.concatenate([own, other], axis=axis),
        jnp.concatenate([other, own], axis=axis),
    )


class Gather:
    def __init__(self, order, block, first, second):
        self.order, self.first, self.second = order, first, second
        self.n1, self.n2 = lax.axis_size(first), lax.axis_size(second)
        self.found = {(0, 0): block}

    def near(self, depth=1):
        for i in range(1, self.n1):
            self.found[i, 0] = self.order.send(self.found[0, 0], self.first, i, depth)
        return [self.found[i, 0] for i in range(1, self.n1)]

    def side(self, depth=1):
        for j in range(1, self.n2):
            self.found[0, j] = self.order.send(self.found[0, 0], self.second, j, depth)
        return [self.found[0, j] for j in range(1, self.n2)]

    def cross(self, depth=1):
        found = []
        for i in range(1, self.n1):
            for j in range(1, self.n2):
                self.found[i, j] = self.order.send(self.found[i, 0], self.second, j, depth)
                found.append(self.found[i, j])
        return found

    def blocks(self):
        if self.first == X:
            return [self.found[b, a] for a in range(self.n2) for b in range(self.n1)]
        return [self.found[a, b] for a in range(self.n1) for b in range(self.n2)]


class ScatterIn:
    def __init__(self, order, layout, table, features, right):
        self.order, self.layout, self.table = order, layout, table
        self.features, self.right = features, right

    def compute(self):
        layout, n_x = self.layout, self.layout.n_x
        which = [a * n_x + b for a in range(1, layout.n_y) for b in range(n_x)]
        (self.parts,) = self.order.run(
            lambda f, r: grad_in(layout, self.table, f, r, which), self.features, self.right
        )

    def begin(self, depth=1):
        size = self.layout.n_x * self.layout.block
        self.received = [
            self.order.send(self.parts[(a - 1) * size : a * size], Y, -a, depth)
            for a in range(1, self.layout.n_y)
        ]

    def middle(self):
        layout = self.layout
        self.first, self.away, self.others = self.order.run(
            lambda f, r, d: grad_in(layout, self.table, f, r, range(layout.n_x), d),
            self.features,
            self.right,
            self.received,
        )

    def finish(self, depth=2):
        block = self.layout.block
        self.near = [
            self.order.send(self.others[(b - 1) * block : b * block], X, -b, depth)
            for b in range(1, self.layout.n_x)
        ]

    def swap(self):
        away = self.order.run(
            lambda a, b: fold(self.table, a, b, True), self.away, self.near
        )
        self.sums = ([self.first, *self.near], [self.order.send(away, C, 1, 3)])


class ScatterOut:
    def __init__(self, order, layout, table, lefts, grad):
        self.order, self.layout, self.table = order, layout, table
        self.lefts, self.grad = lefts, grad
        self.received = [[] for _ in range(layout.n_y)]

    def compute(self):
        layout, n_x = self.layout, self.layout.n_x
        which = [a * n_x + b for a in range(layout.n_y) for b in range(1, n_x)]
        self.parts = self.order.run(
            lambda l, g: grad_out(layout, self.table, l, g, which), self.lefts, self.grad
        )

    def begin(self, a, depth=1):
        n_x = self.layout.n_x
        for b in range(1, n_x):
            part = self.parts[a * (n_x - 1) + b - 1]
            self.received[a].append(self.order.send(part, X, -b, depth))

    def all_received(self):
        return [value for row in self.received for value in row]

    def middle(self):
        layout = self.layout
        which = [a * layout.n_x for a in range(layout.n_y)]
        self.first, self.away, *self.others = self.order.run(
            lambda l, g, d: grad_out(layout, self.table, l, g, which, d),
            self.lefts,
            self.grad,
            self.received,
        )

    def finish(self, depth=2):
        self.near = [
            self.order.send(self.others[a - 1], Y, -a, depth) for a in range(1, self.layout.n_y)
        ]

    def swap(self):
        away = self.order.run(
            lambda a, b: fold(self.table, a, b, False), self.away, self.near
        )
        self.sums = ([self.first, *self.near], [self.order.send(away, C, 1, 3)])


def per_device(
    layer_input,
    segment_ids,
    positions,
    norm_gain,
    norm_bias,
    qkv_weight,
    qkv_bias,
    dense_weight,
    dense_bias,
    up_weight,
    up_bias,
    down_weight,
    down_bias,
    output_cotangent,
):
    layer_count = qkv_weight.shape[0]
    last = layer_count - 1
    core, x = lax.axis_index(C), lax.axis_index(X)
    z, n_z = lax.axis_index(Z), lax.axis_size(Z)
    layout = Layout(*layer_input.shape)
    n_x = layout.n_x
    tokens, width = layout.tokens, layout.width
    columns = qkv_weight.shape[3] // layout.n_c
    hidden = up_weight.shape[2] // layout.n_c
    table = width_table(layout)
    query_begin = x * tokens
    begins = [
        jnp.stack([query_begin, (x - b + n_x) % n_x * tokens]).astype(jnp.int32) for b in range(n_x)
    ]
    order = Order()
    gathers = {}
    kept = [SimpleNamespace(layer=layer) for layer in range(layer_count)]
    outputs = [None] * layer_count
    sums = [None] * layer_count

    def arrived(*transfers):
        order.wait(*transfers)


    def sources_of(layer, group):
        if group == OUT:
            shape = (columns + hidden, layout.block)
            return shape, [
                ColumnSource(dense_weight, layer, 0),
                ColumnSource(down_weight, layer, columns),
            ]
        sources = []
        if group != UP:
            sources.append(RowSource(qkv_weight.transpose(0, 2, 1, 3), layer, 0))
        if group != QKV:
            begin = 3 * columns if group == IN else 0
            sources.append(RowSource(up_weight, layer, begin))
        return (layout.block, sum(source.shape[1] for source in sources)), sources

    def make_ready(layer, groups):
        found = []
        for group in groups:
            shape, sources = sources_of(layer, group)

            def cut(arrays, sources=sources):
                for source, array in zip(sources, arrays):
                    source.array = array
                return cut_weights(layout, table, sources)

            parts = order.run(cut, [source.array for source in sources])
            found.append((sources, shape, parts[::2], parts[1::2]))
        swapped = [[shift(value, C, 1) for value in order.after(away)] for *_, away in found]
        for group, (sources, shape, owns, _), received in zip(groups, found, swapped):
            block = order.run(
                lambda o, r, s=sources, h=shape: join_weights(table, s, h, o, r), owns, received
            )
            ways = (Y, X) if group == OUT else (X, Y)
            gathers[layer, group] = Gather(order, block, *ways)

    def blocks_of(layer, group):
        if (layer, group) not in gathers:
            group = IN
        return gathers[layer, group].blocks()


    def gather_features(block):
        return lax.all_gather(order.after([block])[0], (C, Z), axis=0, tiled=False)

    def scatter_features(summed):
        return lax.psum_scatter(order.after([summed])[0], Z, scatter_dimension=1, tiled=True)

    def to_owner(lefts, weights, transposed, name, awaited=()):
        away = order.run(
            lambda *a: project_back(layout, table, a[0], a[1], transposed, True, name), lefts, weights
        )
        received = [order.send(piece, C, 1, PIECES) for piece in away]
        (own,) = order.run(
            lambda *a: project_back(layout, table, a[0], a[1], transposed, False, name), lefts, weights
        )
        if awaited:
            order.wait(*awaited)
        return order.run(lambda a, b: merge_cores(layout, table, a, b), own, received)

    def moments(value, axes):
        mean = jnp.sum(value, axis=axes) / width
        return mean, jnp.sum(value * value, axis=axes) / width

    def inverse_of(mean, square):
        return lax.rsqrt(square - mean * mean + EPSILON)

    def normalise(k, residual):
        stats = jnp.stack([jnp.sum(residual, axis=1), jnp.sum(residual * residual, axis=1)])
        stats = sum_over(stats, Z) / width
        k.inverse = inverse_of(stats[0], stats[1])
        k.centred = (residual - stats[0][:, None]) * k.inverse[:, None]
        normed = (k.centred * norm_gain[k.layer] + norm_bias[k.layer]).astype(BF16)
        (normed,) = order.wait(normed)
        k.features = gather_features(normed)
        order.wait(normed)

    def qkv_shift(layer):
        return core_half(qkv_bias[layer], 1, core).reshape(1, -1)

    def up_shift(layer):
        return core_half(up_bias[layer], 0, core).reshape(1, -1)

    def project_q(k):
        k.q, pairs = order.run(
            lambda f, w, b, t: project_qkv(layout, table, f, w, b, t),
            k.features,
            blocks_of(k.layer, QKV),
            qkv_shift(k.layer),
            tables,
        )
        k.pairs = [pairs] + [order.send(pairs, X, b) for b in range(1, n_x)]

    def project_hidden(k, *grad):
        k.active, k.slope = order.run(
            lambda f, w, b, *g: project_up(layout, table, f, w, b, *g),
            k.features,
            blocks_of(k.layer, UP),
            up_shift(k.layer),
            *grad,
        )

    def grads_of_branch(k, grad_features, *slope):
        k.mixed_grad, k.hidden_grad = order.run(
            lambda g, w, *s: branch_grads(layout, table, g, w, columns, *s),
            grad_features,
            blocks_of(k.layer, OUT),
            *slope,
        )

    def own_attention(k):
        k.found = order.run(attend, begins[0], k.q, k.pairs[0], starts)

    def far_attention(k):
        for b in range(1, n_x):
            k.found = order.run(attend, begins[b], k.q, k.pairs[b], starts, k.found[1:])
        k.mixed_low, k.mixed, k.logs = k.found

    def far_gradients(k):
        k.query_grad, k.away_pairs = [], []
        for b in range(1, n_x):
            found, pair_grad = order.run(
                lambda *a: attend_backward(*a[:7], False, *a[7:]),
                *(begins[b], k.q, k.pairs[b], starts, k.mixed, k.logs, k.mixed_grad),
                *k.query_grad,
            )
            k.query_grad = [found]
            k.away_pairs.append(order.send(pair_grad, X, -b))

    def own_gradients(k):
        k.query_grad, k.own_pairs = order.run(
            lambda *a: attend_backward(*a[:7], True, *a[7:]),
            *(begins[0], k.q, k.pairs[0], starts, k.mixed, k.logs, k.mixed_grad),
            *k.query_grad,
        )

    def join_gradients(k):
        k.qkv_low, k.qkv_sum = order.run(
            lambda *a: join_qkv_grads(table, *a), k.query_grad, k.own_pairs, k.away_pairs, tables
        )

    def branch_sum(k):
        lefts = [k.mixed_low, k.active]
        pairs = [(block,) for block in blocks_of(k.layer, OUT)]
        return to_owner(lefts, pairs, False, "project_out")

    def feature_sum(k, *awaited):
        if (k.layer, IN) in gathers:
            pairs = [(block,) for block in blocks_of(k.layer, IN)]
        else:
            pairs = list(zip(blocks_of(k.layer, QKV), blocks_of(k.layer, UP)))
        return to_owner([k.qkv_low, k.up_low], pairs, True, "feature_grads", awaited)

    def add_branch(residual, branch, layer):
        return residual + branch.astype(F32) + dense_bias[layer] + down_bias[layer]


    residual = layer_input.astype(F32)
    raw = gather_features(layer_input)
    make_ready(0, [QKV])
    qkv = gathers[0, QKV]
    first_near, first_side = qkv.near(), qkv.side()
    grad_features = gather_features(output_cotangent)
    make_ready(0, [UP, OUT])
    up, out = gathers[0, UP], gathers[0, OUT]
    arrived(*first_near, *first_side)
    up_near, qkv_cross = up.near(), qkv.cross()
    query_segments = lax.dynamic_slice_in_dim(segment_ids, query_begin, tokens, 0)
    starts = jnp.sum(
        (segment_ids[:, None] < query_segments[None, :]).astype(jnp.int32), axis=0, keepdims=True
    )
    places = lax.dynamic_slice_in_dim(positions, query_begin, tokens, 0)
    tables = rope_tables(order.after([places])[0])
    starts, tables = order.wait(starts, tables)
    affine = order.after([jnp.stack([norm_gain[0], norm_bias[0]])])[0]
    spread = [affine] + [shift(affine, Z, k) for k in range(1, n_z)]
    spread = jnp.stack(spread)[(z - jnp.arange(n_z) + n_z) % n_z]
    (spread,) = order.wait(spread)
    arrived(*up_near, *qkv_cross)
    out_near, out_side = out.near(), out.side()
    (raw,) = order.wait(raw)
    blocks = raw.reshape(layout.n_c, n_z, layout.own_tokens, layout.part).astype(F32)
    mean, square = moments(blocks, (1, 3))
    inverse = inverse_of(mean, square)
    gain, bias = (spread[:, i][None, :, None, :] for i in range(2))
    normed = (blocks - mean[:, None, :, None]) * inverse[:, None, :, None] * gain + bias
    kept[0].inverse = lax.dynamic_index_in_dim(inverse, core, 0, keepdims=False)
    own_mean = lax.dynamic_index_in_dim(mean, core, 0, keepdims=False)
    (kept[0].features,) = order.wait(normed.astype(BF16).reshape(raw.shape))
    for k in kept[:-1]:
        layer = k.layer
        project_q(k)
        if layer == 0:
            up_side = up.side(2)
        own_attention(k)
        arrived(*k.pairs[1:])
        if layer == 0:
            arrived(*up_side, *out_near, *out_side)
            out_cross, up_cross = out.cross(), up.cross()
        far_attention(k)
        make_ready(layer + 1, [IN, OUT])
        in_next, out_next = gathers[layer + 1, IN], gathers[layer + 1, OUT]
        if layer == 0:
            arrived(grad_features, *up_cross, *out_cross)
        next_near, next_side = out_next.near(), out_next.side()
        project_hidden(k)
        summed = branch_sum(k)
        arrived(*next_near, *next_side)
        branch = scatter_features(summed)
        order.wait(summed)
        arrived(*in_next.near(), *in_next.side())
        (branch,) = order.wait(branch)
        residual = outputs[layer] = add_branch(residual, branch, layer)
        k = kept[layer + 1]
        normalise(k, residual)
        next_cross, in_cross = out_next.cross(), in_next.cross()
        if k.layer == last:
            arrived(*next_cross)
            grads_of_branch(k, grad_features)
        arrived(*in_cross)
        order.wait(k.features)


    k = kept[last]
    project_q(k)
    project_hidden(k, k.hidden_grad)
    k.up_low = k.slope
    gradient = output_cotangent.astype(F32)
    held = {UP: None, QKV: None, OUT: None}
    shapes = {
        UP: (layer_count, layout.place, layout.n_c * hidden),
        QKV: (layer_count, 3, layout.place, layout.n_c * columns),
        OUT: [
            (layer_count, layout.n_c * columns, layout.place),
            (layer_count, layout.n_c * hidden, layout.place),
        ],
    }

    def place(layer, group, scatter):
        def write(owns, others, before):
            if group == OUT:
                return place_out(layout, table, layer, owns, others, shapes[group], before)
            parts = 3 if group == QKV else 1
            return place_in(layout, table, layer, owns, others, shapes[group], before, parts)

        held[group] = order.run(write, *scatter.sums, held[group])

    def norm_backward(k, normed_grad, gradient):
        normed_grad = normed_grad.astype(F32)
        scaled_grad = normed_grad * norm_gain[k.layer]
        means = jnp.stack([jnp.sum(scaled_grad, axis=1), jnp.sum(scaled_grad * k.centred, axis=1)])
        means = sum_over(means, Z) / width
        new = gradient + k.inverse[:, None] * (
            scaled_grad - means[0][:, None] - k.centred * means[1][:, None]
        )

        def to_both(value):
            return in_core_order(value, jnp.zeros_like(value), value.ndim - 1).reshape(-1)

        sums[k.layer] = jnp.concatenate(
            [
                jnp.sum(normed_grad * k.centred, axis=0),
                jnp.sum(normed_grad, axis=0),
                to_both(k.qkv_sum.reshape(3, columns)),
                jnp.sum(gradient, axis=0),
                to_both(k.up_sum),
            ]
        )
        return new

    kept[0].centred = (layer_input.astype(F32) - own_mean[:, None]) * kept[0].inverse[:, None]
    before = None

    for k in reversed(kept):
        layer = k.layer
        scatter_in = lambda right: ScatterIn(order, layout, table, k.features, right)
        if layer == last:
            own_attention(k)
            arrived(*k.pairs[1:])
            up = scatter_in(k.up_low)
            up.compute()
            up.begin()
            far_attention(k)
        else:
            (grad_features,) = order.wait(grad_features)
            branch = None
            if layer + 1 == last:
                branch = scatter_features(out_summed)
        out = ScatterOut(order, layout, table, [k.mixed_low, k.active], grad_features)
        if layer < last:
            out.compute()
            out.begin(layout.n_y - 1, 1)
            grads_of_branch(k, grad_features, k.slope)
            k.up_low = k.hidden_grad
            up = scatter_in(k.up_low)
        far_gradients(k)
        if layer < last:
            up.compute()
            up.begin()
        own_gradients(k)
        if layer < last:
            before.swap()
            place(layer + 1, QKV, before)
            arrived(*k.away_pairs, *out.received[-1])
            for a in reversed(range(layout.n_y - 1)):
                out.begin(a, 1)
        else:
            out.compute()
            arrived(*k.away_pairs, *up.received)
        join_gradients(k)
        (k.up_sum,) = order.wait(jnp.sum(order.after([k.up_low])[0], axis=0, dtype=F32))
        qkv = scatter_in(k.qkv_low)
        if layer < last:
            qkv.compute()
        awaited = [] if layer == last else [*up.received, *out.all_received()]
        summed = feature_sum(k, *awaited)
        normed_grad = scatter_features(summed)
        order.wait(summed)
        if layer == last:
            for a in reversed(range(1, layout.n_y)):
                out.begin(a, 1)
            qkv.compute()
            qkv.begin()
            up.middle()
            out_summed = branch_sum(k)
            out.begin(0, 1)
            (normed_grad,) = order.wait(normed_grad)
            gradient = norm_backward(k, normed_grad, gradient)
            (low,) = order.wait(gradient.astype(BF16))
            arrived(*out.all_received(), *qkv.received)
            grad_features = gather_features(low)
            order.wait(low)
            up.finish(1)
            out.middle()
            out.finish(1)
            qkv.middle()
            qkv.finish(1)
            arrived(*up.near)
            up.swap()
            place(layer, UP, up)
            arrived(*out.near)
            out.swap()
            place(layer, OUT, out)
            arrived(*qkv.near)
        else:
            qkv.begin()
            up.middle()
            up.finish(1)
            if branch is not None:
                outputs[last] = add_branch(residual, branch, last)
                (outputs[last],) = order.wait(outputs[last])
            out.middle()
            arrived(*qkv.received)
            out.finish(1)
            qkv.middle()
            qkv.finish(1)
            (normed_grad,) = order.wait(normed_grad)
            gradient = norm_backward(k, normed_grad, gradient)
            (gradient,) = order.wait(gradient)
            if layer > 0:
                up.swap()
                out.swap()
                place(layer, UP, up)
                place(layer, OUT, out)
        before = qkv

    small = sum_over(jnp.stack(order.after(sums)), C)
    arrived(*qkv.near, *up.near, *out.near)
    (small,) = order.wait(small)
    small = sum_over(small, X)
    qkv.swap()
    up.swap()
    out.swap()
    place(0, UP, up)
    (small,) = order.wait(small)
    small = sum_over(small, Y)
    place(0, OUT, out)
    place(0, QKV, qkv)

    small, gradient, outputs = order.now((small, gradient, outputs))
    held = order.now(held)
    part, both = layout.part, layout.n_c * columns
    ends = [0]
    for size in (part, part, 3 * both, part, layout.n_c * hidden):
        ends.append(ends[-1] + size)
    gain_grad, shift_grad, qkv_grad, out_bias_grad, up_grad = [
        small[:, begin:end] for begin, end in zip(ends[:-1], ends[1:])
    ]
    return (
        jnp.stack(outputs),
        gradient,
        gain_grad,
        shift_grad,
        held[QKV].transpose(0, 2, 1, 3),
        qkv_grad.reshape(layer_count, 3, both),
        held[OUT][0],
        out_bias_grad,
        held[UP],
        up_grad,
        held[OUT][1],
        out_bias_grad,
    )


def solution(mesh):
    n_y, n_row, n_z = (mesh.shape[name] for name in mesh.axis_names)
    split = Mesh(mesh.devices.reshape(n_y, n_row // 2, 2, n_z), (Y, X, C, Z))
    rows = (Y, X, C)
    placed = (
        P(rows, Z),
        P(Y),
        P(Y),
        P(None, Z),
        P(None, Z),
        P(None, rows, None, Z),
        P(None, None, Z),
        P(None, Z, rows),
        P(None, Z),
        P(None, rows, Z),
        P(None, Z),
        P(None, Z, rows),
        P(None, Z),
        P(rows, Z),
    )
    return jax.shard_map(
        per_device,
        mesh=split,
        in_specs=placed,
        out_specs=(
            P(None, rows, Z),
            P(rows, Z),
            P(None, Z),
            P(None, Z),
            P(None, rows, None, Z),
            P(None, None, Z),
            P(None, Z, rows),
            P(None, Z),
            P(None, rows, Z),
            P(None, Z),
            P(None, Z, rows),
            P(None, Z),
        ),
        check_vma=False,
    )
```
